32 devices in a mesh: dp: 4 (over z), row: 4 (over y, x), col: 2 (over core).
Axes of the slice: x: 2, y: 2, z: 4, core: 2. Of those that a mesh axis runs over, the one named last changes fastest.
Arguments:
- tokens: bfloat16 [9232, 1024], P('dp', ('row', 'col')), may hold values from -80 to 80
- projector: bfloat16 [3, 1024, 1024], P(None, 'row', 'col'), may hold values from -0.25 to 0.25
- offsets: float32 [2, 1024], P(None, 'col'), may hold values from -3 to 3
- combiner: bfloat16 [1024, 1024], P('col', 'row'), may hold values from -0.25 to 0.25
- baseline: float32 [1024], P(('row', 'col')), may hold values from -2 to 2
- widener: bfloat16 [1024, 4096], P('row', 'col'), may hold values from -0.1875 to 0.1875
- thresholds: float32 [4096], P('col'), may hold values from -3 to 3
- narrower: bfloat16 [4096, 1024], P('col', 'row'), may hold values from -0.125 to 0.125
- residue: float32 [1024], P(('row', 'col')), may hold values from -2 to 2
- stretch: float32 [1024], P(('row', 'col')), may hold values from 0.5 to 1.5
- lifting: float32 [1024], P(('row', 'col')), may hold values from -2 to 2
- dilation: float32 [1024], P(('row', 'col')), may hold values from 0.5 to 1.5
- elevation: float32 [1024], P(('row', 'col')), may hold values from -2 to 2
- cotangent: bfloat16 [9232, 1024], P('dp', ('row', 'col')), may hold values from -6 to 6
Outputs:
- layer_output: float32 [9232, 1024], P('dp', ('row', 'col'))
- tokens_delta: float32 [9232, 1024], P('dp', ('row', 'col'))
- projector_delta: float32 [3, 1024, 1024], P(None, 'row', 'col')
- offsets_delta: float32 [2, 1024], P(None, 'col')
- combiner_delta: float32 [1024, 1024], P('col', 'row')
- baseline_delta: float32 [1024], P(('row', 'col'))
- widener_delta: float32 [1024, 4096], P('row', 'col')
- thresholds_delta: float32 [4096], P('col')
- narrower_delta: float32 [4096, 1024], P('col', 'row')
- residue_delta: float32 [1024], P(('row', 'col'))
- stretch_delta: float32 [1024], P(('row', 'col'))
- lifting_delta: float32 [1024], P(('row', 'col'))
- dilation_delta: float32 [1024], P(('row', 'col'))
- elevation_delta: float32 [1024], P(('row', 'col'))
The draws below stay inside these ranges and needn't reach their ends.
All inputs are finite; a program needn't handle non-finite values.
Results may differ from the reference program's by a relative error of at most 0.015.
Values may be sent and summed in bfloat16 or wider, within the bound.
No kernel may reach another device: no remote copies, remote signals or barrier semaphores. Data moves between devices by JAX's collectives and lax.ppermute only.
A program may use at most 128 MiB of HBM per device.

```python
import math
import jax
import jax.numpy as jnp
from jax import lax

D = 1024
H = 16
HD = 64
FF = 4096
SEQ = 577
IMAGES = 16
TOKENS = 9232


def draw_tokens(key, part):
    subkeys = jax.random.split(key, 4)
    column = jnp.arange(D, dtype=jnp.float32) / D
    roughness = jnp.exp(jax.random.uniform(subkeys[0], (D,), jnp.float32, -0.35, 0.35))
    column_scale = jnp.exp(column * math.log(3.0)) * roughness
    centre = jax.random.uniform(subkeys[1], (D,), jnp.float32, -0.5, 0.5)
    base_draw = jax.random.truncated_normal(subkeys[2], -4.0, 4.0, (TOKENS, D), jnp.float32)
    row_scale = jnp.exp(jax.random.uniform(subkeys[3], (TOKENS, 1), jnp.float32, -1.15, 1.15))
    return ((base_draw + centre) * column_scale * row_scale).astype(jnp.bfloat16)


def level_of(rng, shape, pieces, smallest, largest):
    def one(axis_at, blocks):
        heights = jax.random.uniform(jax.random.fold_in(jax.random.fold_in(rng, 6), axis_at), (blocks,), jnp.float32, smallest / len(pieces), largest / len(pieces))
        return jnp.repeat(jnp.exp(heights), shape[axis_at] // blocks).reshape((-1,) + (1,) * (len(shape) - axis_at - 1))

    level = one(*pieces[0])
    for cut in pieces[1:]:
        level = level * one(*cut)
    return level


def bell_draw(rng, extent, scale, reach, shards=(), kind=jnp.bfloat16):
    values = jax.random.normal(rng, extent, jnp.float32) * scale
    if len(shards) > 0:
        values = level_of(rng, extent, shards, -0.22, 0.18) * values
    return jnp.clip(values, min=-reach, max=reach).astype(kind)


def setup_inputs(seed: int = 0) -> dict:
    seeds = jax.random.split(jax.random.key(seed), 15)
    tokens = draw_tokens(jax.random.fold_in(seeds[14], 71), 0)
    projector = bell_draw(seeds[1], (3, D, D), (D // 2) ** -0.5, 0.25, ((1, 4), (2, 2)))
    offsets = bell_draw(seeds[2], (2, D), 0.5, 3.0, ((1, 2),), jnp.float32)
    combiner = bell_draw(seeds[3], (D, D), (D // 2) ** -0.5, 0.25, ((0, 2), (1, 4)))
    baseline = bell_draw(seeds[4], (D,), 0.3, 2.0, ((0, 8),), jnp.float32)
    widener = bell_draw(seeds[5], (D, FF), D ** -0.5, 0.1875, ((0, 4), (1, 2)))
    thresholds = bell_draw(seeds[6], (FF,), 0.5, 3.0, ((0, 2),), jnp.float32)
    narrower = bell_draw(seeds[7], (FF, D), (FF // 2) ** -0.5, 0.125, ((0, 2), (1, 4)))
    residue = bell_draw(seeds[8], (D,), 0.3, 2.0, ((0, 8),), jnp.float32)
    stretch = jnp.clip(1.0 + 0.1 * jax.random.normal(seeds[9], (D,), jnp.float32), 0.5, 1.5)
    lifting = bell_draw(seeds[10], (D,), 0.3, 2.0, ((0, 8),), jnp.float32)
    dilation = jnp.clip(1.0 + 0.1 * jax.random.normal(seeds[11], (D,), jnp.float32), 0.5, 1.5)
    elevation = bell_draw(seeds[12], (D,), 0.3, 2.0, ((0, 8),), jnp.float32)
    cotangent = bell_draw(seeds[13], (TOKENS, D), 1.0, 6.0, ((0, 4), (1, 8)))
    return {"tokens": tokens, "projector": projector, "offsets": offsets, "combiner": combiner, "baseline": baseline, "widener": widener, "thresholds": thresholds, "narrower": narrower, "residue": residue, "stretch": stretch, "lifting": lifting, "dilation": dilation, "elevation": elevation, "cotangent": cotangent}


NORM_EPSILON = 1e-05
SIGMOID_SLOPE = 1.702

@jax.custom_vjp
def low(v):
    return lax.optimization_barrier(v.astype(jnp.bfloat16)).astype(jnp.float32)

@jax.custom_vjp
def low_back(v):
    return v

def low_keep(v):
    return (low(v), None)

def low_pass(kept, grad):
    return (grad,)

def back_keep(v):
    return (v, None)

def back_low(kept, grad):
    return (low(grad),)
low.defvjp(low_keep, low_pass)
low_back.defvjp(back_keep, back_low)

def highest(left_side, right_side):
    return jnp.dot(left_side, right_side, precision=lax.Precision.HIGHEST)

def layer_norm(values, gain_vector, shift_vector):
    average = lax.optimization_barrier(jnp.mean(values, axis=-1, keepdims=True))
    centred = values - average
    spread = lax.optimization_barrier(jnp.mean(centred * centred, axis=-1, keepdims=True))
    return centred * lax.rsqrt(spread + NORM_EPSILON) * gain_vector + shift_vector

def image_layer(params, image):
    projector, offsets, combiner, baseline, widener, thresholds, narrower, residue, stretch, lifting, dilation, elevation = params
    normed_one = low(layer_norm(image, stretch, lifting))
    queries = low_back(low(highest(normed_one, projector[0]) + offsets[0])).reshape(SEQ, H, HD)
    keyset = low_back(low(highest(normed_one, projector[1]))).reshape(SEQ, H, HD)
    valueset = low_back(low(highest(normed_one, projector[2]) + offsets[1])).reshape(SEQ, H, HD)
    scores = low_back(jnp.einsum('qhd,khd->hqk', queries, keyset, precision=lax.Precision.HIGHEST) * HD ** (-0.5))
    weights = low(jax.nn.softmax(scores, axis=-1))
    mixed = jnp.einsum('hqk,khd->qhd', weights, valueset, precision=lax.Precision.HIGHEST).reshape(SEQ, D)
    mixed = low_back(low(mixed))
    resid_two = image + low_back(highest(mixed, combiner)) + baseline
    normed_two = low(layer_norm(resid_two, dilation, elevation))
    expanded = low_back(highest(normed_two, widener) + thresholds)
    hidden = low(expanded * jax.nn.sigmoid(SIGMOID_SLOPE * expanded))
    return resid_two + low_back(highest(hidden, narrower)) + residue

def add_pair(left_item, right_item):
    return left_item + right_item

def reference(tokens, projector, offsets, combiner, baseline, widener, thresholds, narrower, residue, stretch, lifting, dilation, elevation, cotangent):
    params = tuple((item.astype(jnp.float32) for item in (projector, offsets, combiner, baseline, widener, thresholds, narrower, residue, stretch, lifting, dilation, elevation)))
    images = tokens.astype(jnp.float32).reshape(IMAGES, SEQ, D)
    upstream = cotangent.astype(jnp.float32).reshape(IMAGES, SEQ, D)

    def per_image(totals, inputs):
        image, image_cot = inputs
        result, pullback = jax.vjp(image_layer, params, image)
        param_grads, image_grad = pullback(image_cot)
        return (jax.tree.map(add_pair, totals, param_grads), (result, image_grad))
    zeros = jax.tree.map(jnp.zeros_like, params)
    totals, (results, image_grads) = lax.scan(per_image, zeros, (images, upstream))
    return (results.reshape(TOKENS, D), image_grads.reshape(TOKENS, D), totals[0], totals[1], totals[2], totals[3], totals[4], totals[5], totals[6], totals[7], totals[8], totals[9], totals[10], totals[11])
```

```python
import functools

import jax
import jax.numpy as jnp
from jax import lax
from jax.experimental import pallas as pl
from jax.experimental.pallas import tpu as pltpu
from jax.sharding import PartitionSpec as P

D = 1024
HD = 64
SEQ = 577
PAD = 592
RB = 4
KB = D // RB

NORM_EPSILON = 1e-05
SIGMOID_SLOPE = 1.702
F32 = jnp.float32
BF16 = jnp.bfloat16
VMEM_LIMIT = 60 * 1024 * 1024

STRETCH, LIFTING, BASELINE, DILATION, ELEVATION, RESIDUE = range(6)


def mm(a, b):
    return lax.dot_general(a, b, (((1,), (0,)), ((), ())), preferred_element_type=F32)


def mm_nt(a, b):
    return lax.dot_general(a, b, (((1,), (1,)), ((), ())), preferred_element_type=F32)


def mm_tn(a, b):
    return lax.dot_general(a, b, (((0,), (0,)), ((), ())), preferred_element_type=F32)


def sds(shape, dtype=BF16):
    return jax.ShapeDtypeStruct(shape, dtype)


def whole(shape):
    return pl.BlockSpec(shape, lambda *_: (0,) * len(shape))


def call(body, grid, in_specs, out_specs, out_shape, flops, nbytes, scratch=(), transcendentals=0):
    return pl.pallas_call(
        body,
        grid=grid,
        in_specs=in_specs,
        out_specs=out_specs,
        out_shape=out_shape,
        scratch_shapes=list(scratch),
        compiler_params=pltpu.CompilerParams(
            vmem_limit_bytes=VMEM_LIMIT, dimension_semantics=("arbitrary",) * len(grid)
        ),
        cost_estimate=pl.CostEstimate(
            flops=int(flops), bytes_accessed=int(nbytes), transcendentals=int(transcendentals)
        ),
    )


def row_mask(shape):
    return lax.broadcasted_iota(jnp.int32, shape, 0) < SEQ


def standardize(value):
    average = jnp.mean(value, axis=1, keepdims=True)
    centred = value - average
    spread = jnp.mean(centred * centred, axis=1, keepdims=True)
    reciprocal = lax.rsqrt(spread + NORM_EPSILON)
    return centred * reciprocal, reciprocal


def norm_backward(upstream, standard, reciprocal, gain):
    scaled = upstream * gain
    mean_scaled = jnp.mean(scaled, axis=1, keepdims=True)
    mean_along = jnp.mean(scaled * standard, axis=1, keepdims=True)
    return reciprocal * (scaled - mean_scaled - standard * mean_along)


def qkv_kernel(x, vec, w0, w1, w2, w3, bias, normed_t, qkv, normed):
    @pl.when(pl.program_id(0) == 0)
    def _():
        standard, _r = standardize(x[...].astype(F32))
        value = standard * vec[STRETCH : STRETCH + 1] + vec[LIFTING : LIFTING + 1]
        normed[...] = value.astype(BF16)
        normed_t[...] = value.T.astype(BF16)

    total = bias[0]
    for k, w in enumerate((w0, w1, w2, w3)):
        total = total + mm(normed[:, k * KB : (k + 1) * KB], w[0])
    qkv[...] = total.astype(BF16)


def qkv_call(x, vec, blocks, bias):
    width = blocks[0].shape[2]
    wspec = pl.BlockSpec((1, KB, width), lambda j: (j, 0, 0))
    return call(
        qkv_kernel,
        (3,),
        [whole((PAD, D)), whole(vec.shape)] + [wspec] * 4 + [pl.BlockSpec((1, 1, width), lambda j: (j, 0, 0))],
        [whole((D, PAD)), pl.BlockSpec((PAD, width), lambda j: (0, j))],
        [sds((D, PAD)), sds((PAD, 3 * width))],
        2 * PAD * D * 3 * width,
        2 * D * 3 * width + 4 * PAD * D + 6 * PAD * width,
        [pltpu.VMEM((PAD, D), BF16)],
    )(x, vec, *blocks, bias)


def head_mask(i, shape):
    lane = lax.broadcasted_iota(jnp.int32, shape, 1)
    return (lane >= i * HD) & (lane < (i + 1) * HD)


def attend_kernel(q, k, v, mixed, probs):
    queries = q[...]
    keys = k[...]
    values_t = v[...].astype(F32).T.astype(BF16)
    outs = []
    for i in range(2):
        picked = jnp.where(head_mask(i, queries.shape), queries.astype(F32) * HD ** (-0.5), 0.0)
        scores = mm_nt(keys, picked.astype(BF16))
        scores = jnp.where(row_mask(scores.shape), scores, -1e30)
        top = jnp.max(scores, axis=0, keepdims=True)
        weights = jnp.exp(scores - top)
        total = jnp.sum(weights, axis=0, keepdims=True)
        rounded = (weights * (1.0 / total)).astype(BF16)
        probs[i] = rounded
        outs.append(mm(values_t[i * HD : (i + 1) * HD], rounded))
    mixed[...] = jnp.concatenate(outs, axis=0).T.astype(BF16)


def attend_call(qkv):
    width = qkv.shape[1] // 3
    pairs = width // 128
    spec = lambda j: pl.BlockSpec((PAD, 128), lambda h, j=j: (0, j * pairs + h))
    return call(
        attend_kernel,
        (pairs,),
        [spec(0), spec(1), spec(2)],
        [pl.BlockSpec((PAD, 128), lambda h: (0, h)), pl.BlockSpec((2, PAD, PAD), lambda h: (h, 0, 0))],
        [sds((PAD, width)), sds((2 * pairs, PAD, PAD))],
        pairs * 2 * 2 * 2 * PAD * PAD * 128,
        pairs * 2 * PAD * PAD * 2,
        transcendentals=pairs * 2 * PAD * PAD,
    )(qkv, qkv, qkv)


def combine_kernel(mixed, w0, w1, w2, w3, part):
    for k, w in enumerate((w0, w1, w2, w3)):
        part[:, k * KB : (k + 1) * KB] = mm(mixed[...], w[...]).astype(BF16)


def combine_call(mixed, blocks):
    width = mixed.shape[1]
    return call(
        combine_kernel,
        (1,),
        [whole((PAD, width))] + [whole((width, KB))] * 4,
        whole((PAD, D)),
        sds((PAD, D)),
        2 * PAD * D * width,
        2 * (PAD * D + width * D + PAD * width),
    )(mixed, *blocks)


def split_lanes(value, refs):
    refs[0][...] = value[:, :KB].astype(BF16)
    for k in range(1, RB):
        for h in range(2):
            lo = k * KB + h * (KB // 2)
            refs[1 + 2 * (k - 1) + h][...] = value[:, lo : lo + KB // 2].astype(BF16)


def split_rows(value, refs, at=None):
    refs[0][...] = value[:KB].astype(BF16)
    for k in range(1, RB):
        for h in range(2):
            lo = k * KB + h * (KB // 2)
            refs[1 + 2 * (k - 1) + h][...] = value[lo : lo + KB // 2].astype(BF16)


def forward_kernel(tile, x, part, sib, vec, w0, w1, w2, w3, thresholds, cot, *rest):
    resid, normed_t, hidden, slope = rest[:4]
    deltas = rest[4:11]
    normed = rest[11]

    @pl.when(pl.program_id(0) == 0)
    def _():
        total = x[...].astype(F32) + (part[...].astype(F32) + sib[...].astype(F32)) + vec[BASELINE : BASELINE + 1]
        total = jnp.where(row_mask(total.shape), total, 0.0)
        resid[...] = total
        standard, _r = standardize(total)
        value = standard * vec[DILATION : DILATION + 1] + vec[ELEVATION : ELEVATION + 1]
        normed[...] = value.astype(BF16)
        normed_t[...] = value.T.astype(BF16)

    expanded = thresholds[...]
    for k, w in enumerate((w0, w1, w2, w3)):
        expanded = expanded + mm(normed[:, k * KB : (k + 1) * KB], w[...])
    gate = jax.nn.sigmoid(SIGMOID_SLOPE * expanded)
    active = (expanded * gate).astype(BF16)
    hidden[...] = active
    slope[...] = (gate + SIGMOID_SLOPE * expanded * gate * (1.0 - gate)).astype(BF16)
    split_lanes(mm_tn(active, cot[...]), deltas)


def forward_call(x, part, sib, vec, blocks, thresholds, cot):
    width = blocks[0].shape[1]
    tile = min(512, width)
    cols = pl.BlockSpec((PAD, tile), lambda t: (0, t))
    wspec = pl.BlockSpec((KB, tile), lambda t: (0, t))
    half = KB // 2
    return call(
        functools.partial(forward_kernel, tile),
        (width // tile,),
        [whole((PAD, D))] * 3
        + [whole(vec.shape)]
        + [wspec] * 4
        + [pl.BlockSpec((1, tile), lambda t: (0, t)), whole((PAD, D))],
        [whole((PAD, D)), whole((D, PAD)), cols, cols]
        + [pl.BlockSpec((tile, KB), lambda t: (t, 0))]
        + [pl.BlockSpec((tile, half), lambda t: (t, 0))] * 6,
        [sds((PAD, D), F32), sds((D, PAD)), sds((PAD, width)), sds((PAD, width)), sds((width, KB))]
        + [sds((width, half))] * 6,
        4 * PAD * D * width,
        4 * D * width + 14 * PAD * D + 4 * PAD * width,
        [pltpu.VMEM((PAD, D), BF16)],
        transcendentals=PAD * width,
    )(x, part, sib, vec, *blocks, thresholds, cot)


def backward_kernel(cot, n0, n1, n2, n3, slope, normed_t, w0, w1, w2, w3, *rest):
    part, thresholds_sum = rest[:2]
    deltas = rest[2:9]
    total = rest[9]
    step = pl.program_id(0)
    grad = None
    for k, n in enumerate((n0, n1, n2, n3)):
        term = mm_nt(cot[:, k * KB : (k + 1) * KB], n[...])
        grad = term if grad is None else grad + term
    grad = (grad * slope[...].astype(F32)).astype(BF16)
    thresholds_sum[...] = jnp.sum(grad.astype(F32), axis=0, keepdims=True)
    split_rows(mm(normed_t[...], grad), deltas)
    for k, w in enumerate((w0, w1, w2, w3)):
        at = slice(k * KB, (k + 1) * KB)
        term = mm_nt(grad, w[...])

        @pl.when(step == 0)
        def _():
            total[:, at] = term

        @pl.when(step > 0)
        def _():
            total[:, at] += term

    @pl.when(step == pl.num_programs(0) - 1)
    def _():
        part[...] = total[...].astype(BF16)


def backward_call(cot, narrow_blocks, slope, normed_t, wide_blocks):
    width = slope.shape[1]
    tile = min(512, width)
    half = KB // 2
    return call(
        backward_kernel,
        (width // tile,),
        [whole((PAD, D))]
        + [pl.BlockSpec((tile, KB), lambda t: (t, 0))] * 4
        + [pl.BlockSpec((PAD, tile), lambda t: (0, t)), whole((D, PAD))]
        + [pl.BlockSpec((KB, tile), lambda t: (0, t))] * 4,
        [whole((PAD, D)), pl.BlockSpec((1, tile), lambda t: (0, t)), pl.BlockSpec((KB, tile), lambda t: (0, t))]
        + [pl.BlockSpec((half, tile), lambda t: (0, t))] * 6,
        [sds((PAD, D)), sds((1, width), F32), sds((KB, width))] + [sds((half, width))] * 6,
        6 * PAD * D * width,
        6 * D * width + 6 * PAD * D + 2 * PAD * width,
        [pltpu.VMEM((PAD, D), F32)],
    )(cot, *narrow_blocks, slope, normed_t, *wide_blocks)


def narrow_kernel(hidden, n0, n1, n2, n3, part, total):
    step = pl.program_id(0)
    for k, n in enumerate((n0, n1, n2, n3)):
        at = slice(k * KB, (k + 1) * KB)
        term = mm(hidden[...], n[...])

        @pl.when(step == 0)
        def _():
            total[:, at] = term

        @pl.when(step > 0)
        def _():
            total[:, at] += term

    @pl.when(step == pl.num_programs(0) - 1)
    def _():
        part[...] = total[...].astype(BF16)


def narrow_call(hidden, blocks):
    width = hidden.shape[1]
    tile = min(512, width)
    return call(
        narrow_kernel,
        (width // tile,),
        [pl.BlockSpec((PAD, tile), lambda t: (0, t))] + [pl.BlockSpec((tile, KB), lambda t: (t, 0))] * 4,
        whole((PAD, D)),
        sds((PAD, D)),
        2 * PAD * D * width,
        2 * D * width + 2 * PAD * D + 2 * PAD * width,
        [pltpu.VMEM((PAD, D), F32)],
    )(hidden, *blocks)


def resid_kernel(part, sib, resid, cot, vec, mixed, w0, w1, w2, w3, *rest):
    grad_resid, grad_mixed, sums = rest[:3]
    deltas = rest[3:10]
    upstream = part[...].astype(F32) + sib[...].astype(F32)
    standard, reciprocal = standardize(resid[...])
    sums[0:1] = jnp.sum(upstream * standard, axis=0, keepdims=True)
    sums[1:2] = jnp.sum(upstream, axis=0, keepdims=True)
    grad = cot[...].astype(F32) + norm_backward(upstream, standard, reciprocal, vec[DILATION : DILATION + 1])
    sums[2:3] = jnp.sum(grad, axis=0, keepdims=True)
    sums[3:4] = jnp.sum(cot[...].astype(F32), axis=0, keepdims=True)
    sums[4:8] = jnp.zeros((4, D), F32)
    grad_resid[...] = grad
    rounded = grad.astype(BF16)
    total = None
    for k, w in enumerate((w0, w1, w2, w3)):
        term = mm_nt(rounded[:, k * KB : (k + 1) * KB], w[...])
        total = term if total is None else total + term
    grad_mixed[...] = total.astype(BF16)
    split_lanes(mm_tn(mixed[...], rounded), deltas)


def resid_call(part, sib, resid, cot, vec, mixed, blocks):
    width = mixed.shape[1]
    half = KB // 2
    return call(
        resid_kernel,
        (1,),
        [whole((PAD, D))] * 4 + [whole(vec.shape), whole((PAD, width))] + [whole((width, KB))] * 4,
        [whole((PAD, D)), whole((PAD, width)), whole((8, D)), whole((width, KB))] + [whole((width, half))] * 6,
        [sds((PAD, D), F32), sds((PAD, width)), sds((8, D), F32), sds((width, KB))] + [sds((width, half))] * 6,
        4 * PAD * D * width,
        14 * PAD * D + 4 * width * D + 4 * PAD * width,
    )(part, sib, resid, cot, vec, mixed, *blocks)


def attend_back_kernel(q, k, v, upstream, probs, grad_q, grad_k, grad_v):
    scaled = (q[...].astype(F32) * HD ** (-0.5)).astype(BF16)
    keys_t = (k[...].astype(F32) * HD ** (-0.5)).T.astype(BF16)
    values = v[...]
    up = upstream[...]
    grads_q = []
    kept_k = None
    kept_v = None
    for i in range(2):
        mask = head_mask(i, values.shape)
        rounded = probs[i]
        weights = rounded.astype(F32)
        picked = jnp.where(mask, values.astype(F32), 0.0).astype(BF16)
        weight_grad = mm_nt(picked, up)
        along = jnp.sum(weights * weight_grad, axis=0, keepdims=True)
        score_grad = (weights * (weight_grad - along)).astype(BF16)
        value_grad = mm(rounded, up)
        key_grad = mm(score_grad, scaled)
        kept_v = value_grad if i == 0 else jnp.where(mask, value_grad, kept_v)
        kept_k = key_grad if i == 0 else jnp.where(mask, key_grad, kept_k)
        grads_q.append(mm(keys_t[i * HD : (i + 1) * HD], score_grad))
    grad_q[...] = jnp.concatenate(grads_q, axis=0).T.astype(BF16)
    grad_k[...] = kept_k.astype(BF16)
    grad_v[...] = kept_v.astype(BF16)


def attend_back_call(qkv, upstream, probs):
    width = qkv.shape[1] // 3
    pairs = width // 128
    spec = lambda j: pl.BlockSpec((PAD, 128), lambda h, j=j: (0, j * pairs + h))
    return call(
        attend_back_kernel,
        (pairs,),
        [spec(0), spec(1), spec(2), spec(0), pl.BlockSpec((2, PAD, PAD), lambda h: (h, 0, 0))],
        [spec(0)] * 3,
        [sds((PAD, width))] * 3,
        pairs * 2 * 4 * 2 * PAD * PAD * 128,
        pairs * 2 * PAD * PAD * 2,
    )(qkv, qkv, qkv, upstream, probs)


def project_kernel(gq, gk, gv, normed_t, w0, w1, w2, w3, *rest):
    part, sums = rest[:2]
    deltas = rest[2:9]
    total = rest[9]
    step = pl.program_id(0)

    def one(g):
        grad = g[...]
        sums[0] = jnp.sum(grad.astype(F32), axis=0, keepdims=True)
        split_rows(mm(normed_t[...], grad), deltas)
        for k, w in enumerate((w0, w1, w2, w3)):
            at = slice(k * KB, (k + 1) * KB)
            term = mm_nt(grad, w[0])
            if g is gq:
                total[:, at] = term
            elif g is gk:
                total[:, at] += term
            else:
                part[:, at] = (total[:, at] + term).astype(BF16)

    for j, g in enumerate((gq, gk, gv)):
        pl.when(step == j)(lambda g=g: one(g))


def project_call(grads, normed_t, blocks):
    width = grads[0].shape[1]
    half = KB // 2
    return call(
        project_kernel,
        (3,),
        [whole((PAD, width))] * 3
        + [whole((D, PAD))]
        + [pl.BlockSpec((1, KB, width), lambda j: (j, 0, 0))] * 4,
        [whole((PAD, D)), pl.BlockSpec((1, 1, width), lambda j: (j, 0, 0)), pl.BlockSpec((KB, width), lambda j: (0, j))]
        + [pl.BlockSpec((half, width), lambda j: (0, j))] * 6,
        [sds((PAD, D)), sds((3, 1, width), F32), sds((KB, 3 * width))] + [sds((half, 3 * width))] * 6,
        4 * PAD * D * 3 * width,
        4 * D * 3 * width + 4 * PAD * D + 6 * PAD * width,
        [pltpu.VMEM((PAD, D), F32)],
    )(*grads, normed_t, *blocks)


def tokens_kernel(part, sib, x, grad_resid, cot, vec, delta, sums):
    upstream = part[...].astype(F32) + sib[...].astype(F32)
    standard, reciprocal = standardize(x[...].astype(F32))
    sums[0:1] = jnp.sum(upstream * standard, axis=0, keepdims=True)
    sums[1:2] = jnp.sum(upstream, axis=0, keepdims=True)
    sums[2:8] = jnp.zeros((6, D), F32)
    grad = grad_resid[...] + norm_backward(upstream, standard, reciprocal, vec[STRETCH : STRETCH + 1])
    delta[...] = (grad - cot[...].astype(F32)).astype(BF16)


def tokens_call(part, sib, x, grad_resid, cot, vec):
    return call(
        tokens_kernel,
        (1,),
        [whole((PAD, D))] * 5 + [whole(vec.shape)],
        [whole((PAD, D)), whole((8, D))],
        [sds((PAD, D)), sds((8, D), F32)],
        20 * PAD * D,
        14 * PAD * D,
    )(part, sib, x, grad_resid, cot, vec)


def swap(value, k):
    return lax.ppermute(value, "row", [(i, i ^ k) for i in range(RB)])


def after(value, *earlier):
    return lax.optimization_barrier((value,) + earlier)[0]


def sibling(part):
    size = lax.axis_size("col")
    if size == 2:
        return lax.ppermute(part, "col", [(0, 1), (1, 0)])
    total = None
    for s in range(1, size):
        term = lax.ppermute(part, "col", [(i, (i + s) % size) for i in range(size)]).astype(F32)
        total = term if total is None else total + term
    return total.astype(BF16)


def col_gather(value):
    size = lax.axis_size("col")
    if size == 2:
        other = lax.ppermute(value, "col", [(0, 1), (1, 0)])
        first = lax.axis_index("col") == 0
        return jnp.stack([jnp.where(first, value, other), jnp.where(first, other, value)], axis=-2)
    return lax.all_gather(value, "col", axis=value.ndim - 1)


def gather_blocks(block, axis, earlier):
    block = after(block, *earlier)
    near_x = swap(block, 1)
    near_y = swap(block, 2)
    size = block.shape[axis] // 2
    first = lax.slice_in_dim(near_x, 0, size, axis=axis)
    second = lax.slice_in_dim(near_y, size, 2 * size, axis=axis)
    far = jnp.concatenate([swap(first, 2), swap(second, 1)], axis=axis)
    return (block, near_x, near_y, far), (near_x, near_y)


def add(*terms):
    total = terms[0].astype(F32)
    for term in terms[1:]:
        total = total + term.astype(F32)
    return total.astype(terms[0].dtype)


def dp_sum(value):
    size = lax.axis_size("dp")
    if size == 1:
        return value
    if size % 2:
        return lax.psum(value, "dp")
    half = size // 2
    where = lax.axis_index("dp")
    for s in range(half - 1):
        value = add(value, lax.ppermute(value, "dp", [(s, s + 1), (size - 1 - s, size - 2 - s)]))
    value = add(value, lax.ppermute(value, "dp", [(half - 1, half), (half, half - 1)]))
    for s in reversed(range(half - 1)):
        moved = lax.ppermute(value, "dp", [(s + 1, s), (size - 2 - s, size - 1 - s)])
        value = jnp.where((where == s) | (where == size - 1 - s), moved, value)
    return value


def reduce_blocks(blocks, axis):
    own, x0, x1, y0, y1, far0, far1 = blocks
    via_x = swap(far0, 1)
    via_y = swap(far1, 2)
    half = own.shape[axis] // 2
    halves = (lax.slice_in_dim(own, 0, half, axis=axis), lax.slice_in_dim(own, half, 2 * half, axis=axis))
    first = add(halves[0], swap(x0, 1), swap(add(y0, via_x), 2))
    second = add(halves[1], swap(y1, 2), swap(add(x1, via_y), 1))
    return jnp.concatenate([dp_sum(first), dp_sum(second)], axis=axis).astype(F32)


def per_device(
    tokens,
    projector,
    offsets,
    combiner,
    baseline,
    widener,
    thresholds,
    narrower,
    residue,
    stretch,
    lifting,
    dilation,
    elevation,
    cotangent,
):
    row = lax.axis_index("row")
    columns = lax.axis_size("col")
    features = tokens.shape[1]
    width = projector.shape[2]

    def pick(stack, index):
        return lax.dynamic_index_in_dim(stack, index, 0, keepdims=False)

    def padded(value):
        return jnp.pad(value.reshape(RB, SEQ, features), ((0, 0), (0, PAD - SEQ), (0, 0)))

    def image_in(stack):
        near = jnp.stack([pick(stack, row)] + [swap(pick(stack, row ^ k), k) for k in range(1, RB)], axis=1)
        return col_gather(near).reshape(PAD, D)

    def image_out(value):
        mine = lax.dynamic_index_in_dim(
            value.reshape(PAD, RB, columns, features), lax.axis_index("col"), 2, keepdims=False
        )
        got = jnp.stack([mine[:SEQ, 0]] + [swap(mine[:SEQ, k], k) for k in range(1, RB)])
        return jnp.concatenate([pick(got, row ^ j) for j in range(RB)], axis=0)

    vectors = jnp.stack([stretch, lifting, baseline, dilation, elevation, residue, residue, residue])
    vec = jnp.stack([vectors] + [swap(vectors, k) for k in range(1, RB)], axis=1)
    vec = col_gather(vec).reshape(8, D)
    x = image_in(padded(tokens))
    project_w, sent = gather_blocks(projector, 1, (x,))
    combine_w, sent = gather_blocks(combiner, 0, sent)
    cot = image_in(padded(after(cotangent, *sent)))
    wide_w, sent = gather_blocks(widener, 0, sent)
    narrow_w, sent = gather_blocks(narrower, 0, sent)

    bias = jnp.stack([offsets[0], jnp.zeros((width,), F32), offsets[1]])[:, None]
    normed_one_t, qkv = qkv_call(x, vec, project_w, bias)
    mixed, probs = attend_call(qkv)
    part = combine_call(mixed, combine_w)
    out = forward_call(x, part, sibling(part), vec, wide_w, thresholds[None], cot)
    resid, normed_two_t, hidden, slope = out[:4]
    narrower_delta = reduce_blocks(out[4:11], 1)

    out = backward_call(cot, narrow_w, slope, normed_two_t, wide_w)
    part, thresholds_sum = out[:2]
    widener_delta = reduce_blocks(out[2:9], 0)
    out = resid_call(part, sibling(part), resid, cot, vec, mixed, combine_w)
    grad_resid, grad_mixed, sums_two = out[:3]
    combiner_delta = reduce_blocks(out[3:10], 1)
    grads = attend_back_call(qkv, grad_mixed, probs)
    out = project_call(grads, normed_one_t, project_w)
    part, grad_sums = out[:2]
    delta = reduce_blocks(out[2:9], 0)
    projector_delta = jnp.stack([delta[:, j * width : (j + 1) * width] for j in range(3)])
    delta, sums_one = tokens_call(part, sibling(part), x, grad_resid, cot, vec)
    tokens_delta = image_out(delta) + cotangent.astype(F32)

    ffn_part = narrow_call(hidden, narrow_w)
    ffn = ffn_part.astype(F32) + sibling(ffn_part).astype(F32) + vec[RESIDUE]
    layer_output = image_out((ffn + (resid - x.astype(F32))).astype(BF16)) + tokens.astype(F32)

    featured = jnp.concatenate([sums_one[:2], sums_two[:4]]).reshape(6, RB, columns, features)
    featured = lax.dynamic_index_in_dim(featured, lax.axis_index("col"), 2, keepdims=False)
    shared = jnp.concatenate([grad_sums[0, 0], grad_sums[2, 0], thresholds_sum[0]])
    pack = [jnp.concatenate([featured[:, k].reshape(-1), shared]) for k in range(RB)]
    small = dp_sum(add(pack[0], *[swap(pack[k], k) for k in range(1, RB)]))
    count = 6 * features
    vector = small[:count].reshape(6, features)
    offsets_delta = small[count : count + 2 * width].reshape(2, width)
    thresholds_delta = small[count + 2 * width :]
    return (
        layer_output,
        tokens_delta,
        projector_delta,
        offsets_delta,
        combiner_delta,
        vector[4],
        widener_delta,
        thresholds_delta,
        narrower_delta,
        vector[5],
        vector[0],
        vector[1],
        vector[2],
        vector[3],
    )


def solution(mesh):
    features = P(("row", "col"))
    specs = {
        "tokens": P("dp", ("row", "col")),
        "projector": P(None, "row", "col"),
        "offsets": P(None, "col"),
        "combiner": P("col", "row"),
        "baseline": features,
        "widener": P("row", "col"),
        "thresholds": P("col"),
        "narrower": P("col", "row"),
        "residue": features,
        "stretch": features,
        "lifting": features,
        "dilation": features,
        "elevation": features,
    }
    weights = tuple(specs.values())
    return jax.shard_map(
        per_device,
        mesh=mesh,
        in_specs=weights + (specs["tokens"],),
        out_specs=(specs["tokens"], specs["tokens"]) + weights[1:],
        check_vma=False,
    )
```

```python
import jax
import jax.numpy as jnp
from jax import lax
from jax.experimental import pallas as pl
from jax.experimental.pallas import tpu as pltpu
from jax.sharding import PartitionSpec as P

D = 1024
HD = 64
SEQ = 577
PAD = 592
RB = 4
KB = D // RB

NORM_EPSILON = 1e-05
SIGMOID_SLOPE = 1.702
F32 = jnp.float32
BF16 = jnp.bfloat16
VMEM_LIMIT = 60 * 1024 * 1024
SHRINK = 64
DEPTH = 2

STRETCH, LIFTING, BASELINE, DILATION, ELEVATION, RESIDUE = range(6)


def mm(a, b):
    return lax.dot_general(a, b, (((1,), (0,)), ((), ())), preferred_element_type=F32)


def mm_nt(a, b):
    return lax.dot_general(a, b, (((1,), (1,)), ((), ())), preferred_element_type=F32)


def mm_tn(a, b):
    return lax.dot_general(a, b, (((0,), (0,)), ((), ())), preferred_element_type=F32)


def sds(shape, dtype=BF16):
    return jax.ShapeDtypeStruct(shape, dtype)


def whole(shape):
    return pl.BlockSpec(shape, lambda *_: (0,) * len(shape))


def call(body, grid, in_specs, out_specs, out_shape, flops, nbytes, scratch=(), transcendentals=0):
    return pl.pallas_call(
        body,
        grid=grid,
        in_specs=in_specs,
        out_specs=out_specs,
        out_shape=out_shape,
        scratch_shapes=list(scratch),
        compiler_params=pltpu.CompilerParams(
            vmem_limit_bytes=VMEM_LIMIT, dimension_semantics=("arbitrary",) * len(grid)
        ),
        cost_estimate=pl.CostEstimate(
            flops=int(flops) // SHRINK, bytes_accessed=int(nbytes) // SHRINK, transcendentals=int(transcendentals) // SHRINK
        ),
    )


def row_mask(shape):
    return lax.broadcasted_iota(jnp.int32, shape, 0) < SEQ


def standardize(value):
    average = jnp.mean(value, axis=1, keepdims=True)
    centred = value - average
    spread = jnp.mean(centred * centred, axis=1, keepdims=True)
    reciprocal = lax.rsqrt(spread + NORM_EPSILON)
    return centred * reciprocal, reciprocal


def norm_backward(upstream, standard, reciprocal, gain):
    scaled = upstream * gain
    mean_scaled = jnp.mean(scaled, axis=1, keepdims=True)
    mean_along = jnp.mean(scaled * standard, axis=1, keepdims=True)
    return reciprocal * (scaled - mean_scaled - standard * mean_along)


def qkv_kernel(x, vec, *rest):
    weights, (bias, normed_t, qkv, normed) = rest[:5], rest[5:]

    @pl.when(pl.program_id(0) == 0)
    def _():
        standard, _r = standardize(x[...].astype(F32))
        value = standard * vec[STRETCH : STRETCH + 1] + vec[LIFTING : LIFTING + 1]
        normed[...] = value.astype(BF16)
        normed_t[...] = value.T.astype(BF16)

    total = bias[0]
    for k, w in enumerate(joined(weights)):
        total = total + mm(normed[:, k * KB : (k + 1) * KB], w)
    qkv[...] = total.astype(BF16)


def attn_specs(width, at):
    full = pl.BlockSpec((1, KB, width), lambda j: (at(j), 0, 0))
    half = pl.BlockSpec((1, KB // 2, width), lambda j: (at(j), 0, 0))
    return [full] * 3 + [half] * 2


def joined(weights):
    blocks = [w[...].reshape(w.shape[-2:]) for w in weights]
    return blocks[:3] + [jnp.concatenate(blocks[3:], axis=0)]


def qkv_call(x, vec, blocks, bias):
    width = blocks[0].shape[2]
    return call(
        qkv_kernel,
        (3,),
        [whole((PAD, D)), whole(vec.shape)]
        + attn_specs(width, lambda j: j)
        + [pl.BlockSpec((1, 1, width), lambda j: (j, 0, 0))],
        [whole((D, PAD)), pl.BlockSpec((PAD, width), lambda j: (0, j))],
        [sds((D, PAD)), sds((PAD, 3 * width))],
        2 * PAD * D * 3 * width,
        2 * D * 3 * width + 4 * PAD * D + 6 * PAD * width,
        [pltpu.VMEM((PAD, D), BF16)],
    )(x, vec, *blocks, bias)


def head_mask(i, shape):
    lane = lax.broadcasted_iota(jnp.int32, shape, 1)
    return (lane >= i * HD) & (lane < (i + 1) * HD)


def attend_kernel(q, k, v, mixed, probs):
    queries = q[...]
    keys = k[...]
    values_t = v[...].astype(F32).T.astype(BF16)
    outs = []
    for i in range(2):
        picked = jnp.where(head_mask(i, queries.shape), queries.astype(F32) * HD ** (-0.5), 0.0)
        scores = mm_nt(keys, picked.astype(BF16))
        scores = jnp.where(row_mask(scores.shape), scores, -1e30)
        top = jnp.max(scores, axis=0, keepdims=True)
        weights = jnp.exp(scores - top)
        total = jnp.sum(weights, axis=0, keepdims=True)
        rounded = (weights * (1.0 / total)).astype(BF16)
        probs[i] = rounded
        outs.append(mm(values_t[i * HD : (i + 1) * HD], rounded))
    mixed[...] = jnp.concatenate(outs, axis=0).T.astype(BF16)


def attend_call(qkv):
    width = qkv.shape[1] // 3
    pairs = width // 128
    spec = lambda j: pl.BlockSpec((PAD, 128), lambda h, j=j: (0, j * pairs + h))
    return call(
        attend_kernel,
        (pairs,),
        [spec(0), spec(1), spec(2)],
        [pl.BlockSpec((PAD, 128), lambda h: (0, h)), pl.BlockSpec((2, PAD, PAD), lambda h: (h, 0, 0))],
        [sds((PAD, width)), sds((2 * pairs, PAD, PAD))],
        pairs * 2 * 2 * 2 * PAD * PAD * 128,
        pairs * 2 * PAD * PAD * 2,
        transcendentals=pairs * 2 * PAD * PAD,
    )(qkv, qkv, qkv)


def combine_kernel(mixed, *rest):
    part = rest[5]
    for k, w in enumerate(joined(rest[:5])):
        part[:, k * KB : (k + 1) * KB] = mm_nt(mixed[...], w).astype(BF16)


def combine_call(mixed, blocks):
    width = mixed.shape[1]
    return call(
        combine_kernel,
        (1,),
        [whole((PAD, width))] + attn_specs(width, lambda i: 3),
        whole((PAD, D)),
        sds((PAD, D)),
        2 * PAD * D * width,
        2 * (PAD * D + width * D + PAD * width),
    )(mixed, *blocks)


def split_rows(value, refs):
    own, first_x, first_y, later_x, later_y = refs
    half = KB // 2
    value = value.astype(BF16)
    own[...] = value[:KB]
    first_x[:half] = value[6 * half : 7 * half]
    first_x[half:] = value[2 * half : 3 * half]
    first_y[:half] = value[7 * half :]
    first_y[half:] = value[5 * half : 6 * half]
    later_x[...] = value[3 * half : 4 * half]
    later_y[...] = value[4 * half : 5 * half]


def delta_specs(tile, at):
    half = KB // 2
    return [pl.BlockSpec((KB, tile), at)] * 3 + [pl.BlockSpec((half, tile), at)] * 2


def delta_shapes(width):
    half = KB // 2
    return [sds((KB, width))] * 3 + [sds((half, width))] * 2


def forward_kernel(x, part, sib, vec, *rest):
    weights, (thresholds, cot), rest = rest[:5], rest[5:7], rest[7:]
    resid, normed_t, hidden, slope = rest[:4]
    deltas = rest[4:9]
    normed, cot_t = rest[9:]

    @pl.when(pl.program_id(0) == 0)
    def _():
        total = x[...].astype(F32) + (part[...].astype(F32) + sib[...].astype(F32)) + vec[BASELINE : BASELINE + 1]
        total = jnp.where(row_mask(total.shape), total, 0.0)
        resid[...] = total
        standard, _r = standardize(total)
        value = standard * vec[DILATION : DILATION + 1] + vec[ELEVATION : ELEVATION + 1]
        normed[...] = value.astype(BF16)
        normed_t[...] = value.T.astype(BF16)
        cot_t[...] = cot[...].astype(F32).T.astype(BF16)

    expanded = thresholds[...]
    for k, w in enumerate(joined(weights)):
        expanded = expanded + mm(normed[:, k * KB : (k + 1) * KB], w)
    gate = jax.nn.sigmoid(SIGMOID_SLOPE * expanded)
    active = (expanded * gate).astype(BF16)
    hidden[...] = active
    slope[...] = (gate + SIGMOID_SLOPE * expanded * gate * (1.0 - gate)).astype(BF16)
    split_rows(mm(cot_t[...], active), deltas)


def forward_call(x, part, sib, vec, blocks, thresholds, cot):
    width = blocks[0].shape[1]
    tile = min(512, width)
    cols = pl.BlockSpec((PAD, tile), lambda t: (0, t))
    half = pl.BlockSpec((KB // 2, tile), lambda t: (0, t))
    wspecs = [pl.BlockSpec((KB, tile), lambda t: (0, t))] * 3 + [half] * 2
    return call(
        forward_kernel,
        (width // tile,),
        [whole((PAD, D))] * 3
        + [whole(vec.shape)]
        + wspecs
        + [pl.BlockSpec((1, tile), lambda t: (0, t)), whole((PAD, D))],
        [whole((PAD, D)), whole((D, PAD)), cols, cols] + delta_specs(tile, lambda t: (0, t)),
        [sds((PAD, D), F32), sds((D, PAD)), sds((PAD, width)), sds((PAD, width))] + delta_shapes(width),
        4 * PAD * D * width,
        4 * D * width + 14 * PAD * D + 4 * PAD * width,
        [pltpu.VMEM((PAD, D), BF16), pltpu.VMEM((D, PAD), BF16)],
        transcendentals=PAD * width,
    )(x, part, sib, vec, *blocks, thresholds, cot)


def backward_kernel(cot, *rest):
    narrow, (slope, normed_t), wide, rest = rest[:5], rest[5:7], rest[7:12], rest[12:]
    part, thresholds_sum = rest[:2]
    deltas = rest[2:7]
    total = rest[7]
    step = pl.program_id(0)
    grad = None
    for k, n in enumerate(narrow[:3]):
        term = mm_nt(cot[:, k * KB : (k + 1) * KB], n[...])
        grad = term if grad is None else grad + term
    far = jnp.concatenate([narrow[3][...], narrow[4][...]], axis=1)
    grad = grad + mm_nt(cot[:, 3 * KB :], far)
    grad = (grad * slope[...].astype(F32)).astype(BF16)
    thresholds_sum[...] = jnp.sum(grad.astype(F32), axis=0, keepdims=True)
    split_rows(mm(normed_t[...], grad), deltas)
    for k, w in enumerate(joined(wide)):
        at = slice(k * KB, (k + 1) * KB)
        term = mm_nt(grad, w)

        @pl.when(step == 0)
        def _():
            total[:, at] = term

        @pl.when(step > 0)
        def _():
            total[:, at] += term

    @pl.when(step == pl.num_programs(0) - 1)
    def _():
        part[...] = total[...].astype(BF16)


def narrow_specs(tile):
    half = pl.BlockSpec((tile, KB // 2), lambda t: (t, 0))
    return [pl.BlockSpec((tile, KB), lambda t: (t, 0))] * 3 + [half] * 2


def backward_call(cot, narrow_blocks, slope, normed_t, wide_blocks):
    width = slope.shape[1]
    tile = min(512, width)
    return call(
        backward_kernel,
        (width // tile,),
        [whole((PAD, D))]
        + narrow_specs(tile)
        + [pl.BlockSpec((PAD, tile), lambda t: (0, t)), whole((D, PAD))]
        + [pl.BlockSpec((KB, tile), lambda t: (0, t))] * 3
        + [pl.BlockSpec((KB // 2, tile), lambda t: (0, t))] * 2,
        [whole((PAD, D)), pl.BlockSpec((1, tile), lambda t: (0, t))] + delta_specs(tile, lambda t: (0, t)),
        [sds((PAD, D)), sds((1, width), F32)] + delta_shapes(width),
        6 * PAD * D * width,
        6 * D * width + 6 * PAD * D + 2 * PAD * width,
        [pltpu.VMEM((PAD, D), F32)],
    )(cot, *narrow_blocks, slope, normed_t, *wide_blocks)


def narrow_kernel(hidden, *rest):
    weights, (part, total) = rest[:5], rest[5:]
    step = pl.program_id(0)
    blocks = [n[...] for n in weights]
    blocks = blocks[:3] + [jnp.concatenate(blocks[3:], axis=1)]
    for k, n in enumerate(blocks):
        at = slice(k * KB, (k + 1) * KB)
        term = mm(hidden[...], n)

        @pl.when(step == 0)
        def _():
            total[:, at] = term

        @pl.when(step > 0)
        def _():
            total[:, at] += term

    @pl.when(step == pl.num_programs(0) - 1)
    def _():
        part[...] = total[...].astype(BF16)


def narrow_call(hidden, blocks):
    width = hidden.shape[1]
    tile = min(512, width)
    return call(
        narrow_kernel,
        (width // tile,),
        [pl.BlockSpec((PAD, tile), lambda t: (0, t))] + narrow_specs(tile),
        whole((PAD, D)),
        sds((PAD, D)),
        2 * PAD * D * width,
        2 * D * width + 2 * PAD * D + 2 * PAD * width,
        [pltpu.VMEM((PAD, D), F32)],
    )(hidden, *blocks)


def resid_kernel(part, sib, resid, cot, vec, *rest):
    weights, (grad_resid, grad_mixed, grad_t, sums) = rest[:5], rest[5:]
    upstream = part[...].astype(F32) + sib[...].astype(F32)
    standard, reciprocal = standardize(resid[...])
    sums[0:1] = jnp.sum(upstream * standard, axis=0, keepdims=True)
    sums[1:2] = jnp.sum(upstream, axis=0, keepdims=True)
    grad = cot[...].astype(F32) + norm_backward(upstream, standard, reciprocal, vec[DILATION : DILATION + 1])
    sums[2:3] = jnp.sum(grad, axis=0, keepdims=True)
    sums[3:4] = jnp.sum(cot[...].astype(F32), axis=0, keepdims=True)
    sums[4:8] = jnp.zeros((4, D), F32)
    grad_resid[...] = grad
    rounded = grad.astype(BF16)
    total = None
    for k, w in enumerate(joined(weights)):
        term = mm(rounded[:, k * KB : (k + 1) * KB], w)
        total = term if total is None else total + term
    grad_mixed[...] = total.astype(BF16)
    grad_t[...] = grad.T.astype(BF16)


def resid_call(part, sib, resid, cot, vec, blocks):
    width = blocks[0].shape[2]
    return call(
        resid_kernel,
        (1,),
        [whole((PAD, D))] * 4 + [whole(vec.shape)] + attn_specs(width, lambda i: 3),
        [whole((PAD, D)), whole((PAD, width)), whole((D, PAD)), whole((8, D))],
        [sds((PAD, D), F32), sds((PAD, width)), sds((D, PAD)), sds((8, D), F32)],
        2 * PAD * D * width,
        16 * PAD * D + 2 * width * D + 2 * PAD * width,
    )(part, sib, resid, cot, vec, *blocks)


def attend_back_kernel(q, k, v, upstream, probs, grad_q, grad_k, grad_v):
    scaled = (q[...].astype(F32) * HD ** (-0.5)).astype(BF16)
    keys_t = (k[...].astype(F32) * HD ** (-0.5)).T.astype(BF16)
    values = v[...]
    up = upstream[...]
    grads_q = []
    kept_k = None
    kept_v = None
    for i in range(2):
        mask = head_mask(i, values.shape)
        rounded = probs[i]
        weights = rounded.astype(F32)
        picked = jnp.where(mask, values.astype(F32), 0.0).astype(BF16)
        weight_grad = mm_nt(picked, up)
        along = jnp.sum(weights * weight_grad, axis=0, keepdims=True)
        score_grad = (weights * (weight_grad - along)).astype(BF16)
        value_grad = mm(rounded, up)
        key_grad = mm(score_grad, scaled)
        kept_v = value_grad if i == 0 else jnp.where(mask, value_grad, kept_v)
        kept_k = key_grad if i == 0 else jnp.where(mask, key_grad, kept_k)
        grads_q.append(mm(keys_t[i * HD : (i + 1) * HD], score_grad))
    grad_q[...] = jnp.concatenate(grads_q, axis=0).T.astype(BF16)
    grad_k[...] = kept_k.astype(BF16)
    grad_v[...] = kept_v.astype(BF16)


def attend_back_call(qkv, upstream, probs):
    width = qkv.shape[1] // 3
    pairs = width // 128
    spec = lambda j: pl.BlockSpec((PAD, 128), lambda h, j=j: (0, j * pairs + h))
    return call(
        attend_back_kernel,
        (pairs,),
        [spec(0), spec(1), spec(2), spec(0), pl.BlockSpec((2, PAD, PAD), lambda h: (h, 0, 0))],
        [spec(0)] * 3,
        [sds((PAD, width))] * 3,
        pairs * 2 * 4 * 2 * PAD * PAD * 128,
        pairs * 2 * PAD * PAD * 2,
    )(qkv, qkv, qkv, upstream, probs)


def project_kernel(gq, gk, gv, normed_t, grad_t, mixed, *rest):
    weights, (part, sums), deltas, total = rest[:5], rest[5:7], rest[7:12], rest[12]
    step = pl.program_id(0)

    def one(j, g):
        grad = g[...]
        sums[0] = jnp.sum(grad.astype(F32), axis=0, keepdims=True)
        split_rows(mm(normed_t[...], grad), deltas)
        for k, w in enumerate(joined(weights)):
            at = slice(k * KB, (k + 1) * KB)
            term = mm_nt(grad, w)
            if j == 0:
                total[:, at] = term
            elif j == 1:
                total[:, at] += term
            else:
                part[:, at] = (total[:, at] + term).astype(BF16)

    for j, g in enumerate((gq, gk, gv)):
        pl.when(step == j)(lambda j=j, g=g: one(j, g))

    @pl.when(step == 3)
    def _():
        split_rows(mm(grad_t[...], mixed[...]), deltas)


def project_call(grads, normed_t, grad_t, mixed, blocks):
    width = grads[0].shape[1]
    at = lambda j: jnp.minimum(j, 2)
    return call(
        project_kernel,
        (4,),
        [whole((PAD, width))] * 3 + [whole((D, PAD))] * 2 + [whole((PAD, width))] + attn_specs(width, at),
        [whole((PAD, D)), pl.BlockSpec((1, 1, width), lambda j: (at(j), 0, 0))]
        + delta_specs(width, lambda j: (0, j)),
        [sds((PAD, D)), sds((3, 1, width), F32)] + delta_shapes(4 * width),
        4 * PAD * D * 3 * width + 2 * PAD * D * width,
        4 * D * 4 * width + 6 * PAD * D + 6 * PAD * width,
        [pltpu.VMEM((PAD, D), F32)],
    )(*grads, normed_t, grad_t, mixed, *blocks)


def tokens_kernel(part, sib, x, grad_resid, cot, vec, delta, sums):
    upstream = part[...].astype(F32) + sib[...].astype(F32)
    standard, reciprocal = standardize(x[...].astype(F32))
    sums[0:1] = jnp.sum(upstream * standard, axis=0, keepdims=True)
    sums[1:2] = jnp.sum(upstream, axis=0, keepdims=True)
    sums[2:8] = jnp.zeros((6, D), F32)
    grad = grad_resid[...] + norm_backward(upstream, standard, reciprocal, vec[STRETCH : STRETCH + 1])
    delta[...] = (grad - cot[...].astype(F32)).astype(BF16)


def tokens_call(part, sib, x, grad_resid, cot, vec):
    return call(
        tokens_kernel,
        (1,),
        [whole((PAD, D))] * 5 + [whole(vec.shape)],
        [whole((PAD, D)), whole((8, D))],
        [sds((PAD, D)), sds((8, D), F32)],
        20 * PAD * D,
        14 * PAD * D,
    )(part, sib, x, grad_resid, cot, vec)


class Links:
    def __init__(self):
        self.sent = {1: [], 2: [], 3: [], "dp": []}

    def permute(self, value, axis, pairs, link):
        line = self.sent[link]
        if len(line) >= DEPTH:
            value = lax.optimization_barrier((value, line[-DEPTH]))[0]
        got = lax.ppermute(value, axis, pairs)
        line.append(got)
        return got

    def swap(self, value, k):
        return self.permute(value, "row", [(i, i ^ k) for i in range(RB)], k)

    def along(self, value, pairs):
        return self.permute(value, "dp", pairs, "dp")


def swap(value, k):
    return lax.ppermute(value, "row", [(i, i ^ k) for i in range(RB)])


def after(value, *earlier):
    return lax.optimization_barrier((value,) + earlier)[0]


def sibling(part):
    size = lax.axis_size("col")
    if size == 2:
        return lax.ppermute(part, "col", [(0, 1), (1, 0)])
    total = None
    for s in range(1, size):
        term = lax.ppermute(part, "col", [(i, (i + s) % size) for i in range(size)]).astype(F32)
        total = term if total is None else total + term
    return total.astype(BF16)


def col_gather(value):
    size = lax.axis_size("col")
    if size == 2:
        other = lax.ppermute(value, "col", [(0, 1), (1, 0)])
        first = lax.axis_index("col") == 0
        return jnp.stack([jnp.where(first, value, other), jnp.where(first, other, value)], axis=-2)
    return lax.all_gather(value, "col", axis=value.ndim - 1)


def gather_far(links, near, axis, *earlier):
    size = near[1].shape[axis] // 2
    near_x, near_y = [after(block, *earlier) for block in near[1:3]] if earlier else near[1:3]
    first = lax.slice_in_dim(near_x, 0, size, axis=axis)
    second = lax.slice_in_dim(near_y, size, 2 * size, axis=axis)
    return [links.swap(first, 2), links.swap(second, 1)]


def add(*terms):
    total = terms[0].astype(F32)
    for term in terms[1:]:
        total = total + term.astype(F32)
    return total.astype(terms[0].dtype)


def inward(values):
    size = lax.axis_size("dp")
    for s in range(size // 2 - 1):
        moved = [along(value, [(s, s + 1), (size - 1 - s, size - 2 - s)]) for value in values]
        values = [add(*pair) for pair in zip(values, moved)]
    return values


def across(values):
    half = lax.axis_size("dp") // 2
    moved = [along(value, [(half - 1, half), (half, half - 1)]) for value in values]
    return [add(*pair) for pair in zip(values, moved)]


def outward(values):
    size = lax.axis_size("dp")
    where = lax.axis_index("dp")
    for s in reversed(range(size // 2 - 1)):
        moved = [along(value, [(s + 1, s), (size - 2 - s, size - 1 - s)]) for value in values]
        outer = (where == s) | (where == size - 1 - s)
        values = [jnp.where(outer, new, value) for value, new in zip(values, moved)]
    return values


def along(self, value, pairs):
        return self.permute(value, "dp", pairs, "dp")


def swap(value, k):
    return lax.ppermute(value, "row", [(i, i ^ k) for i in range(RB)])


def after(value, *earlier):
    return lax.optimization_barrier((value,) + earlier)[0]


def sibling(part):
    size = lax.axis_size("col")
    if size == 2:
        return lax.ppermute(part, "col", [(0, 1), (1, 0)])
    total = None
    for s in range(1, size):
        term = lax.ppermute(part, "col", [(i, (i + s) % size) for i in range(size)]).astype(F32)
        total = term if total is None else total + term
    return total.astype(BF16)


def col_gather(value):
    size = lax.axis_size("col")
    if size == 2:
        other = lax.ppermute(value, "col", [(0, 1), (1, 0)])
        first = lax.axis_index("col") == 0
        return jnp.stack([jnp.where(first, value, other), jnp.where(first, other, value)], axis=-2)
    return lax.all_gather(value, "col", axis=value.ndim - 1)


def gather_far(links, near, axis, *earlier):
    size = near[1].shape[axis] // 2
    near_x, near_y = [after(block, *earlier) for block in near[1:3]] if earlier else near[1:3]
    first = lax.slice_in_dim(near_x, 0, size, axis=axis)
    second = lax.slice_in_dim(near_y, size, 2 * size, axis=axis)
    return [links.swap(first, 2), links.swap(second, 1)]


def add(*terms):
    total = terms[0].astype(F32)
    for term in terms[1:]:
        total = total + term.astype(F32)
    return total.astype(terms[0].dtype)


def dp_sum(values, permute):
    size = lax.axis_size("dp")
    if size == 1:
        return values
    if size % 2:
        return [lax.psum(value, "dp") for value in values]
    half = size // 2
    where = lax.axis_index("dp")
    for s in range(half - 1):
        moved = [permute(value, [(s, s + 1), (size - 1 - s, size - 2 - s)]) for value in values]
        values = [add(*pair) for pair in zip(values, moved)]
    moved = [permute(value, [(half - 1, half), (half, half - 1)]) for value in values]
    values = [add(*pair) for pair in zip(values, moved)]
    for s in reversed(range(half - 1)):
        moved = [permute(value, [(s + 1, s), (size - 2 - s, size - 1 - s)]) for value in values]
        outer = (where == s) | (where == size - 1 - s)
        values = [jnp.where(outer, new, value) for value, new in zip(values, moved)]
    return values


def along(value, pairs):
    return lax.ppermute(value, "dp", pairs)


def first_sends(blocks):
    return swap(blocks[1], 1), swap(blocks[2], 2)


def last_terms(blocks, came):
    return add(blocks[3], came[1][: KB // 2]), add(blocks[4], came[0][: KB // 2])


def last_sends(terms):
    return swap(terms[0], 1), swap(terms[1], 2)


def own_sums(blocks, came, last):
    half = KB // 2
    return add(blocks[0][:half], came[0][half:], last[1]), add(blocks[0][half:], came[1][half:], last[0])


def afters(values, *earlier):
    return [after(value, *earlier) for value in values]


def per_device(
    tokens,
    projector,
    offsets,
    combiner,
    baseline,
    widener,
    thresholds,
    narrower,
    residue,
    stretch,
    lifting,
    dilation,
    elevation,
    cotangent,
):
    row = lax.axis_index("row")
    columns = lax.axis_size("col")
    features = tokens.shape[1]
    width = projector.shape[2]

    links = Links()

    def pick(stack, index, axis=0):
        return lax.dynamic_index_in_dim(stack, index, axis, keepdims=False)

    def padded(value):
        return jnp.pad(value.reshape(RB, SEQ, features), ((0, 0), (0, PAD - SEQ), (0, 0)))

    def images_out(values):
        mine = pick(values.reshape(-1, PAD, RB, columns, features), lax.axis_index("col"), 3)
        mine = mine[:, :SEQ]
        got = jnp.stack([mine[:, :, 0]] + [swap(mine[:, :, k], k) for k in range(1, RB)])
        return jnp.concatenate([pick(got, row ^ j) for j in range(RB)], axis=1)

    vectors = jnp.stack([stretch, lifting, baseline, dilation, elevation, residue, residue, residue])
    vec = jnp.stack([vectors] + [links.swap(vectors, k) for k in range(1, RB)], axis=1)
    vec = col_gather(vec).reshape(8, D)
    both = jnp.stack([padded(tokens), padded(cotangent)])
    near = [pick(both, row, 1)] + [links.swap(pick(both, row ^ k, 1), k) for k in range(1, RB)]
    both = col_gather(jnp.stack(near, axis=2)).reshape(2, PAD, D)
    x, cot = both[0], both[1]
    attn = after(jnp.concatenate([projector, combiner.T[None]]), near[1], near[2])
    attn_w = [attn, links.swap(attn, 1), links.swap(attn, 2)]
    wide_w = [widener, links.swap(widener, 1), links.swap(widener, 2)]
    attn_w += gather_far(links, attn_w, 1)
    wide_w += gather_far(links, wide_w, 0)
    narrow_w = [narrower, links.swap(narrower, 1), links.swap(narrower, 2)]
    narrow_w += gather_far(links, narrow_w, 1)

    bias = jnp.stack([offsets[0], jnp.zeros((width,), F32), offsets[1]])[:, None]
    normed_one_t, qkv = qkv_call(x, vec, attn_w, bias)
    mixed, probs = attend_call(qkv)
    part = combine_call(mixed, attn_w)
    out = forward_call(x, part, sibling(after(part, *wide_w[3:])), vec, wide_w, thresholds[None], cot)
    resid, normed_two_t, hidden, slope = out[:4]
    blocks_n = afters(out[4:], *narrow_w[3:])
    came_n = first_sends(blocks_n)

    out = backward_call(cot, narrow_w, slope, normed_two_t, wide_w)
    part, thresholds_sum = out[:2]
    blocks_w = out[2:]
    terms_n = last_terms(blocks_n, afters(came_n, part))
    last_n = last_sends(terms_n)
    came_w = first_sends(afters(blocks_w, *terms_n))
    out = resid_call(part, sibling(after(part, *came_n)), resid, cot, vec, attn_w)
    grad_resid, grad_mixed, grad_t, sums_two = out
    halves_n = jnp.concatenate(own_sums(blocks_n, came_n, afters(last_n, grad_mixed)))
    sum_n = lax.psum(halves_n, "dp")
    grads = attend_back_call(qkv, after(grad_mixed, halves_n), probs)
    out = project_call(grads, normed_one_t, grad_t, mixed, attn_w)
    part, grad_sums = out[:2]
    came_w = afters(came_w, part)
    terms = last_terms(blocks_w, came_w)
    last_w = last_sends(terms)
    blocks_p = afters(out[2:], *terms)
    came_p = first_sends(blocks_p)
    halves_w = own_sums(blocks_w, came_w, afters(last_w, part))
    inner_w = inward([jnp.concatenate(halves_w)])
    middle_w = across(inner_w)
    widener_delta = outward(middle_w)[0].astype(F32)
    ffn_part = narrow_call(after(hidden, *halves_w), narrow_w)
    ffn_other = sibling(after(ffn_part, *inner_w))
    delta, sums_one = tokens_call(part, after(sibling(part), *came_p, *inner_w), x, grad_resid, cot, vec)
    last_p = last_sends(last_terms(blocks_p, came_p))
    halves_p = own_sums(blocks_p, came_p, last_p)

    featured = jnp.concatenate([sums_one[:2], sums_two[:4]]).reshape(6, RB, columns, features)
    featured = pick(featured, lax.axis_index("col"), 2)
    shared = jnp.concatenate([grad_sums[0, 0], grad_sums[2, 0], thresholds_sum[0]])
    pack = [jnp.concatenate([featured[:, k].reshape(-1), shared]) for k in range(RB)]
    small = add(pack[0], *[swap(after(pack[k], *halves_p), k) for k in range(1, RB)]).astype(BF16)
    size, line = small.shape[0], 4 * width
    lines = -(-size // (16 * line)) * 16
    small = jnp.pad(small, (0, lines * line - size)).reshape(lines, line)
    inner_p = inward([halves_p[0], jnp.concatenate([halves_p[1], small])])
    middle_p = across(inner_p)
    first, second = outward(middle_p)
    small = second[KB // 2 :].reshape(-1)[:size].astype(F32)
    total_p = jnp.concatenate([first, second[: KB // 2]]).astype(F32)
    projector_delta = jnp.stack([total_p[:, j * width : (j + 1) * width] for j in range(3)])
    combiner_delta = total_p[:, 3 * width :].T

    ffn = ffn_part.astype(F32) + ffn_other.astype(F32) + vec[RESIDUE]
    layer = (ffn + (resid - x.astype(F32))).astype(BF16)
    outs = images_out(after(jnp.stack([layer, delta]), *inner_p))
    layer_output = outs[0] + tokens.astype(F32)
    tokens_delta = outs[1] + cotangent.astype(F32)
    narrower_delta = after(sum_n, outs).astype(F32).T

    count = 6 * features
    vector = small[:count].reshape(6, features)
    offsets_delta = small[count : count + 2 * width].reshape(2, width)
    thresholds_delta = small[count + 2 * width :]
    return (
        layer_output,
        tokens_delta,
        projector_delta,
        offsets_delta,
        combiner_delta,
        vector[4],
        widener_delta,
        thresholds_delta,
        narrower_delta,
        vector[5],
        vector[0],
        vector[1],
        vector[2],
        vector[3],
    )


def solution(mesh):
    features = P(("row", "col"))
    specs = {
        "tokens": P("dp", ("row", "col")),
        "projector": P(None, "row", "col"),
        "offsets": P(None, "col"),
        "combiner": P("col", "row"),
        "baseline": features,
        "widener": P("row", "col"),
        "thresholds": P("col"),
        "narrower": P("col", "row"),
        "residue": features,
        "stretch": features,
        "lifting": features,
        "dilation": features,
        "elevation": features,
    }
    weights = tuple(specs.values())
    return jax.shard_map(
        per_device,
        mesh=mesh,
        in_specs=weights + (specs["tokens"],),
        out_specs=(specs["tokens"], specs["tokens"]) + weights[1:],
        check_vma=False,
    )
```

```python
import jax
import jax.numpy as jnp
from jax import lax
from jax.experimental import pallas as pl
from jax.experimental.pallas import tpu as pltpu
from jax.sharding import PartitionSpec as P

D = 1024
HD = 64
SEQ = 577
PAD = 592
RB = 4
KB = D // RB

NORM_EPSILON = 1e-05
SIGMOID_SLOPE = 1.702
F32 = jnp.float32
BF16 = jnp.bfloat16
VMEM_LIMIT = 60 * 1024 * 1024
SHRINK = 64
DEPTH = 2

STRETCH, LIFTING, BASELINE, DILATION, ELEVATION, RESIDUE = range(6)


def mm(a, b):
    return lax.dot_general(a, b, (((1,), (0,)), ((), ())), preferred_element_type=F32)


def mm_nt(a, b):
    return lax.dot_general(a, b, (((1,), (1,)), ((), ())), preferred_element_type=F32)


def mm_tn(a, b):
    return lax.dot_general(a, b, (((0,), (0,)), ((), ())), preferred_element_type=F32)


def sds(shape, dtype=BF16):
    return jax.ShapeDtypeStruct(shape, dtype)


def whole(shape):
    return pl.BlockSpec(shape, lambda *_: (0,) * len(shape))


def call(body, grid, in_specs, out_specs, out_shape, flops, nbytes, scratch=(), transcendentals=0):
    return pl.pallas_call(
        body,
        grid=grid,
        in_specs=in_specs,
        out_specs=out_specs,
        out_shape=out_shape,
        scratch_shapes=list(scratch),
        compiler_params=pltpu.CompilerParams(
            vmem_limit_bytes=VMEM_LIMIT, dimension_semantics=("arbitrary",) * len(grid)
        ),
        cost_estimate=pl.CostEstimate(
            flops=int(flops) // SHRINK, bytes_accessed=int(nbytes) // SHRINK, transcendentals=int(transcendentals) // SHRINK
        ),
    )


def row_mask(shape):
    return lax.broadcasted_iota(jnp.int32, shape, 0) < SEQ


def standardize(value):
    average = jnp.mean(value, axis=1, keepdims=True)
    centred = value - average
    spread = jnp.mean(centred * centred, axis=1, keepdims=True)
    reciprocal = lax.rsqrt(spread + NORM_EPSILON)
    return centred * reciprocal, reciprocal


def norm_backward(upstream, standard, reciprocal, gain):
    scaled = upstream * gain
    mean_scaled = jnp.mean(scaled, axis=1, keepdims=True)
    mean_along = jnp.mean(scaled * standard, axis=1, keepdims=True)
    return reciprocal * (scaled - mean_scaled - standard * mean_along)


def qkv_kernel(x, vec, *rest):
    weights, (bias, normed_t, qkv, normed) = rest[:5], rest[5:]

    @pl.when(pl.program_id(0) == 0)
    def _():
        standard, _r = standardize(x[...].astype(F32))
        value = standard * vec[STRETCH : STRETCH + 1] + vec[LIFTING : LIFTING + 1]
        normed[...] = value.astype(BF16)
        normed_t[...] = value.T.astype(BF16)

    total = bias[0]
    for k, w in enumerate(joined(weights)):
        total = total + mm(normed[:, k * KB : (k + 1) * KB], w)
    qkv[...] = total.astype(BF16)


def attn_specs(width, at):
    full = pl.BlockSpec((1, KB, width), lambda j: (at(j), 0, 0))
    half = pl.BlockSpec((1, KB // 2, width), lambda j: (at(j), 0, 0))
    return [full] * 3 + [half] * 2


def joined(weights):
    blocks = [w[...].reshape(w.shape[-2:]) for w in weights]
    return blocks[:3] + [jnp.concatenate(blocks[3:], axis=0)]


def qkv_call(x, vec, blocks, bias):
    width = blocks[0].shape[2]
    return call(
        qkv_kernel,
        (3,),
        [whole((PAD, D)), whole(vec.shape)]
        + attn_specs(width, lambda j: j)
        + [pl.BlockSpec((1, 1, width), lambda j: (j, 0, 0))],
        [whole((D, PAD)), pl.BlockSpec((PAD, width), lambda j: (0, j))],
        [sds((D, PAD)), sds((PAD, 3 * width))],
        2 * PAD * D * 3 * width,
        2 * D * 3 * width + 4 * PAD * D + 6 * PAD * width,
        [pltpu.VMEM((PAD, D), BF16)],
    )(x, vec, *blocks, bias)


def head_mask(i, shape):
    lane = lax.broadcasted_iota(jnp.int32, shape, 1)
    return (lane >= i * HD) & (lane < (i + 1) * HD)


def attend_kernel(q, k, v, mixed, probs):
    queries = q[...]
    keys = k[...]
    values_t = v[...].astype(F32).T.astype(BF16)
    outs = []
    for i in range(2):
        picked = jnp.where(head_mask(i, queries.shape), queries.astype(F32) * HD ** (-0.5), 0.0)
        scores = mm_nt(keys, picked.astype(BF16))
        scores = jnp.where(row_mask(scores.shape), scores, -1e30)
        top = jnp.max(scores, axis=0, keepdims=True)
        weights = jnp.exp(scores - top)
        total = jnp.sum(weights, axis=0, keepdims=True)
        rounded = (weights * (1.0 / total)).astype(BF16)
        probs[i] = rounded
        outs.append(mm(values_t[i * HD : (i + 1) * HD], rounded))
    mixed[...] = jnp.concatenate(outs, axis=0).T.astype(BF16)


def attend_call(qkv):
    width = qkv.shape[1] // 3
    pairs = width // 128
    spec = lambda j: pl.BlockSpec((PAD, 128), lambda h, j=j: (0, j * pairs + h))
    return call(
        attend_kernel,
        (pairs,),
        [spec(0), spec(1), spec(2)],
        [pl.BlockSpec((PAD, 128), lambda h: (0, h)), pl.BlockSpec((2, PAD, PAD), lambda h: (h, 0, 0))],
        [sds((PAD, width)), sds((2 * pairs, PAD, PAD))],
        pairs * 2 * 2 * 2 * PAD * PAD * 128,
        pairs * 2 * PAD * PAD * 2,
        transcendentals=pairs * 2 * PAD * PAD,
    )(qkv, qkv, qkv)


def combine_kernel(mixed, *rest):
    part = rest[5]
    for k, w in enumerate(joined(rest[:5])):
        part[:, k * KB : (k + 1) * KB] = mm_nt(mixed[...], w).astype(BF16)


def combine_call(mixed, blocks):
    width = mixed.shape[1]
    return call(
        combine_kernel,
        (1,),
        [whole((PAD, width))] + attn_specs(width, lambda i: 3),
        whole((PAD, D)),
        sds((PAD, D)),
        2 * PAD * D * width,
        2 * (PAD * D + width * D + PAD * width),
    )(mixed, *blocks)


def split_rows(value, refs):
    own, first_x, first_y, later_x, later_y = refs
    half = KB // 2
    value = value.astype(BF16)
    own[...] = value[:KB]
    first_x[:half] = value[6 * half : 7 * half]
    first_x[half:] = value[2 * half : 3 * half]
    first_y[:half] = value[7 * half :]
    first_y[half:] = value[5 * half : 6 * half]
    later_x[...] = value[3 * half : 4 * half]
    later_y[...] = value[4 * half : 5 * half]


def delta_specs(tile, at):
    half = KB // 2
    return [pl.BlockSpec((KB, tile), at)] * 3 + [pl.BlockSpec((half, tile), at)] * 2


def delta_shapes(width):
    half = KB // 2
    return [sds((KB, width))] * 3 + [sds((half, width))] * 2


def forward_kernel(x, part, sib, vec, *rest):
    weights, (thresholds, cot), rest = rest[:5], rest[5:7], rest[7:]
    resid, normed_t, hidden, slope = rest[:4]
    deltas = rest[4:9]
    normed, cot_t = rest[9:]

    @pl.when(pl.program_id(0) == 0)
    def _():
        total = x[...].astype(F32) + (part[...].astype(F32) + sib[...].astype(F32)) + vec[BASELINE : BASELINE + 1]
        total = jnp.where(row_mask(total.shape), total, 0.0)
        resid[...] = total
        standard, _r = standardize(total)
        value = standard * vec[DILATION : DILATION + 1] + vec[ELEVATION : ELEVATION + 1]
        normed[...] = value.astype(BF16)
        normed_t[...] = value.T.astype(BF16)
        cot_t[...] = cot[...].astype(F32).T.astype(BF16)

    expanded = thresholds[...]
    for k, w in enumerate(joined(weights)):
        expanded = expanded + mm(normed[:, k * KB : (k + 1) * KB], w)
    gate = jax.nn.sigmoid(SIGMOID_SLOPE * expanded)
    active = (expanded * gate).astype(BF16)
    hidden[...] = active
    slope[...] = (gate + SIGMOID_SLOPE * expanded * gate * (1.0 - gate)).astype(BF16)
    split_rows(mm(cot_t[...], active), deltas)


def forward_call(x, part, sib, vec, blocks, thresholds, cot):
    width = blocks[0].shape[1]
    tile = min(512, width)
    cols = pl.BlockSpec((PAD, tile), lambda t: (0, t))
    half = pl.BlockSpec((KB // 2, tile), lambda t: (0, t))
    wspecs = [pl.BlockSpec((KB, tile), lambda t: (0, t))] * 3 + [half] * 2
    return call(
        forward_kernel,
        (width // tile,),
        [whole((PAD, D))] * 3
        + [whole(vec.shape)]
        + wspecs
        + [pl.BlockSpec((1, tile), lambda t: (0, t)), whole((PAD, D))],
        [whole((PAD, D)), whole((D, PAD)), cols, cols] + delta_specs(tile, lambda t: (0, t)),
        [sds((PAD, D), F32), sds((D, PAD)), sds((PAD, width)), sds((PAD, width))] + delta_shapes(width),
        4 * PAD * D * width,
        4 * D * width + 14 * PAD * D + 4 * PAD * width,
        [pltpu.VMEM((PAD, D), BF16), pltpu.VMEM((D, PAD), BF16)],
        transcendentals=PAD * width,
    )(x, part, sib, vec, *blocks, thresholds, cot)


def accumulate(total, at, term):
    step = pl.program_id(0)

    @pl.when(step == 0)
    def _():
        total[:, at] = term

    @pl.when(step > 0)
    def _():
        total[:, at] += term


def backward_kernel(cot, *rest):
    narrow, (slope, hidden, normed_t), wide, rest = rest[:5], rest[5:8], rest[8:13], rest[13:]
    part, out, thresholds_sum = rest[:3]
    deltas, (total, out_total) = rest[3:8], rest[8:]
    grad = None
    blocks = [n[...] for n in narrow]
    blocks = blocks[:3] + [jnp.concatenate(blocks[3:], axis=1)]
    for k, n in enumerate(blocks):
        at = slice(k * KB, (k + 1) * KB)
        term = mm_nt(cot[:, at], n)
        grad = term if grad is None else grad + term
        accumulate(out_total, at, mm(hidden[...], n))
    grad = (grad * slope[...].astype(F32)).astype(BF16)
    thresholds_sum[...] = jnp.sum(grad.astype(F32), axis=0, keepdims=True)
    split_rows(mm(normed_t[...], grad), deltas)
    for k, w in enumerate(joined(wide)):
        accumulate(total, slice(k * KB, (k + 1) * KB), mm_nt(grad, w))

    @pl.when(pl.program_id(0) == pl.num_programs(0) - 1)
    def _():
        part[...] = total[...].astype(BF16)
        out[...] = out_total[...].astype(BF16)


def narrow_specs(tile):
    half = pl.BlockSpec((tile, KB // 2), lambda t: (t, 0))
    return [pl.BlockSpec((tile, KB), lambda t: (t, 0))] * 3 + [half] * 2


def backward_call(cot, narrow_blocks, slope, hidden, normed_t, wide_blocks):
    width = slope.shape[1]
    tile = min(512, width)
    cols = pl.BlockSpec((PAD, tile), lambda t: (0, t))
    return call(
        backward_kernel,
        (width // tile,),
        [whole((PAD, D))]
        + narrow_specs(tile)
        + [cols, cols, whole((D, PAD))]
        + [pl.BlockSpec((KB, tile), lambda t: (0, t))] * 3
        + [pl.BlockSpec((KB // 2, tile), lambda t: (0, t))] * 2,
        [whole((PAD, D))] * 2 + [pl.BlockSpec((1, tile), lambda t: (0, t))] + delta_specs(tile, lambda t: (0, t)),
        [sds((PAD, D))] * 2 + [sds((1, width), F32)] + delta_shapes(width),
        8 * PAD * D * width,
        6 * D * width + 8 * PAD * D + 4 * PAD * width,
        [pltpu.VMEM((PAD, D), F32)] * 2,
    )(cot, *narrow_blocks, slope, hidden, normed_t, *wide_blocks)


def resid_kernel(part, sib, resid, cot, vec, *rest):
    weights, (grad_resid, grad_mixed, grad_t, sums) = rest[:5], rest[5:]
    upstream = part[...].astype(F32) + sib[...].astype(F32)
    standard, reciprocal = standardize(resid[...])
    sums[0:1] = jnp.sum(upstream * standard, axis=0, keepdims=True)
    sums[1:2] = jnp.sum(upstream, axis=0, keepdims=True)
    grad = cot[...].astype(F32) + norm_backward(upstream, standard, reciprocal, vec[DILATION : DILATION + 1])
    sums[2:3] = jnp.sum(grad, axis=0, keepdims=True)
    sums[3:4] = jnp.sum(cot[...].astype(F32), axis=0, keepdims=True)
    sums[4:8] = jnp.zeros((4, D), F32)
    grad_resid[...] = grad
    rounded = grad.astype(BF16)
    total = None
    for k, w in enumerate(joined(weights)):
        term = mm(rounded[:, k * KB : (k + 1) * KB], w)
        total = term if total is None else total + term
    grad_mixed[...] = total.astype(BF16)
    grad_t[...] = grad.T.astype(BF16)


def resid_call(part, sib, resid, cot, vec, blocks):
    width = blocks[0].shape[2]
    return call(
        resid_kernel,
        (1,),
        [whole((PAD, D))] * 4 + [whole(vec.shape)] + attn_specs(width, lambda i: 3),
        [whole((PAD, D)), whole((PAD, width)), whole((D, PAD)), whole((8, D))],
        [sds((PAD, D), F32), sds((PAD, width)), sds((D, PAD)), sds((8, D), F32)],
        2 * PAD * D * width,
        16 * PAD * D + 2 * width * D + 2 * PAD * width,
    )(part, sib, resid, cot, vec, *blocks)


def attend_back_kernel(q, k, v, upstream, probs, grad_q, grad_k, grad_v):
    scaled = (q[...].astype(F32) * HD ** (-0.5)).astype(BF16)
    keys_t = (k[...].astype(F32) * HD ** (-0.5)).T.astype(BF16)
    values = v[...]
    up = upstream[...]
    grads_q = []
    kept_k = None
    kept_v = None
    for i in range(2):
        mask = head_mask(i, values.shape)
        rounded = probs[i]
        weights = rounded.astype(F32)
        picked = jnp.where(mask, values.astype(F32), 0.0).astype(BF16)
        weight_grad = mm_nt(picked, up)
        along = jnp.sum(weights * weight_grad, axis=0, keepdims=True)
        score_grad = (weights * (weight_grad - along)).astype(BF16)
        value_grad = mm(rounded, up)
        key_grad = mm(score_grad, scaled)
        kept_v = value_grad if i == 0 else jnp.where(mask, value_grad, kept_v)
        kept_k = key_grad if i == 0 else jnp.where(mask, key_grad, kept_k)
        grads_q.append(mm(keys_t[i * HD : (i + 1) * HD], score_grad))
    grad_q[...] = jnp.concatenate(grads_q, axis=0).T.astype(BF16)
    grad_k[...] = kept_k.astype(BF16)
    grad_v[...] = kept_v.astype(BF16)


def attend_back_call(qkv, upstream, probs):
    width = qkv.shape[1] // 3
    pairs = width // 128
    spec = lambda j: pl.BlockSpec((PAD, 128), lambda h, j=j: (0, j * pairs + h))
    return call(
        attend_back_kernel,
        (pairs,),
        [spec(0), spec(1), spec(2), spec(0), pl.BlockSpec((2, PAD, PAD), lambda h: (h, 0, 0))],
        [spec(0)] * 3,
        [sds((PAD, width))] * 3,
        pairs * 2 * 4 * 2 * PAD * PAD * 128,
        pairs * 2 * PAD * PAD * 2,
    )(qkv, qkv, qkv, upstream, probs)


def project_kernel(gq, gk, gv, normed_t, grad_t, mixed, *rest):
    weights, (part, sums), deltas, total = rest[:5], rest[5:7], rest[7:12], rest[12]
    step = pl.program_id(0)

    def one(j, g):
        grad = g[...]
        sums[0] = jnp.sum(grad.astype(F32), axis=0, keepdims=True)
        split_rows(mm(normed_t[...], grad), deltas)
        for k, w in enumerate(joined(weights)):
            at = slice(k * KB, (k + 1) * KB)
            term = mm_nt(grad, w)
            if j == 0:
                total[:, at] = term
            elif j == 1:
                total[:, at] += term
            else:
                part[:, at] = (total[:, at] + term).astype(BF16)

    for j, g in enumerate((gq, gk, gv)):
        pl.when(step == j)(lambda j=j, g=g: one(j, g))

    @pl.when(step == 3)
    def _():
        split_rows(mm(grad_t[...], mixed[...]), deltas)


def project_call(grads, normed_t, grad_t, mixed, blocks):
    width = grads[0].shape[1]
    at = lambda j: jnp.minimum(j, 2)
    return call(
        project_kernel,
        (4,),
        [whole((PAD, width))] * 3 + [whole((D, PAD))] * 2 + [whole((PAD, width))] + attn_specs(width, at),
        [whole((PAD, D)), pl.BlockSpec((1, 1, width), lambda j: (at(j), 0, 0))]
        + delta_specs(width, lambda j: (0, j)),
        [sds((PAD, D)), sds((3, 1, width), F32)] + delta_shapes(4 * width),
        4 * PAD * D * 3 * width + 2 * PAD * D * width,
        4 * D * 4 * width + 6 * PAD * D + 6 * PAD * width,
        [pltpu.VMEM((PAD, D), F32)],
    )(*grads, normed_t, grad_t, mixed, *blocks)


def tokens_kernel(part, sib, x, grad_resid, cot, vec, delta, sums):
    upstream = part[...].astype(F32) + sib[...].astype(F32)
    standard, reciprocal = standardize(x[...].astype(F32))
    sums[0:1] = jnp.sum(upstream * standard, axis=0, keepdims=True)
    sums[1:2] = jnp.sum(upstream, axis=0, keepdims=True)
    sums[2:8] = jnp.zeros((6, D), F32)
    grad = grad_resid[...] + norm_backward(upstream, standard, reciprocal, vec[STRETCH : STRETCH + 1])
    delta[...] = (grad - cot[...].astype(F32)).astype(BF16)


def tokens_call(part, sib, x, grad_resid, cot, vec):
    return call(
        tokens_kernel,
        (1,),
        [whole((PAD, D))] * 5 + [whole(vec.shape)],
        [whole((PAD, D)), whole((8, D))],
        [sds((PAD, D)), sds((8, D), F32)],
        20 * PAD * D,
        14 * PAD * D,
    )(part, sib, x, grad_resid, cot, vec)


class Links:
    def __init__(self):
        self.sent = {1: [], 2: [], 3: [], "dp": []}

    def permute(self, value, axis, pairs, link):
        line = self.sent[link]
        if len(line) >= DEPTH:
            value = lax.optimization_barrier((value, line[-DEPTH]))[0]
        got = lax.ppermute(value, axis, pairs)
        line.append(got)
        return got

    def swap(self, value, k):
        return self.permute(value, "row", [(i, i ^ k) for i in range(RB)], k)

    def along(self, value, pairs):
        return self.permute(value, "dp", pairs, "dp")


def swap(value, k):
    return lax.ppermute(value, "row", [(i, i ^ k) for i in range(RB)])


def after(value, *earlier):
    return lax.optimization_barrier((value,) + earlier)[0]


def sibling(part):
    size = lax.axis_size("col")
    if size == 2:
        return lax.ppermute(part, "col", [(0, 1), (1, 0)])
    total = None
    for s in range(1, size):
        term = lax.ppermute(part, "col", [(i, (i + s) % size) for i in range(size)]).astype(F32)
        total = term if total is None else total + term
    return total.astype(BF16)


def col_gather(value):
    size = lax.axis_size("col")
    if size == 2:
        other = lax.ppermute(value, "col", [(0, 1), (1, 0)])
        first = lax.axis_index("col") == 0
        return jnp.stack([jnp.where(first, value, other), jnp.where(first, other, value)], axis=-2)
    return lax.all_gather(value, "col", axis=value.ndim - 1)


def gather_far(links, near, axis, *earlier):
    size = near[1].shape[axis] // 2
    near_x, near_y = [after(block, *earlier) for block in near[1:3]] if earlier else near[1:3]
    first = lax.slice_in_dim(near_x, 0, size, axis=axis)
    second = lax.slice_in_dim(near_y, size, 2 * size, axis=axis)
    return [links.swap(first, 2), links.swap(second, 1)]


def add(*terms):
    total = terms[0].astype(F32)
    for term in terms[1:]:
        total = total + term.astype(F32)
    return total.astype(terms[0].dtype)


class Clock:
    def __init__(self):
        self.last = ()

    def __call__(self, *values):
        values = lax.optimization_barrier(tuple(values) + self.last)[: len(values)]
        self.last = values[:1]
        return values


class LineSum:
    def __init__(self, clock, value):
        size = lax.axis_size("dp")
        half = size // 2
        inward = [(s, s + 1) for s in range(half - 1)]
        self.clock = clock
        self.value = value
        if size % 2:
            self.value = lax.psum(value, "dp")
            self.steps = []
            return
        self.steps = [(None, [pair, (size - 1 - pair[0], size - 1 - pair[1])]) for pair in inward]
        self.steps.append((None, [(half - 1, half), (half, half - 1)]))
        for s, t in reversed(inward):
            self.steps.append((s, [(t, s), (size - 1 - t, size - 1 - s)]))
        self.send()

    def send(self):
        if self.steps:
            self.moved = lax.ppermute(self.value, "dp", self.steps[0][1])

    def advance(self):
        if not self.steps:
            return
        moved = self.clock(self.moved)[0]
        outer, pairs = self.steps.pop(0)
        if outer is None:
            self.value = add(self.value, moved)
        else:
            where = lax.axis_index("dp")
            far = lax.axis_size("dp") - 1 - outer
            self.value = jnp.where((where == outer) | (where == far), moved, self.value)
        self.send()


def first_sends(blocks):
    return swap(blocks[1], 1), swap(blocks[2], 2)


def last_terms(blocks, came):
    return add(blocks[3], came[1][: KB // 2]), add(blocks[4], came[0][: KB // 2])


def last_sends(terms):
    return swap(terms[0], 1), swap(terms[1], 2)


def own_sums(blocks, came, last):
    half = KB // 2
    return add(blocks[0][:half], came[0][half:], last[1]), add(blocks[0][half:], came[1][half:], last[0])


def afters(values, *earlier):
    return [after(value, *earlier) for value in values]


def per_device(
    tokens,
    projector,
    offsets,
    combiner,
    baseline,
    widener,
    thresholds,
    narrower,
    residue,
    stretch,
    lifting,
    dilation,
    elevation,
    cotangent,
):
    row = lax.axis_index("row")
    columns = lax.axis_size("col")
    features = tokens.shape[1]
    width = projector.shape[2]

    links = Links()

    def pick(stack, index, axis=0):
        return lax.dynamic_index_in_dim(stack, index, axis, keepdims=False)

    def padded(value):
        return jnp.pad(value.reshape(RB, SEQ, features), ((0, 0), (0, PAD - SEQ), (0, 0)))

    def images_out(values, clock):
        mine = pick(values.reshape(-1, PAD, RB, columns, features), lax.axis_index("col"), 3)
        mine = mine[:, :SEQ]
        sent = clock(*[swap(mine[:, :, k], k) for k in range(1, RB)])
        got = jnp.stack([mine[:, :, 0], *sent])
        return jnp.concatenate([pick(got, row ^ j) for j in range(RB)], axis=1)

    vectors = jnp.stack([stretch, lifting, baseline, dilation, elevation, residue, residue, residue])
    vec = jnp.stack([vectors] + [links.swap(vectors, k) for k in range(1, RB)], axis=1)
    vec = col_gather(vec).reshape(8, D)
    both = jnp.stack([padded(tokens), padded(cotangent)])
    near = [pick(both, row, 1)] + [links.swap(pick(both, row ^ k, 1), k) for k in range(1, RB)]
    both = col_gather(jnp.stack(near, axis=2)).reshape(2, PAD, D)
    x, cot = both[0], both[1]
    attn = after(jnp.concatenate([projector, combiner.T[None]]), near[1], near[2])
    attn_w = [attn, links.swap(attn, 1), links.swap(attn, 2)]
    wide_w = [widener, links.swap(widener, 1), links.swap(widener, 2)]
    attn_w += gather_far(links, attn_w, 1)
    wide_w += gather_far(links, wide_w, 0)
    narrow_w = [narrower, links.swap(narrower, 1), links.swap(narrower, 2)]
    narrow_w += gather_far(links, narrow_w, 1)

    bias = jnp.stack([offsets[0], jnp.zeros((width,), F32), offsets[1]])[:, None]
    normed_one_t, qkv = qkv_call(x, vec, attn_w, bias)
    mixed, probs = attend_call(qkv)
    part = combine_call(mixed, attn_w)
    out = forward_call(x, part, sibling(after(part, *wide_w[3:])), vec, wide_w, thresholds[None], cot)
    resid, normed_two_t, hidden, slope = out[:4]
    blocks_n = afters(out[4:], *narrow_w[3:])
    came_n = first_sends(blocks_n)

    clock = Clock()
    out = backward_call(cot, narrow_w, slope, hidden, normed_two_t, wide_w)
    part, ffn_part, thresholds_sum = out[:3]
    blocks_w = out[3:]
    *came_n, part = clock(*came_n, part)
    terms = last_terms(blocks_n, came_n)
    last_n = last_sends(terms)
    came_w = first_sends(afters(blocks_w, *terms))
    grad_resid, grad_mixed, grad_t, sums_two = resid_call(part, sibling(part), resid, cot, vec, attn_w)
    *last_n, grad_mixed = clock(*last_n, grad_mixed)
    halves = jnp.concatenate(own_sums(blocks_n, came_n, last_n))
    sum_n = LineSum(clock, halves)
    grads = attend_back_call(qkv, after(grad_mixed, halves), probs)
    out = project_call(grads, normed_one_t, grad_t, mixed, attn_w)
    part, grad_sums = out[:2]
    *came_w, part = clock(*came_w, part)
    terms = last_terms(blocks_w, came_w)
    last_w = last_sends(terms)
    sum_n.advance()
    blocks_p = afters(out[2:], *terms)
    came_p = first_sends(blocks_p)
    last_w = clock(*last_w)
    sum_w = LineSum(clock, jnp.concatenate(own_sums(blocks_w, came_w, last_w)))
    other = sibling(after(part, *last_w))
    sum_n.advance()
    came_p = clock(*came_p)
    last_p = last_sends(last_terms(blocks_p, came_p))
    other = clock(other)[0]
    delta, sums_one = tokens_call(part, other, x, grad_resid, cot, vec)
    sum_w.advance()
    last_p = clock(*last_p)
    halves_p = own_sums(blocks_p, came_p, last_p)
    sum_p = [LineSum(clock, halves_p[0])]

    featured = jnp.concatenate([sums_one[:2], sums_two[:4]]).reshape(6, RB, columns, features)
    featured = pick(featured, lax.axis_index("col"), 2)
    shared = jnp.concatenate([grad_sums[0, 0], grad_sums[2, 0], thresholds_sum[0]])
    pack = [jnp.concatenate([featured[:, k].reshape(-1), shared]) for k in range(RB)]
    sent = clock(*[swap(after(pack[k], *halves_p), k) for k in range(1, RB)])
    small = add(pack[0], *sent).astype(BF16)
    size, line = small.shape[0], 4 * width
    lines = -(-size // (16 * line)) * 16
    small = jnp.pad(small, (0, lines * line - size)).reshape(lines, line)
    sum_p.append(LineSum(clock, jnp.concatenate([halves_p[1], small])))
    ffn_other = sibling(after(ffn_part, *sent))
    sum_n.advance()
    sum_p[0].advance()
    sum_w.advance()
    sum_p[1].advance()
    ffn_other = clock(ffn_other)[0]
    ffn = ffn_part.astype(F32) + ffn_other.astype(F32) + vec[RESIDUE]
    layer = (ffn + (resid - x.astype(F32))).astype(BF16)
    sum_p[0].advance()
    sum_p[1].advance()
    outs = images_out(jnp.stack([layer, delta]), clock)
    layer_output = outs[0] + tokens.astype(F32)
    tokens_delta = outs[1] + cotangent.astype(F32)
    for line_sum in (sum_n, sum_w, *sum_p):
        while line_sum.steps:
            line_sum.advance()
    narrower_delta = sum_n.value.astype(F32).T
    widener_delta = sum_w.value.astype(F32)
    first, second = [line_sum.value for line_sum in sum_p]
    small = second[KB // 2 :].reshape(-1)[:size].astype(F32)
    total_p = jnp.concatenate([first, second[: KB // 2]]).astype(F32)
    projector_delta = jnp.stack([total_p[:, j * width : (j + 1) * width] for j in range(3)])
    combiner_delta = total_p[:, 3 * width :].T

    count = 6 * features
    vector = small[:count].reshape(6, features)
    offsets_delta = small[count : count + 2 * width].reshape(2, width)
    thresholds_delta = small[count + 2 * width :]
    return (
        layer_output,
        tokens_delta,
        projector_delta,
        offsets_delta,
        combiner_delta,
        vector[4],
        widener_delta,
        thresholds_delta,
        narrower_delta,
        vector[5],
        vector[0],
        vector[1],
        vector[2],
        vector[3],
    )


def solution(mesh):
    features = P(("row", "col"))
    specs = {
        "tokens": P("dp", ("row", "col")),
        "projector": P(None, "row", "col"),
        "offsets": P(None, "col"),
        "combiner": P("col", "row"),
        "baseline": features,
        "widener": P("row", "col"),
        "thresholds": P("col"),
        "narrower": P("col", "row"),
        "residue": features,
        "stretch": features,
        "lifting": features,
        "dilation": features,
        "elevation": features,
    }
    weights = tuple(specs.values())
    return jax.shard_map(
        per_device,
        mesh=mesh,
        in_specs=weights + (specs["tokens"],),
        out_specs=(specs["tokens"], specs["tokens"]) + weights[1:],
        check_vma=False,
    )
```

```python
import jax
import jax.numpy as jnp
from jax import lax
from jax.experimental import pallas as pl
from jax.experimental.pallas import tpu as pltpu
from jax.sharding import PartitionSpec as P

D = 1024
HD = 64
SEQ = 577
PAD = 592
RB = 4
KB = D // RB
PLANE = 96
SHARED = 80
TOP = 304

NORM_EPSILON = 1e-05
SIGMOID_SLOPE = 1.702
F32 = jnp.float32
BF16 = jnp.bfloat16
VMEM_LIMIT = 60 * 1024 * 1024
SHRINK = 64
DEPTH = 2

STRETCH, LIFTING, BASELINE, DILATION, ELEVATION, RESIDUE = range(6)


def mm(a, b):
    return lax.dot_general(a, b, (((1,), (0,)), ((), ())), preferred_element_type=F32)


def mm_nt(a, b):
    return lax.dot_general(a, b, (((1,), (1,)), ((), ())), preferred_element_type=F32)


def mm_tn(a, b):
    return lax.dot_general(a, b, (((0,), (0,)), ((), ())), preferred_element_type=F32)


def sds(shape, dtype=BF16):
    return jax.ShapeDtypeStruct(shape, dtype)


def whole(shape):
    return pl.BlockSpec(shape, lambda *_: (0,) * len(shape))


def call(body, grid, in_specs, out_specs, out_shape, flops, nbytes, scratch=(), transcendentals=0):
    return pl.pallas_call(
        body,
        grid=grid,
        in_specs=in_specs,
        out_specs=out_specs,
        out_shape=out_shape,
        scratch_shapes=list(scratch),
        compiler_params=pltpu.CompilerParams(
            vmem_limit_bytes=VMEM_LIMIT, dimension_semantics=("arbitrary",) * len(grid)
        ),
        cost_estimate=pl.CostEstimate(
            flops=int(flops) // SHRINK, bytes_accessed=int(nbytes) // SHRINK, transcendentals=int(transcendentals) // SHRINK
        ),
    )


PIECES = (TOP, PAD - TOP)


def piece_specs():
    return [pl.BlockSpec((rows, D), lambda *step: (0, 0)) for rows in PIECES]


def piece_shapes():
    return [sds((rows, D)) for rows in PIECES]


def store_pieces(refs, value):
    refs[0][...] = value[:TOP].astype(BF16)
    refs[1][...] = value[TOP:].astype(BF16)


def load_sum(pieces):
    top, bottom, other_top, other_bottom = [piece[...].astype(F32) for piece in pieces]
    return jnp.concatenate([top + other_top, bottom + other_bottom], axis=0)


def row_mask(shape):
    return lax.broadcasted_iota(jnp.int32, shape, 0) < SEQ


def standardize(value):
    average = jnp.mean(value, axis=1, keepdims=True)
    centred = value - average
    spread = jnp.mean(centred * centred, axis=1, keepdims=True)
    reciprocal = lax.rsqrt(spread + NORM_EPSILON)
    return centred * reciprocal, reciprocal


def norm_backward(upstream, standard, reciprocal, gain):
    scaled = upstream * gain
    mean_scaled = jnp.mean(scaled, axis=1, keepdims=True)
    mean_along = jnp.mean(scaled * standard, axis=1, keepdims=True)
    return reciprocal * (scaled - mean_scaled - standard * mean_along)


def qkv_kernel(x, vec, *rest):
    weights, (bias, normed_t, qkv, normed, buffer) = rest[:9], rest[9:]

    @pl.when(pl.program_id(0) == 0)
    def _():
        standard, _r = standardize(x[...].astype(F32))
        value = standard * vec[STRETCH : STRETCH + 1] + vec[LIFTING : LIFTING + 1]
        normed[...] = value.astype(BF16)
        normed_t[...] = value.T.astype(BF16)

    total = bias[0]
    for k, w in enumerate(joined(weights, buffer)):
        total = total + mm(normed[:, k * KB : (k + 1) * KB], w)
    qkv[...] = total.astype(BF16)


BLOCK_ROWS = (KB, PLANE + SHARED, PLANE + SHARED, PLANE, SHARED, SHARED, SHARED, SHARED)


def weight_specs(tile, at):
    pieces = [pl.BlockSpec((rows, tile), lambda *step: (0, at(*step))) for rows in BLOCK_ROWS]
    return [pl.BlockSpec(memory_space=pltpu.SMEM)] + pieces


def plain_specs(tile, at):
    half = pl.BlockSpec((KB // 2, tile), lambda *step: (0, at(*step)))
    return [pl.BlockSpec((KB, tile), lambda *step: (0, at(*step)))] * 3 + [half] * 2


def weight_buffer(tile):
    return pltpu.VMEM((RB - 1, KB, tile), BF16)


def joined(pieces, buffer):
    plane, own, near_x, near_y, far_plane, far_shared, other_x, other_y, other_far = pieces
    mine = pl.multiple_of(PLANE + SHARED * plane[0], 16)
    others = pl.multiple_of(PLANE + SHARED * (1 - plane[0]), 16)
    for k, (near, other) in enumerate(((near_x, other_x), (near_y, other_y))):
        buffer[k, :PLANE] = near[:PLANE]
        buffer[k, pl.ds(mine, SHARED)] = near[PLANE:]
        buffer[k, pl.ds(others, SHARED)] = other[...]
    buffer[2, :PLANE] = far_plane[...]
    buffer[2, pl.ds(mine, SHARED)] = far_shared[...]
    buffer[2, pl.ds(others, SHARED)] = other_far[...]
    return [own[...], buffer[0], buffer[1], buffer[2]]


def qkv_call(x, vec, blocks, bias):
    width = bias.shape[2]
    return call(
        qkv_kernel,
        (3,),
        [whole((PAD, D)), whole(vec.shape)]
        + weight_specs(width, lambda j: j)
        + [pl.BlockSpec((1, 1, width), lambda j: (j, 0, 0))],
        [whole((D, PAD)), pl.BlockSpec((PAD, width), lambda j: (0, j))],
        [sds((D, PAD)), sds((PAD, 3 * width))],
        2 * PAD * D * 3 * width,
        2 * D * 3 * width + 4 * PAD * D + 6 * PAD * width,
        [pltpu.VMEM((PAD, D), BF16), weight_buffer(width)],
    )(x, vec, *blocks, bias)


def head_mask(i, shape):
    lane = lax.broadcasted_iota(jnp.int32, shape, 1)
    return (lane >= i * HD) & (lane < (i + 1) * HD)


def attend_kernel(q, k, v, mixed, probs):
    queries = q[...]
    keys = k[...]
    values_t = v[...].astype(F32).T.astype(BF16)
    outs = []
    for i in range(2):
        picked = jnp.where(head_mask(i, queries.shape), queries.astype(F32) * HD ** (-0.5), 0.0)
        scores = mm_nt(keys, picked.astype(BF16))
        scores = jnp.where(row_mask(scores.shape), scores, -1e30)
        top = jnp.max(scores, axis=0, keepdims=True)
        weights = jnp.exp(scores - top)
        total = jnp.sum(weights, axis=0, keepdims=True)
        rounded = (weights * (1.0 / total)).astype(BF16)
        probs[i] = rounded
        outs.append(mm(values_t[i * HD : (i + 1) * HD], rounded))
    mixed[...] = jnp.concatenate(outs, axis=0).T.astype(BF16)


def attend_call(qkv):
    width = qkv.shape[1] // 3
    pairs = width // 128
    spec = lambda j: pl.BlockSpec((PAD, 128), lambda h, j=j: (0, j * pairs + h))
    return call(
        attend_kernel,
        (pairs,),
        [spec(0), spec(1), spec(2)],
        [pl.BlockSpec((PAD, 128), lambda h: (0, h)), pl.BlockSpec((2, PAD, PAD), lambda h: (h, 0, 0))],
        [sds((PAD, width)), sds((2 * pairs, PAD, PAD))],
        pairs * 2 * 2 * 2 * PAD * PAD * 128,
        pairs * 2 * PAD * PAD * 2,
        transcendentals=pairs * 2 * PAD * PAD,
    )(qkv, qkv, qkv)


def combine_kernel(mixed, *rest):
    top, bottom, buffer = rest[9:]
    for k, w in enumerate(joined(rest[:9], buffer)):
        term = mm_nt(mixed[...], w).astype(BF16)
        top[:, k * KB : (k + 1) * KB] = term[:TOP]
        bottom[:, k * KB : (k + 1) * KB] = term[TOP:]


def combine_call(mixed, blocks):
    width = mixed.shape[1]
    return call(
        combine_kernel,
        (1,),
        [whole((PAD, width))] + weight_specs(width, lambda i: 3),
        piece_specs(),
        piece_shapes(),
        2 * PAD * D * width,
        2 * (PAD * D + width * D + PAD * width),
        [weight_buffer(width)],
    )(mixed, *blocks)


def split_rows(value, refs):
    own, first_x, first_y, later_x, later_y = refs
    half = KB // 2
    value = value.astype(BF16)
    own[...] = value[:KB]
    first_x[:half] = value[6 * half : 7 * half]
    first_x[half:] = value[2 * half : 3 * half]
    first_y[:half] = value[7 * half :]
    first_y[half:] = value[5 * half : 6 * half]
    later_x[...] = value[3 * half : 4 * half]
    later_y[...] = value[4 * half : 5 * half]


def delta_specs(tile, at):
    half = KB // 2
    return [pl.BlockSpec((KB, tile), at)] * 3 + [pl.BlockSpec((half, tile), at)] * 2


def delta_shapes(width):
    half = KB // 2
    return [sds((KB, width))] * 3 + [sds((half, width))] * 2


def forward_kernel(x, *rest):
    parts, vec, rest = rest[:4], rest[4], rest[5:]
    weights, (thresholds, cot), rest = rest[:9], rest[9:11], rest[11:]
    resid, normed_t, hidden, slope = rest[:4]
    deltas = rest[4:9]
    normed, cot_t, buffer = rest[9:]

    @pl.when(pl.program_id(0) == 0)
    def _():
        total = x[...].astype(F32) + load_sum(parts) + vec[BASELINE : BASELINE + 1]
        total = jnp.where(row_mask(total.shape), total, 0.0)
        resid[...] = total
        standard, _r = standardize(total)
        value = standard * vec[DILATION : DILATION + 1] + vec[ELEVATION : ELEVATION + 1]
        normed[...] = value.astype(BF16)
        normed_t[...] = value.T.astype(BF16)
        cot_t[...] = cot[...].astype(F32).T.astype(BF16)

    expanded = thresholds[...]
    for k, w in enumerate(joined(weights, buffer)):
        expanded = expanded + mm(normed[:, k * KB : (k + 1) * KB], w)
    gate = jax.nn.sigmoid(SIGMOID_SLOPE * expanded)
    active = (expanded * gate).astype(BF16)
    hidden[...] = active
    slope[...] = (gate + SIGMOID_SLOPE * expanded * gate * (1.0 - gate)).astype(BF16)
    split_rows(mm(cot_t[...], active), deltas)


def forward_call(x, parts, vec, blocks, thresholds, cot):
    width = thresholds.shape[1]
    tile = min(512, width)
    cols = pl.BlockSpec((PAD, tile), lambda t: (0, t))
    return call(
        forward_kernel,
        (width // tile,),
        [whole((PAD, D))]
        + piece_specs() * 2
        + [whole(vec.shape)]
        + weight_specs(tile, lambda t: t)
        + [pl.BlockSpec((1, tile), lambda t: (0, t)), whole((PAD, D))],
        [whole((PAD, D)), whole((D, PAD)), cols, cols] + delta_specs(tile, lambda t: (0, t)),
        [sds((PAD, D), F32), sds((D, PAD)), sds((PAD, width)), sds((PAD, width))] + delta_shapes(width),
        4 * PAD * D * width,
        4 * D * width + 14 * PAD * D + 4 * PAD * width,
        [pltpu.VMEM((PAD, D), BF16), pltpu.VMEM((D, PAD), BF16), weight_buffer(tile)],
        transcendentals=PAD * width,
    )(x, *parts, vec, *blocks, thresholds, cot)


def accumulate(total, at, term):
    step = pl.program_id(0)

    @pl.when(step == 0)
    def _():
        total[:, at] = term

    @pl.when(step > 0)
    def _():
        total[:, at] += term


def backward_kernel(cot, *rest):
    narrow, (slope, hidden, normed_t), wide, rest = rest[:5], rest[5:8], rest[8:17], rest[17:]
    part, out, thresholds_sum = rest[:2], rest[2:4], rest[4]
    deltas, (total, out_total, wide_buffer) = rest[5:10], rest[10:]
    grad = None
    blocks = [n[...] for n in narrow]
    blocks = blocks[:3] + [jnp.concatenate(blocks[3:], axis=0)]
    for k, n in enumerate(blocks):
        at = slice(k * KB, (k + 1) * KB)
        term = mm(cot[:, at], n)
        grad = term if grad is None else grad + term
        accumulate(out_total, at, mm_nt(hidden[...], n))
    grad = (grad * slope[...].astype(F32)).astype(BF16)
    thresholds_sum[...] = jnp.sum(grad.astype(F32), axis=0, keepdims=True)
    split_rows(mm(normed_t[...], grad), deltas)
    for k, w in enumerate(joined(wide, wide_buffer)):
        accumulate(total, slice(k * KB, (k + 1) * KB), mm_nt(grad, w))

    @pl.when(pl.program_id(0) == pl.num_programs(0) - 1)
    def _():
        store_pieces(part, total[...])
        store_pieces(out, out_total[...])


def backward_call(cot, narrow_blocks, slope, hidden, normed_t, wide_blocks):
    width = slope.shape[1]
    tile = min(512, width)
    cols = pl.BlockSpec((PAD, tile), lambda t: (0, t))
    return call(
        backward_kernel,
        (width // tile,),
        [whole((PAD, D))]
        + plain_specs(tile, lambda t: t)
        + [cols, cols, whole((D, PAD))]
        + weight_specs(tile, lambda t: t),
        piece_specs() * 2 + [pl.BlockSpec((1, tile), lambda t: (0, t))] + delta_specs(tile, lambda t: (0, t)),
        piece_shapes() * 2 + [sds((1, width), F32)] + delta_shapes(width),
        8 * PAD * D * width,
        6 * D * width + 8 * PAD * D + 4 * PAD * width,
        [pltpu.VMEM((PAD, D), F32)] * 2 + [weight_buffer(tile)],
    )(cot, *narrow_blocks, slope, hidden, normed_t, *wide_blocks)


def resid_kernel(*rest):
    parts, (resid, cot, vec), rest = rest[:4], rest[4:7], rest[7:]
    weights, (grad_resid, grad_mixed, grad_t, sums, buffer) = rest[:9], rest[9:]
    upstream = load_sum(parts)
    standard, reciprocal = standardize(resid[...])
    sums[0:1] = jnp.sum(upstream * standard, axis=0, keepdims=True)
    sums[1:2] = jnp.sum(upstream, axis=0, keepdims=True)
    grad = cot[...].astype(F32) + norm_backward(upstream, standard, reciprocal, vec[DILATION : DILATION + 1])
    sums[2:3] = jnp.sum(grad, axis=0, keepdims=True)
    sums[3:4] = jnp.sum(cot[...].astype(F32), axis=0, keepdims=True)
    sums[4:8] = jnp.zeros((4, D), F32)
    grad_resid[...] = grad
    rounded = grad.astype(BF16)
    total = None
    for k, w in enumerate(joined(weights, buffer)):
        term = mm(rounded[:, k * KB : (k + 1) * KB], w)
        total = term if total is None else total + term
    grad_mixed[...] = total.astype(BF16)
    grad_t[...] = grad.T.astype(BF16)


def resid_call(parts, resid, cot, vec, blocks):
    width = blocks[1].shape[1] // 4
    return call(
        resid_kernel,
        (1,),
        piece_specs() * 2 + [whole((PAD, D))] * 2 + [whole(vec.shape)] + weight_specs(width, lambda i: 3),
        [whole((PAD, D)), whole((PAD, width)), whole((D, PAD)), whole((8, D))],
        [sds((PAD, D), F32), sds((PAD, width)), sds((D, PAD)), sds((8, D), F32)],
        2 * PAD * D * width,
        16 * PAD * D + 2 * width * D + 2 * PAD * width,
        [weight_buffer(width)],
    )(*parts, resid, cot, vec, *blocks)


def attend_back_kernel(q, k, v, upstream, probs, grad_q, grad_k, grad_v):
    scaled = (q[...].astype(F32) * HD ** (-0.5)).astype(BF16)
    keys_t = (k[...].astype(F32) * HD ** (-0.5)).T.astype(BF16)
    values = v[...]
    up = upstream[...]
    grads_q = []
    kept_k = None
    kept_v = None
    for i in range(2):
        mask = head_mask(i, values.shape)
        rounded = probs[i]
        weights = rounded.astype(F32)
        picked = jnp.where(mask, values.astype(F32), 0.0).astype(BF16)
        weight_grad = mm_nt(picked, up)
        along = jnp.sum(weights * weight_grad, axis=0, keepdims=True)
        score_grad = (weights * (weight_grad - along)).astype(BF16)
        value_grad = mm(rounded, up)
        key_grad = mm(score_grad, scaled)
        kept_v = value_grad if i == 0 else jnp.where(mask, value_grad, kept_v)
        kept_k = key_grad if i == 0 else jnp.where(mask, key_grad, kept_k)
        grads_q.append(mm(keys_t[i * HD : (i + 1) * HD], score_grad))
    grad_q[...] = jnp.concatenate(grads_q, axis=0).T.astype(BF16)
    grad_k[...] = kept_k.astype(BF16)
    grad_v[...] = kept_v.astype(BF16)


def attend_back_call(qkv, upstream, probs):
    width = qkv.shape[1] // 3
    pairs = width // 128
    spec = lambda j: pl.BlockSpec((PAD, 128), lambda h, j=j: (0, j * pairs + h))
    return call(
        attend_back_kernel,
        (pairs,),
        [spec(0), spec(1), spec(2), spec(0), pl.BlockSpec((2, PAD, PAD), lambda h: (h, 0, 0))],
        [spec(0)] * 3,
        [sds((PAD, width))] * 3,
        pairs * 2 * 4 * 2 * PAD * PAD * 128,
        pairs * 2 * PAD * PAD * 2,
    )(qkv, qkv, qkv, upstream, probs)


def project_kernel(gq, gk, gv, normed_t, grad_t, mixed, *rest):
    weights, part, sums, deltas, (total, buffer) = rest[:9], rest[9:11], rest[11], rest[12:17], rest[17:]
    step = pl.program_id(0)

    def one(j, g):
        grad = g[...]
        sums[0] = jnp.sum(grad.astype(F32), axis=0, keepdims=True)
        split_rows(mm(normed_t[...], grad), deltas)
        for k, w in enumerate(joined(weights, buffer)):
            at = slice(k * KB, (k + 1) * KB)
            term = mm_nt(grad, w)
            if j == 0:
                total[:, at] = term
            else:
                total[:, at] += term
        if j == 2:
            store_pieces(part, total[...])

    for j, g in enumerate((gq, gk, gv)):
        pl.when(step == j)(lambda j=j, g=g: one(j, g))

    @pl.when(step == 3)
    def _():
        split_rows(mm(grad_t[...], mixed[...]), deltas)


def project_call(grads, normed_t, grad_t, mixed, blocks):
    width = grads[0].shape[1]
    at = lambda j: jnp.minimum(j, 2)
    return call(
        project_kernel,
        (4,),
        [whole((PAD, width))] * 3 + [whole((D, PAD))] * 2 + [whole((PAD, width))] + weight_specs(width, at),
        piece_specs()
        + [pl.BlockSpec((1, 1, width), lambda j: (at(j), 0, 0))]
        + delta_specs(width, lambda j: (0, j)),
        piece_shapes() + [sds((3, 1, width), F32)] + delta_shapes(4 * width),
        4 * PAD * D * 3 * width + 2 * PAD * D * width,
        4 * D * 4 * width + 6 * PAD * D + 6 * PAD * width,
        [pltpu.VMEM((PAD, D), F32), weight_buffer(width)],
    )(*grads, normed_t, grad_t, mixed, *blocks)


def share(refs, at, value):
    owners, _rows, features = refs.shape
    for i in range(owners):
        refs[i, at : at + PAD] = value[:, i * features : (i + 1) * features].astype(BF16)


def tokens_kernel(*refs):
    parts, ffn_parts, (x, resid, grad_resid, cot, vec, deltas, sums) = refs[:4], refs[4:8], refs[8:]
    upstream = load_sum(parts)
    tokens = x[...].astype(F32)
    standard, reciprocal = standardize(tokens)
    sums[0:1] = jnp.sum(upstream * standard, axis=0, keepdims=True)
    sums[1:2] = jnp.sum(upstream, axis=0, keepdims=True)
    sums[2:8] = jnp.zeros((6, D), F32)
    share(deltas, 0, load_sum(ffn_parts) + vec[RESIDUE : RESIDUE + 1] + (resid[...] - tokens))
    grad = grad_resid[...] + norm_backward(upstream, standard, reciprocal, vec[STRETCH : STRETCH + 1])
    share(deltas, PAD, grad - cot[...].astype(F32))


def tokens_call(parts, ffn_parts, x, resid, grad_resid, cot, vec, features):
    return call(
        tokens_kernel,
        (1,),
        piece_specs() * 4 + [whole((PAD, D))] * 4 + [whole(vec.shape)],
        [whole((D // features, 2 * PAD, features)), whole((8, D))],
        [sds((D // features, 2 * PAD, features)), sds((8, D), F32)],
        24 * PAD * D,
        24 * PAD * D,
    )(*parts, *ffn_parts, x, resid, grad_resid, cot, vec)


def images_kernel(got, tokens, cot, layer, delta):
    for j in range(RB):
        at = slice(j * SEQ, (j + 1) * SEQ)
        layer[at] = got[j, :SEQ].astype(F32) + tokens[at].astype(F32)
        delta[at] = got[j, PAD : PAD + SEQ].astype(F32) + cot[at].astype(F32)


def images_call(got, tokens, cot):
    rows, features = tokens.shape
    return call(
        images_kernel,
        (1,),
        [whole(got.shape), whole((rows, features)), whole((rows, features))],
        [whole((rows, features))] * 2,
        [sds((rows, features), F32)] * 2,
        4 * rows * features,
        16 * rows * features,
    )(got, tokens, cot)


def swap(value, k):
    return lax.ppermute(value, "row", [(i, i ^ k) for i in range(RB)])


def after(value, *earlier):
    return lax.optimization_barrier((value,) + earlier)[0]


def sibling(part):
    size = lax.axis_size("col")
    if size == 2:
        return lax.ppermute(part, "col", [(0, 1), (1, 0)])
    total = None
    for s in range(1, size):
        term = lax.ppermute(part, "col", [(i, (i + s) % size) for i in range(size)]).astype(F32)
        total = term if total is None else total + term
    return total.astype(BF16)


def col_gather(values):
    size = lax.axis_size("col")
    lanes = values[0].shape[1]
    wide = jnp.concatenate(values, axis=1)
    if size == 2:
        other = lax.ppermute(wide, "col", [(0, 1), (1, 0)])
        first = lax.axis_index("col") == 0
        columns = [jnp.where(first, wide, other), jnp.where(first, other, wide)]
    else:
        columns = list(lax.all_gather(wide, "col"))
    parts = [column[:, k * lanes : (k + 1) * lanes] for k in range(len(values)) for column in columns]
    return jnp.concatenate(parts, axis=1)


class Gather:
    def __init__(self, clock, weight, *earlier):
        self.clock = clock
        self.plane = lax.axis_index("dp") % 2
        self.weight = weight
        shared = lax.dynamic_slice_in_dim(weight, PLANE + SHARED * self.plane, SHARED, axis=0)
        mine = after(jnp.concatenate([weight[:PLANE], shared]), *earlier)
        self.near = [swap(mine, 1), swap(mine, 2)]

    def across(self, value):
        return lax.ppermute(value, "dp", [(i, i ^ 1) for i in range(lax.axis_size("dp"))])

    def relay(self):
        near_x, near_y = self.near = self.clock(*self.near)
        self.far = [swap(near_x[:PLANE], 2), swap(near_y[PLANE:], 1)]
        self.other = [self.across(near_x[PLANE:]), self.across(near_y[PLANE:])]

    def hand_over(self, *earlier):
        *self.far, self.other[0] = self.clock(*self.far, self.other[0], *earlier)[:3]
        self.other.append(self.across(self.far[1]))

    def pieces(self):
        self.other[1:] = self.clock(*self.other[1:])
        return [self.plane.astype(jnp.int32)[None], self.weight, *self.near, *self.far, *self.other]


def add(*terms):
    total = terms[0].astype(F32)
    for term in terms[1:]:
        total = total + term.astype(F32)
    return total.astype(terms[0].dtype)


class Clock:
    def __init__(self):
        self.last = ()

    def __call__(self, *values):
        values = lax.optimization_barrier(tuple(values) + self.last)[: len(values)]
        self.last = values[:1]
        return values


class LineSum:
    def __init__(self, clock, value):
        size = lax.axis_size("dp")
        half = size // 2
        inward = [(s, s + 1) for s in range(half - 1)]
        self.clock = clock
        self.value = value
        if size % 2:
            self.value = lax.psum(value, "dp")
            self.steps = []
            return
        self.steps = [(None, [pair, (size - 1 - pair[0], size - 1 - pair[1])]) for pair in inward]
        self.steps.append((None, [(half - 1, half), (half, half - 1)]))
        for s, t in reversed(inward):
            self.steps.append((s, [(t, s), (size - 1 - t, size - 1 - s)]))
        self.send()

    def send(self):
        if self.steps:
            self.moved = lax.ppermute(self.value, "dp", self.steps[0][1])

    def advance(self):
        if not self.steps:
            return
        moved = self.clock(self.moved)[0]
        outer, pairs = self.steps.pop(0)
        if outer is None:
            self.value = add(self.value, moved)
        else:
            where = lax.axis_index("dp")
            far = lax.axis_size("dp") - 1 - outer
            self.value = jnp.where((where == outer) | (where == far), moved, self.value)
        self.send()


def first_sends(blocks):
    return swap(blocks[1], 1), swap(blocks[2], 2)


def last_terms(blocks, came):
    return add(blocks[3], came[1][: KB // 2]), add(blocks[4], came[0][: KB // 2])


def last_sends(terms):
    return swap(terms[0], 1), swap(terms[1], 2)


def own_sums(blocks, came, last):
    half = KB // 2
    return add(blocks[0][:half], came[0][half:], last[1]), add(blocks[0][half:], came[1][half:], last[0])


def afters(values, *earlier):
    return [after(value, *earlier) for value in values]


def per_device(
    tokens,
    projector,
    offsets,
    combiner,
    baseline,
    widener,
    thresholds,
    narrower,
    residue,
    stretch,
    lifting,
    dilation,
    elevation,
    cotangent,
):
    row = lax.axis_index("row")
    columns = lax.axis_size("col")
    features = tokens.shape[1]
    width = projector.shape[2]

    clock = Clock()

    def pick(stack, index, axis=0):
        return lax.dynamic_index_in_dim(stack, index, axis, keepdims=False)

    def padded(value):
        return jnp.pad(value.reshape(RB, SEQ, features), ((0, 0), (0, PAD - SEQ), (0, 0)))

    vectors = jnp.stack([stretch, lifting, baseline, dilation, elevation, residue, residue, residue])
    coarse = lax.optimization_barrier(vectors.astype(BF16))
    fine = (vectors - coarse.astype(F32)).astype(BF16)
    images = jnp.concatenate([padded(tokens), padded(cotangent)], axis=1)
    to = [jnp.concatenate([pick(images, row ^ k), coarse, fine]) for k in range(RB)]
    near = clock(*[swap(to[k], k) for k in range(1, RB)])
    attn_w = Gather(clock, jnp.concatenate([*projector, combiner.T], axis=1), *near)
    got = clock(col_gather([to[0], *near]))[0]
    x, cot = got[:PAD], got[PAD : 2 * PAD]
    vec = got[2 * PAD : 2 * PAD + 8].astype(F32) + got[2 * PAD + 8 :].astype(F32)
    attn_w.relay()
    attn_w.hand_over()
    wide_w = Gather(clock, widener, *attn_w.far)
    attn_w = attn_w.pieces()
    wide_w.relay()

    bias = jnp.stack([offsets[0], jnp.zeros((width,), F32), offsets[1]])[:, None]
    normed_one_t, qkv = qkv_call(x, vec, attn_w, bias)
    wide_w.hand_over(qkv)
    narrow = after(narrower.T, *wide_w.far)
    near_n = [swap(narrow, 1), swap(narrow, 2)]
    mixed, probs = attend_call(qkv)
    parts = combine_call(mixed, attn_w)
    others = [sibling(part) for part in parts]
    wide_w = wide_w.pieces()
    near_n = clock(*near_n)
    far_n = [swap(near_n[0][: KB // 2], 2), swap(near_n[1][KB // 2 :], 1)]
    others = clock(*others)
    out = forward_call(x, [*parts, *others], vec, wide_w, thresholds[None], cot)
    resid, normed_two_t, hidden, slope = out[:4]
    *far_n, slope = clock(*far_n, slope)
    blocks_n = afters(out[4:], *far_n)
    came_n = first_sends(blocks_n)
    narrow_w = [narrow, *near_n, *far_n]

    out = backward_call(cot, narrow_w, slope, hidden, normed_two_t, wide_w)
    parts, ffn_parts, thresholds_sum = out[:2], out[2:4], out[4]
    blocks_w = out[5:]
    *came_n, top = clock(*came_n, parts[0])
    parts = [top, parts[1]]
    terms = last_terms(blocks_n, came_n)
    last_n = last_sends(terms)
    came_w = list(first_sends(afters(blocks_w, *terms)))
    others = [sibling(part) for part in parts]
    grad_resid, grad_mixed, grad_t, sums_two = resid_call([*parts, *others], resid, cot, vec, attn_w)
    *last_n, grad_mixed = clock(*last_n, grad_mixed)
    halves = jnp.concatenate(own_sums(blocks_n, came_n, last_n))
    sum_n = LineSum(clock, halves)
    ffn_others = [sibling(after(part, *last_n)) for part in ffn_parts]
    grads = attend_back_call(qkv, after(grad_mixed, halves), probs)
    out = project_call(grads, normed_one_t, grad_t, mixed, attn_w)
    parts, grad_sums = out[:2], out[2]
    came_w[0], came_w[1], top, *ffn_others = clock(*came_w, parts[0], *ffn_others)
    parts = [top, parts[1]]
    terms = last_terms(blocks_w, came_w)
    last_w = list(last_sends(terms))
    blocks_p = afters(out[3:], *terms)
    came_p = list(first_sends(blocks_p))
    others = clock(*[sibling(part) for part in parts])
    deltas, sums_one = tokens_call(
        [*parts, *others], [*ffn_parts, *ffn_others], x, resid, grad_resid, cot, vec, features
    )
    featured = jnp.concatenate([sums_one[:2], sums_two[:4]]).reshape(6, RB, columns, features)
    featured = pick(featured, lax.axis_index("col"), 2)
    shared = jnp.concatenate([grad_sums[0, 0], grad_sums[2, 0], thresholds_sum[0]])
    size = 6 * features + shared.shape[0]
    lines = -(-size // (16 * features)) * 16
    mine = pick(deltas.reshape(RB, columns, 2 * PAD, features), lax.axis_index("col"), 1)
    fill = jnp.zeros((lines * features - size,), F32)
    to = []
    for j in range(RB):
        small = pick(featured, row ^ j, 1).reshape(-1)
        small = jnp.concatenate([small, shared, fill]).reshape(lines, features)
        to.append(jnp.concatenate([pick(mine, row ^ j), small.astype(BF16)]))
    last_w[0], last_w[1], to = clock(*last_w, jnp.stack(to))
    sum_w = [LineSum(clock, half) for half in own_sums(blocks_w, came_w, last_w)]
    sum_n.advance()
    came_p = clock(*came_p)
    last_p = last_sends(last_terms(blocks_p, came_p))
    sum_n.advance()
    sum_w[0].advance()
    sum_w[1].advance()
    last_p = clock(*last_p)
    halves_p = own_sums(blocks_p, came_p, last_p)
    sum_p = [LineSum(clock, half) for half in halves_p]
    got = lax.all_to_all(after(to, *halves_p), "row", 0, 0)
    sum_w[0].advance()
    sum_n.advance()
    sum_w[1].advance()
    sum_p[0].advance()
    sum_p[0].advance()
    sum_p[1].advance()
    got = clock(got)[0]
    small = got[:, 2 * PAD :].astype(F32)
    sum_s = LineSum(clock, sum([small[j] for j in range(1, RB)], small[0]))
    narrower_delta = clock(sum_n.value.astype(F32).T)[0]
    sum_w[0].advance()
    sum_w[1].advance()
    sum_p[1].advance()
    sum_s.advance()
    layer_output, tokens_delta = images_call(got, tokens, cotangent)
    sum_s.advance()
    for line_sum in (sum_n, sum_s, *sum_w, *sum_p):
        while line_sum.steps:
            line_sum.advance()
    widener_delta = jnp.concatenate([line_sum.value for line_sum in sum_w]).astype(F32)
    small = sum_s.value.reshape(-1)[:size]
    total_p = jnp.concatenate([line_sum.value for line_sum in sum_p]).astype(F32)
    projector_delta = jnp.stack([total_p[:, j * width : (j + 1) * width] for j in range(3)])
    combiner_delta = total_p[:, 3 * width :].T

    count = 6 * features
    vector = small[:count].reshape(6, features)
    offsets_delta = small[count : count + 2 * width].reshape(2, width)
    thresholds_delta = small[count + 2 * width :]
    return (
        layer_output,
        tokens_delta,
        projector_delta,
        offsets_delta,
        combiner_delta,
        vector[4],
        widener_delta,
        thresholds_delta,
        narrower_delta,
        vector[5],
        vector[0],
        vector[1],
        vector[2],
        vector[3],
    )


def solution(mesh):
    features = P(("row", "col"))
    specs = {
        "tokens": P("dp", ("row", "col")),
        "projector": P(None, "row", "col"),
        "offsets": P(None, "col"),
        "combiner": P("col", "row"),
        "baseline": features,
        "widener": P("row", "col"),
        "thresholds": P("col"),
        "narrower": P("col", "row"),
        "residue": features,
        "stretch": features,
        "lifting": features,
        "dilation": features,
        "elevation": features,
    }
    weights = tuple(specs.values())
    return jax.shard_map(
        per_device,
        mesh=mesh,
        in_specs=weights + (specs["tokens"],),
        out_specs=(specs["tokens"], specs["tokens"]) + weights[1:],
        check_vma=False,
    )
```

```python
import jax
import jax.numpy as jnp
from jax import lax
from jax.experimental import pallas as pl
from jax.experimental.pallas import tpu as pltpu
from jax.sharding import PartitionSpec as P

D = 1024
HD = 64
SEQ = 577
PAD = 592
RB = 4
KB = D // RB
PLANE = 96
SHARED = 80
TOP = 304

NORM_EPSILON = 1e-05
SIGMOID_SLOPE = 1.702
F32 = jnp.float32
BF16 = jnp.bfloat16
VMEM_LIMIT = 60 * 1024 * 1024
SHRINK = 64
DEPTH = 2

STRETCH, LIFTING, BASELINE, DILATION, ELEVATION, RESIDUE = range(6)


def mm(a, b):
    return lax.dot_general(a, b, (((1,), (0,)), ((), ())), preferred_element_type=F32)


def mm_nt(a, b):
    return lax.dot_general(a, b, (((1,), (1,)), ((), ())), preferred_element_type=F32)


def mm_tn(a, b):
    return lax.dot_general(a, b, (((0,), (0,)), ((), ())), preferred_element_type=F32)


def sds(shape, dtype=BF16):
    return jax.ShapeDtypeStruct(shape, dtype)


def whole(shape):
    return pl.BlockSpec(shape, lambda *_: (0,) * len(shape))


def call(body, grid, in_specs, out_specs, out_shape, flops, nbytes, scratch=(), transcendentals=0):
    return pl.pallas_call(
        body,
        grid=grid,
        in_specs=in_specs,
        out_specs=out_specs,
        out_shape=out_shape,
        scratch_shapes=list(scratch),
        compiler_params=pltpu.CompilerParams(
            vmem_limit_bytes=VMEM_LIMIT, dimension_semantics=("arbitrary",) * len(grid)
        ),
        cost_estimate=pl.CostEstimate(
            flops=int(flops) // SHRINK, bytes_accessed=int(nbytes) // SHRINK, transcendentals=int(transcendentals) // SHRINK
        ),
    )


PIECES = (TOP, PAD - TOP)


def piece_specs():
    return [pl.BlockSpec((rows, D), lambda *step: (0, 0)) for rows in PIECES]


def piece_shapes():
    return [sds((rows, D)) for rows in PIECES]


def store_pieces(refs, value):
    refs[0][...] = value[:TOP].astype(BF16)
    refs[1][...] = value[TOP:].astype(BF16)


def load_sum(pieces):
    top, bottom, other_top, other_bottom = [piece[...].astype(F32) for piece in pieces]
    return jnp.concatenate([top + other_top, bottom + other_bottom], axis=0)


def row_mask(shape):
    return lax.broadcasted_iota(jnp.int32, shape, 0) < SEQ


def standardize(value):
    average = jnp.mean(value, axis=1, keepdims=True)
    centred = value - average
    spread = jnp.mean(centred * centred, axis=1, keepdims=True)
    reciprocal = lax.rsqrt(spread + NORM_EPSILON)
    return centred * reciprocal, reciprocal


def norm_backward(upstream, standard, reciprocal, gain):
    scaled = upstream * gain
    mean_scaled = jnp.mean(scaled, axis=1, keepdims=True)
    mean_along = jnp.mean(scaled * standard, axis=1, keepdims=True)
    return reciprocal * (scaled - mean_scaled - standard * mean_along)


def norm_kernel(x, vec, cot, normed, normed_t, cot_t):
    standard, _r = standardize(x[...].astype(F32))
    value = standard * vec[STRETCH : STRETCH + 1] + vec[LIFTING : LIFTING + 1]
    normed[...] = value.astype(BF16)
    normed_t[...] = value.T.astype(BF16)
    cot_t[...] = cot[...].astype(F32).T.astype(BF16)


def norm_call(x, vec, cot):
    return call(
        norm_kernel,
        (1,),
        [whole((PAD, D)), whole(vec.shape), whole((PAD, D))],
        [whole((PAD, D)), whole((D, PAD)), whole((D, PAD))],
        [sds((PAD, D)), sds((D, PAD)), sds((D, PAD))],
        10 * PAD * D,
        10 * PAD * D,
    )(x, vec, cot)


BLOCK_ROWS = (KB, PLANE + SHARED, PLANE + SHARED, PLANE, SHARED, SHARED, SHARED, SHARED)


def weight_specs(tile, at):
    pieces = [pl.BlockSpec((rows, tile), lambda *step: (0, at(*step))) for rows in BLOCK_ROWS]
    return [pl.BlockSpec(memory_space=pltpu.SMEM)] + pieces


def plain_specs(tile, at):
    half = pl.BlockSpec((KB // 2, tile), lambda *step: (0, at(*step)))
    return [pl.BlockSpec((KB, tile), lambda *step: (0, at(*step)))] * 3 + [half] * 2


def weight_buffer(tile):
    return pltpu.VMEM((RB, KB, tile), BF16)


def joined(pieces, buffer):
    plane, own, near_x, near_y, far_plane, far_shared, other_x, other_y, other_far = pieces
    mine = pl.multiple_of(PLANE + SHARED * plane[0], 16)
    others = pl.multiple_of(PLANE + SHARED * (1 - plane[0]), 16)
    buffer[0] = own[...]
    for k, (near, other) in enumerate(((near_x, other_x), (near_y, other_y)), 1):
        buffer[k, :PLANE] = near[:PLANE]
        buffer[k, pl.ds(mine, SHARED)] = near[PLANE:]
        buffer[k, pl.ds(others, SHARED)] = other[...]
    buffer[3, :PLANE] = far_plane[...]
    buffer[3, pl.ds(mine, SHARED)] = far_shared[...]
    buffer[3, pl.ds(others, SHARED)] = other_far[...]
    return buffer[...].reshape(D, buffer.shape[2])


def qkv_kernel(normed, *rest):
    weights, (bias, qkv, buffer) = rest[:9], rest[9:]
    qkv[...] = (bias[0] + mm(normed[...], joined(weights, buffer))).astype(BF16)


def qkv_call(normed, blocks, bias):
    width = bias.shape[2]
    return call(
        qkv_kernel,
        (3,),
        [whole((PAD, D))]
        + weight_specs(width, lambda j: j)
        + [pl.BlockSpec((1, 1, width), lambda j: (j, 0, 0))],
        pl.BlockSpec((PAD, width), lambda j: (0, j)),
        sds((PAD, 3 * width)),
        2 * PAD * D * 3 * width,
        2 * D * 3 * width + 2 * PAD * D + 6 * PAD * width,
        [weight_buffer(width)],
    )(normed, *blocks, bias)


def head_mask(i, shape):
    lane = lax.broadcasted_iota(jnp.int32, shape, 1)
    return (lane >= i * HD) & (lane < (i + 1) * HD)


def attend_kernel(q, k, v, mixed, probs):
    queries = q[...]
    keys = k[...]
    values_t = v[...].astype(F32).T.astype(BF16)
    outs = []
    for i in range(2):
        picked = jnp.where(head_mask(i, queries.shape), queries.astype(F32) * HD ** (-0.5), 0.0)
        scores = mm_nt(keys, picked.astype(BF16))
        scores = jnp.where(row_mask(scores.shape), scores, -1e30)
        top = jnp.max(scores, axis=0, keepdims=True)
        weights = jnp.exp(scores - top)
        total = jnp.sum(weights, axis=0, keepdims=True)
        rounded = (weights * (1.0 / total)).astype(BF16)
        probs[i] = rounded
        outs.append(mm(values_t[i * HD : (i + 1) * HD], rounded))
    mixed[...] = jnp.concatenate(outs, axis=0).T.astype(BF16)


def attend_call(qkv):
    width = qkv.shape[1] // 3
    pairs = width // 128
    spec = lambda j: pl.BlockSpec((PAD, 128), lambda h, j=j: (0, j * pairs + h))
    return call(
        attend_kernel,
        (pairs,),
        [spec(0), spec(1), spec(2)],
        [pl.BlockSpec((PAD, 128), lambda h: (0, h)), pl.BlockSpec((2, PAD, PAD), lambda h: (h, 0, 0))],
        [sds((PAD, width)), sds((2 * pairs, PAD, PAD))],
        pairs * 2 * 2 * 2 * PAD * PAD * 128,
        pairs * 2 * PAD * PAD * 2,
        transcendentals=pairs * 2 * PAD * PAD,
    )(qkv, qkv, qkv)


def combine_kernel(mixed, *rest):
    top, bottom, buffer = rest[9:]
    store_pieces((top, bottom), mm_nt(mixed[...], joined(rest[:9], buffer)))


def combine_call(mixed, blocks):
    width = mixed.shape[1]
    return call(
        combine_kernel,
        (1,),
        [whole((PAD, width))] + weight_specs(width, lambda i: 3),
        piece_specs(),
        piece_shapes(),
        2 * PAD * D * width,
        2 * (PAD * D + width * D + PAD * width),
        [weight_buffer(width)],
    )(mixed, *blocks)


def split_rows(value, refs):
    own, first_x, first_y, later_x, later_y = refs
    half = KB // 2
    value = value.astype(BF16)
    own[...] = value[:KB]
    first_x[:half] = value[6 * half : 7 * half]
    first_x[half:] = value[2 * half : 3 * half]
    first_y[:half] = value[7 * half :]
    first_y[half:] = value[5 * half : 6 * half]
    later_x[...] = value[3 * half : 4 * half]
    later_y[...] = value[4 * half : 5 * half]


def delta_specs(tile, at):
    half = KB // 2
    return [pl.BlockSpec((KB, tile), at)] * 3 + [pl.BlockSpec((half, tile), at)] * 2


def delta_shapes(width):
    half = KB // 2
    return [sds((KB, width))] * 3 + [sds((half, width))] * 2


def forward_kernel(x, *rest):
    parts, vec, rest = rest[:4], rest[4], rest[5:]
    weights, (thresholds, cot_t), rest = rest[:9], rest[9:11], rest[11:]
    resid, normed_t, hidden, slope = rest[:4]
    deltas = rest[4:9]
    normed, buffer = rest[9:]

    @pl.when(pl.program_id(0) == 0)
    def _():
        total = x[...].astype(F32) + load_sum(parts) + vec[BASELINE : BASELINE + 1]
        total = jnp.where(row_mask(total.shape), total, 0.0)
        resid[...] = total
        standard, _r = standardize(total)
        value = standard * vec[DILATION : DILATION + 1] + vec[ELEVATION : ELEVATION + 1]
        normed[...] = value.astype(BF16)
        normed_t[...] = value.T.astype(BF16)

    expanded = thresholds[...] + mm(normed[...], joined(weights, buffer))
    gate = jax.nn.sigmoid(SIGMOID_SLOPE * expanded)
    active = (expanded * gate).astype(BF16)
    hidden[...] = active
    slope[...] = (gate + SIGMOID_SLOPE * expanded * gate * (1.0 - gate)).astype(BF16)
    split_rows(mm(cot_t[...], active), deltas)


def forward_call(x, parts, vec, blocks, thresholds, cot_t):
    width = thresholds.shape[1]
    tile = min(512, width)
    cols = pl.BlockSpec((PAD, tile), lambda t: (0, t))
    return call(
        forward_kernel,
        (width // tile,),
        [whole((PAD, D))]
        + piece_specs() * 2
        + [whole(vec.shape)]
        + weight_specs(tile, lambda t: t)
        + [pl.BlockSpec((1, tile), lambda t: (0, t)), whole((D, PAD))],
        [whole((PAD, D)), whole((D, PAD)), cols, cols] + delta_specs(tile, lambda t: (0, t)),
        [sds((PAD, D), F32), sds((D, PAD)), sds((PAD, width)), sds((PAD, width))] + delta_shapes(width),
        4 * PAD * D * width,
        4 * D * width + 14 * PAD * D + 4 * PAD * width,
        [pltpu.VMEM((PAD, D), BF16), weight_buffer(tile)],
        transcendentals=PAD * width,
    )(x, *parts, vec, *blocks, thresholds, cot_t)


def backward_kernel(cot, *rest):
    narrow, (slope, hidden, normed_t), wide, rest = rest[:5], rest[5:8], rest[8:17], rest[17:]
    part, out, thresholds_sum = rest[:2], rest[2:4], rest[4]
    deltas, (total, out_total, buffer) = rest[5:10], rest[10:]
    step = pl.program_id(0)
    n = jnp.concatenate([n[...] for n in narrow], axis=0)
    grad = (mm(cot[...], n) * slope[...].astype(F32)).astype(BF16)
    out_term = mm_nt(hidden[...], n)
    thresholds_sum[...] = jnp.sum(grad.astype(F32), axis=0, keepdims=True)
    split_rows(mm(normed_t[...], grad), deltas)
    term = mm_nt(grad, joined(wide, buffer))

    @pl.when(step == 0)
    def _():
        total[...] = term
        out_total[...] = out_term

    @pl.when(step > 0)
    def _():
        total[...] += term
        out_total[...] += out_term

    @pl.when(step == pl.num_programs(0) - 1)
    def _():
        store_pieces(part, total[...])
        store_pieces(out, out_total[...])


def backward_call(cot, narrow_blocks, slope, hidden, normed_t, wide_blocks):
    width = slope.shape[1]
    tile = min(512, width)
    cols = pl.BlockSpec((PAD, tile), lambda t: (0, t))
    return call(
        backward_kernel,
        (width // tile,),
        [whole((PAD, D))]
        + plain_specs(tile, lambda t: t)
        + [cols, cols, whole((D, PAD))]
        + weight_specs(tile, lambda t: t),
        piece_specs() * 2 + [pl.BlockSpec((1, tile), lambda t: (0, t))] + delta_specs(tile, lambda t: (0, t)),
        piece_shapes() * 2 + [sds((1, width), F32)] + delta_shapes(width),
        8 * PAD * D * width,
        6 * D * width + 8 * PAD * D + 4 * PAD * width,
        [pltpu.VMEM((PAD, D), F32)] * 2 + [weight_buffer(tile)],
    )(cot, *narrow_blocks, slope, hidden, normed_t, *wide_blocks)


def resid_kernel(*rest):
    parts, (resid, cot, vec), rest = rest[:4], rest[4:7], rest[7:]
    weights, (grad_resid, grad_mixed, grad_t, sums, buffer) = rest[:9], rest[9:]
    upstream = load_sum(parts)
    standard, reciprocal = standardize(resid[...])
    sums[0:1] = jnp.sum(upstream * standard, axis=0, keepdims=True)
    sums[1:2] = jnp.sum(upstream, axis=0, keepdims=True)
    grad = cot[...].astype(F32) + norm_backward(upstream, standard, reciprocal, vec[DILATION : DILATION + 1])
    sums[2:3] = jnp.sum(grad, axis=0, keepdims=True)
    sums[3:4] = jnp.sum(cot[...].astype(F32), axis=0, keepdims=True)
    sums[4:8] = jnp.zeros((4, D), F32)
    grad_resid[...] = grad
    rounded = grad.astype(BF16)
    grad_mixed[...] = mm(rounded, joined(weights, buffer)).astype(BF16)
    grad_t[...] = grad.T.astype(BF16)


def resid_call(parts, resid, cot, vec, blocks):
    width = blocks[1].shape[1] // 4
    return call(
        resid_kernel,
        (1,),
        piece_specs() * 2 + [whole((PAD, D))] * 2 + [whole(vec.shape)] + weight_specs(width, lambda i: 3),
        [whole((PAD, D)), whole((PAD, width)), whole((D, PAD)), whole((8, D))],
        [sds((PAD, D), F32), sds((PAD, width)), sds((D, PAD)), sds((8, D), F32)],
        2 * PAD * D * width,
        16 * PAD * D + 2 * width * D + 2 * PAD * width,
        [weight_buffer(width)],
    )(*parts, resid, cot, vec, *blocks)


def attend_back_kernel(q, k, v, upstream, probs, grad_q, grad_k, grad_v):
    scaled = (q[...].astype(F32) * HD ** (-0.5)).astype(BF16)
    keys_t = (k[...].astype(F32) * HD ** (-0.5)).T.astype(BF16)
    values = v[...]
    up = upstream[...]
    grads_q = []
    kept_k = None
    kept_v = None
    for i in range(2):
        mask = head_mask(i, values.shape)
        rounded = probs[i]
        weights = rounded.astype(F32)
        picked = jnp.where(mask, values.astype(F32), 0.0).astype(BF16)
        weight_grad = mm_nt(picked, up)
        along = jnp.sum(weights * weight_grad, axis=0, keepdims=True)
        score_grad = (weights * (weight_grad - along)).astype(BF16)
        value_grad = mm(rounded, up)
        key_grad = mm(score_grad, scaled)
        kept_v = value_grad if i == 0 else jnp.where(mask, value_grad, kept_v)
        kept_k = key_grad if i == 0 else jnp.where(mask, key_grad, kept_k)
        grads_q.append(mm(keys_t[i * HD : (i + 1) * HD], score_grad))
    grad_q[...] = jnp.concatenate(grads_q, axis=0).T.astype(BF16)
    grad_k[...] = kept_k.astype(BF16)
    grad_v[...] = kept_v.astype(BF16)


def attend_back_call(qkv, upstream, probs):
    width = qkv.shape[1] // 3
    pairs = width // 128
    spec = lambda j: pl.BlockSpec((PAD, 128), lambda h, j=j: (0, j * pairs + h))
    return call(
        attend_back_kernel,
        (pairs,),
        [spec(0), spec(1), spec(2), spec(0), pl.BlockSpec((2, PAD, PAD), lambda h: (h, 0, 0))],
        [spec(0)] * 3,
        [sds((PAD, width))] * 3,
        pairs * 2 * 4 * 2 * PAD * PAD * 128,
        pairs * 2 * PAD * PAD * 2,
    )(qkv, qkv, qkv, upstream, probs)


def project_kernel(gq, gk, gv, normed_t, grad_t, mixed, *rest):
    weights, part, sums, deltas, (total, buffer) = rest[:9], rest[9:11], rest[11], rest[12:17], rest[17:]
    step = pl.program_id(0)

    def one(j, g):
        grad = g[...]
        sums[0] = jnp.sum(grad.astype(F32), axis=0, keepdims=True)
        split_rows(mm(normed_t[...], grad), deltas)
        term = mm_nt(grad, joined(weights, buffer))
        if j == 0:
            total[...] = term
        else:
            total[...] += term
        if j == 2:
            store_pieces(part, total[...])

    for j, g in enumerate((gq, gk, gv)):
        pl.when(step == j)(lambda j=j, g=g: one(j, g))

    @pl.when(step == 3)
    def _():
        split_rows(mm(grad_t[...], mixed[...]), deltas)


def project_call(grads, normed_t, grad_t, mixed, blocks):
    width = grads[0].shape[1]
    at = lambda j: jnp.minimum(j, 2)
    return call(
        project_kernel,
        (4,),
        [whole((PAD, width))] * 3 + [whole((D, PAD))] * 2 + [whole((PAD, width))] + weight_specs(width, at),
        piece_specs()
        + [pl.BlockSpec((1, 1, width), lambda j: (at(j), 0, 0))]
        + delta_specs(width, lambda j: (0, j)),
        piece_shapes() + [sds((3, 1, width), F32)] + delta_shapes(4 * width),
        4 * PAD * D * 3 * width + 2 * PAD * D * width,
        4 * D * 4 * width + 6 * PAD * D + 6 * PAD * width,
        [pltpu.VMEM((PAD, D), F32), weight_buffer(width)],
    )(*grads, normed_t, grad_t, mixed, *blocks)


def share(place, refs, at, value):
    _owners, _rows, features = refs.shape
    columns = value.shape[1] // (RB * features)
    for k in range(RB):
        pieces = [value[:, i * features : (i + 1) * features] for i in range(k * columns, (k + 1) * columns)]
        piece = pieces[0]
        for c in range(1, columns):
            piece = jnp.where(place[1] == c, pieces[c], piece)
        refs[jnp.bitwise_xor(place[0], k), at : at + value.shape[0]] = piece.astype(BF16)


def tokens_kernel(*refs):
    parts, ffn_parts, (place, x, resid, grad_resid, cot, vec, sums_two, shared, to) = refs[:4], refs[4:8], refs[8:]
    upstream = load_sum(parts)
    tokens = x[...].astype(F32)
    standard, reciprocal = standardize(tokens)
    sums = [jnp.sum(upstream * standard, axis=0, keepdims=True), jnp.sum(upstream, axis=0, keepdims=True)]
    sums = jnp.concatenate(sums + [sums_two[:4], jnp.zeros((2, D), F32)], axis=0)
    lines = jnp.tile(shared[...], (1, D // shared.shape[1]))
    share(place, to, 0, load_sum(ffn_parts) + vec[RESIDUE : RESIDUE + 1] + (resid[...] - tokens))
    grad = grad_resid[...] + norm_backward(upstream, standard, reciprocal, vec[STRETCH : STRETCH + 1])
    share(place, to, PAD, grad - cot[...].astype(F32))
    share(place, to, 2 * PAD, jnp.concatenate([lines, sums], axis=0))


def tokens_call(place, parts, ffn_parts, x, resid, grad_resid, cot, vec, sums_two, shared):
    lines, features = shared.shape
    rows = 2 * PAD + lines + 8
    return call(
        tokens_kernel,
        (1,),
        piece_specs() * 4
        + [pl.BlockSpec(memory_space=pltpu.SMEM)]
        + [whole((PAD, D))] * 4
        + [whole(vec.shape), whole(sums_two.shape), whole(shared.shape)],
        whole((RB, rows, features)),
        sds((RB, rows, features)),
        24 * PAD * D,
        24 * PAD * D,
    )(*parts, *ffn_parts, place, x, resid, grad_resid, cot, vec, sums_two, shared)


def images_kernel(got, tokens, cot, layer, delta):
    for j in range(RB):
        at = slice(j * SEQ, (j + 1) * SEQ)
        layer[at] = got[j, :SEQ].astype(F32) + tokens[at].astype(F32)
        delta[at] = got[j, PAD : PAD + SEQ].astype(F32) + cot[at].astype(F32)


def images_call(got, tokens, cot):
    rows, features = tokens.shape
    return call(
        images_kernel,
        (1,),
        [whole(got.shape), whole((rows, features)), whole((rows, features))],
        [whole((rows, features))] * 2,
        [sds((rows, features), F32)] * 2,
        4 * rows * features,
        16 * rows * features,
    )(got, tokens, cot)


def swap(value, k):
    return lax.ppermute(value, "row", [(i, i ^ k) for i in range(RB)])


def after(value, *earlier):
    return lax.optimization_barrier((value,) + earlier)[0]


def sibling(part):
    size = lax.axis_size("col")
    if size == 2:
        return lax.ppermute(part, "col", [(0, 1), (1, 0)])
    total = None
    for s in range(1, size):
        term = lax.ppermute(part, "col", [(i, (i + s) % size) for i in range(size)]).astype(F32)
        total = term if total is None else total + term
    return total.astype(BF16)


def col_gather(values):
    size = lax.axis_size("col")
    lanes = values[0].shape[1]
    wide = jnp.concatenate(values, axis=1)
    if size == 2:
        other = lax.ppermute(wide, "col", [(0, 1), (1, 0)])
        first = lax.axis_index("col") == 0
        columns = [jnp.where(first, wide, other), jnp.where(first, other, wide)]
    else:
        columns = list(lax.all_gather(wide, "col"))
    parts = [column[:, k * lanes : (k + 1) * lanes] for k in range(len(values)) for column in columns]
    return jnp.concatenate(parts, axis=1)


class Gather:
    def __init__(self, clock, weight, *earlier):
        self.clock = clock
        self.plane = lax.axis_index("dp") % 2
        self.weight = weight
        shared = lax.dynamic_slice_in_dim(weight, PLANE + SHARED * self.plane, SHARED, axis=0)
        mine = after(jnp.concatenate([weight[:PLANE], shared]), *earlier)
        self.near = [swap(mine, 1), swap(mine, 2)]

    def across(self, value):
        return lax.ppermute(value, "dp", [(i, i ^ 1) for i in range(lax.axis_size("dp"))])

    def relay(self):
        near_x, near_y = self.near = self.clock(*self.near)
        self.far = [swap(near_x[:PLANE], 2), swap(near_y[PLANE:], 1)]
        self.other = [self.across(near_x[PLANE:]), self.across(near_y[PLANE:])]

    def hand_over(self, *earlier):
        *self.far, self.other[0] = self.clock(*self.far, self.other[0], *earlier)[:3]
        self.other.append(self.across(self.far[1]))

    def pieces(self):
        self.other[1:] = self.clock(*self.other[1:])
        return [self.plane.astype(jnp.int32)[None], self.weight, *self.near, *self.far, *self.other]


def add(*terms):
    total = terms[0].astype(F32)
    for term in terms[1:]:
        total = total + term.astype(F32)
    return total.astype(terms[0].dtype)


class Clock:
    def __init__(self):
        self.last = ()

    def __call__(self, *values):
        values = lax.optimization_barrier(tuple(values) + self.last)[: len(values)]
        self.last = values[:1]
        return values


class LineSum:
    def __init__(self, clock, value):
        size = lax.axis_size("dp")
        half = size // 2
        inward = [(s, s + 1) for s in range(half - 1)]
        self.clock = clock
        self.value = value
        if size % 2:
            self.value = lax.psum(value, "dp")
            self.steps = []
            return
        self.steps = [(None, [pair, (size - 1 - pair[0], size - 1 - pair[1])]) for pair in inward]
        self.steps.append((None, [(half - 1, half), (half, half - 1)]))
        for s, t in reversed(inward):
            self.steps.append((s, [(t, s), (size - 1 - t, size - 1 - s)]))
        self.send()

    def send(self):
        if self.steps:
            self.moved = lax.ppermute(self.value, "dp", self.steps[0][1])

    def advance(self):
        if not self.steps:
            return
        moved = self.clock(self.moved)[0]
        outer, pairs = self.steps.pop(0)
        if outer is None:
            self.value = add(self.value, moved)
        else:
            where = lax.axis_index("dp")
            far = lax.axis_size("dp") - 1 - outer
            self.value = jnp.where((where == outer) | (where == far), moved, self.value)
        self.send()


def first_sends(blocks):
    return swap(blocks[1], 1), swap(blocks[2], 2)


def last_terms(blocks, came):
    return add(blocks[3], came[1][: KB // 2]), add(blocks[4], came[0][: KB // 2])


def last_sends(terms):
    return swap(terms[0], 1), swap(terms[1], 2)


def own_sums(blocks, came, last):
    half = KB // 2
    return add(blocks[0][:half], came[0][half:], last[1]), add(blocks[0][half:], came[1][half:], last[0])


def afters(values, *earlier):
    return [after(value, *earlier) for value in values]


def per_device(
    tokens,
    projector,
    offsets,
    combiner,
    baseline,
    widener,
    thresholds,
    narrower,
    residue,
    stretch,
    lifting,
    dilation,
    elevation,
    cotangent,
):
    row = lax.axis_index("row")
    columns = lax.axis_size("col")
    features = tokens.shape[1]
    width = projector.shape[2]

    clock = Clock()

    def pick(stack, index, axis=0):
        return lax.dynamic_index_in_dim(stack, index, axis, keepdims=False)

    def padded(value):
        return jnp.pad(value.reshape(RB, SEQ, features), ((0, 0), (0, PAD - SEQ), (0, 0)))

    vectors = jnp.stack([stretch, lifting, baseline, dilation, elevation, residue, residue, residue])
    coarse = lax.optimization_barrier(vectors.astype(BF16))
    fine = (vectors - coarse.astype(F32)).astype(BF16)
    images = jnp.concatenate([padded(tokens), padded(cotangent)], axis=1)
    to = [jnp.concatenate([pick(images, row ^ k), coarse, fine]) for k in range(RB)]
    near = clock(*[swap(to[k], k) for k in range(1, RB)])
    attn_w = Gather(clock, jnp.concatenate([*projector, combiner.T], axis=1), *near)
    got = clock(col_gather([to[0], *near]))[0]
    x, cot = got[:PAD], got[PAD : 2 * PAD]
    vec = got[2 * PAD : 2 * PAD + 8].astype(F32) + got[2 * PAD + 8 :].astype(F32)
    x, cot, vec, narrow = clock(x, cot, vec, narrower.T)
    normed_one, normed_one_t, cot_t = clock(*norm_call(x, vec, cot))
    attn_w.relay()
    attn_w.hand_over()
    wide_w = Gather(clock, widener, *attn_w.far)
    attn_w = attn_w.pieces()
    wide_w.relay()

    bias = jnp.stack([offsets[0], jnp.zeros((width,), F32), offsets[1]])[:, None]
    qkv = qkv_call(normed_one, attn_w, bias)
    wide_w.hand_over(qkv)
    narrow = after(narrow, *wide_w.far)
    near_n = [swap(narrow, 1), swap(narrow, 2)]
    mixed, probs = attend_call(qkv)
    parts = combine_call(mixed, attn_w)
    others = [sibling(part) for part in parts]
    wide_w = wide_w.pieces()
    near_n = clock(*near_n)
    far_n = [swap(near_n[0][: KB // 2], 2), swap(near_n[1][KB // 2 :], 1)]
    others = clock(*others)
    out = forward_call(x, [*parts, *others], vec, wide_w, thresholds[None], cot_t)
    resid, normed_two_t, hidden, slope = out[:4]
    *far_n, slope = clock(*far_n, slope)
    blocks_n = afters(out[4:], *far_n)
    came_n = first_sends(blocks_n)
    narrow_w = [narrow, *near_n, *far_n]

    out = backward_call(cot, narrow_w, slope, hidden, normed_two_t, wide_w)
    parts, ffn_parts, thresholds_sum = out[:2], out[2:4], out[4]
    blocks_w = out[5:]
    *came_n, top = clock(*came_n, parts[0])
    parts = [top, parts[1]]
    terms = last_terms(blocks_n, came_n)
    last_n = last_sends(terms)
    came_w = list(first_sends(afters(blocks_w, *terms)))
    others = [sibling(part) for part in parts]
    grad_resid, grad_mixed, grad_t, sums_two = resid_call([*parts, *others], resid, cot, vec, attn_w)
    *last_n, grad_mixed = clock(*last_n, grad_mixed)
    halves = jnp.concatenate(own_sums(blocks_n, came_n, last_n))
    sum_n = LineSum(clock, halves)
    ffn_others = [sibling(after(part, *last_n)) for part in ffn_parts]
    grads = attend_back_call(qkv, after(grad_mixed, halves), probs)
    out = project_call(grads, normed_one_t, grad_t, mixed, attn_w)
    parts, grad_sums = out[:2], out[2]
    came_w[0], came_w[1], top, *ffn_others = clock(*came_w, parts[0], *ffn_others)
    parts = [top, parts[1]]
    terms = last_terms(blocks_w, came_w)
    last_w = list(last_sends(terms))
    blocks_p = afters(out[3:], *terms)
    came_p = list(first_sends(blocks_p))
    others = clock(*[sibling(part) for part in parts])
    shared = jnp.concatenate([grad_sums[0, 0], grad_sums[2, 0], thresholds_sum[0]]).reshape(-1, features)
    place = jnp.stack([row, lax.axis_index("col")]).astype(jnp.int32)
    to = tokens_call(
        place, [*parts, *others], [*ffn_parts, *ffn_others], x, resid, grad_resid, cot, vec, sums_two, shared
    )
    last_w[0], last_w[1], to = clock(*last_w, to)
    sum_w = [LineSum(clock, half) for half in own_sums(blocks_w, came_w, last_w)]
    sum_n.advance()
    came_p = clock(*came_p)
    last_p = last_sends(last_terms(blocks_p, came_p))
    sum_n.advance()
    sum_w[0].advance()
    sum_w[1].advance()
    last_p = clock(*last_p)
    halves_p = own_sums(blocks_p, came_p, last_p)
    sum_p = [LineSum(clock, halves_p[0])]
    got = lax.all_to_all(after(to, *halves_p), "row", 0, 0)
    sum_w[0].advance()
    sum_p.append(LineSum(clock, after(halves_p[1], sum_w[0].value)))
    sum_n.advance()
    sum_w[1].advance()
    sum_p[0].advance()
    sum_p[0].advance()
    sum_p[1].advance()
    got = clock(got)[0]
    small = got[:, 2 * PAD :].astype(F32)
    small = sum([small[j] for j in range(1, RB)], small[0])
    narrower_delta = clock(sum_n.value.astype(F32).T)[0]
    sum_w[0].advance()
    sum_w[1].advance()
    sum_p[1].advance()
    small = after(jnp.stack([small] * lax.axis_size("dp")), sum_p[1].value)
    small = lax.all_to_all(small, "dp", 0, 0)
    layer_output, tokens_delta = images_call(after(got, sum_p[1].value), tokens, cotangent)
    layer_output = clock(layer_output)[0]
    for line_sum in (sum_n, *sum_w, *sum_p):
        while line_sum.steps:
            line_sum.advance()
    widener_delta = jnp.concatenate([line_sum.value for line_sum in sum_w]).astype(F32)
    small = sum([small[i] for i in range(1, small.shape[0])], small[0])
    total_p = jnp.concatenate([line_sum.value for line_sum in sum_p]).astype(F32)
    projector_delta = jnp.stack([total_p[:, j * width : (j + 1) * width] for j in range(3)])
    combiner_delta = total_p[:, 3 * width :].T

    lines = shared.shape[0]
    vector = small[lines : lines + 6]
    small = small[:lines].reshape(-1)
    offsets_delta = small[: 2 * width].reshape(2, width)
    thresholds_delta = small[2 * width :]
    return (
        layer_output,
        tokens_delta,
        projector_delta,
        offsets_delta,
        combiner_delta,
        vector[4],
        widener_delta,
        thresholds_delta,
        narrower_delta,
        vector[5],
        vector[0],
        vector[1],
        vector[2],
        vector[3],
    )


def solution(mesh):
    features = P(("row", "col"))
    specs = {
        "tokens": P("dp", ("row", "col")),
        "projector": P(None, "row", "col"),
        "offsets": P(None, "col"),
        "combiner": P("col", "row"),
        "baseline": features,
        "widener": P("row", "col"),
        "thresholds": P("col"),
        "narrower": P("col", "row"),
        "residue": features,
        "stretch": features,
        "lifting": features,
        "dilation": features,
        "elevation": features,
    }
    weights = tuple(specs.values())
    return jax.shard_map(
        per_device,
        mesh=mesh,
        in_specs=weights + (specs["tokens"],),
        out_specs=(specs["tokens"], specs["tokens"]) + weights[1:],
        check_vma=False,
    )
```

```python
import jax
import jax.numpy as jnp
from jax import lax
from jax.experimental import pallas as pl
from jax.experimental.pallas import tpu as pltpu
from jax.sharding import PartitionSpec as P

D = 1024
HD = 64
SEQ = 577
PAD = 592
RB = 4
KB = D // RB
PLANE = 96
SHARED = 80
TOP = 304

NORM_EPSILON = 1e-05
SIGMOID_SLOPE = 1.702
F32 = jnp.float32
BF16 = jnp.bfloat16
VMEM_LIMIT = 60 * 1024 * 1024
SHRINK = 64
DEPTH = 2

STRETCH, LIFTING, BASELINE, DILATION, ELEVATION, RESIDUE = range(6)


def mm(a, b):
    return lax.dot_general(a, b, (((1,), (0,)), ((), ())), preferred_element_type=F32)


def mm_nt(a, b):
    return lax.dot_general(a, b, (((1,), (1,)), ((), ())), preferred_element_type=F32)


def mm_tn(a, b):
    return lax.dot_general(a, b, (((0,), (0,)), ((), ())), preferred_element_type=F32)


def sds(shape, dtype=BF16):
    return jax.ShapeDtypeStruct(shape, dtype)


def whole(shape):
    return pl.BlockSpec(shape, lambda *_: (0,) * len(shape))


def call(body, grid, in_specs, out_specs, out_shape, flops, nbytes, scratch=(), transcendentals=0):
    return pl.pallas_call(
        body,
        grid=grid,
        in_specs=in_specs,
        out_specs=out_specs,
        out_shape=out_shape,
        scratch_shapes=list(scratch),
        compiler_params=pltpu.CompilerParams(
            vmem_limit_bytes=VMEM_LIMIT, dimension_semantics=("arbitrary",) * len(grid)
        ),
        cost_estimate=pl.CostEstimate(
            flops=int(flops) // SHRINK, bytes_accessed=int(nbytes) // SHRINK, transcendentals=int(transcendentals) // SHRINK
        ),
    )


PIECES = (TOP, PAD - TOP)


def piece_specs():
    return [pl.BlockSpec((rows, D), lambda *step: (0, 0)) for rows in PIECES]


def piece_shapes():
    return [sds((rows, D)) for rows in PIECES]


def store_pieces(refs, value):
    refs[0][...] = value[:TOP].astype(BF16)
    refs[1][...] = value[TOP:].astype(BF16)


def load_sum(pieces):
    top, bottom, other_top, other_bottom = [piece[...].astype(F32) for piece in pieces]
    return jnp.concatenate([top + other_top, bottom + other_bottom], axis=0)


def row_mask(shape):
    return lax.broadcasted_iota(jnp.int32, shape, 0) < SEQ


def standardize(value):
    average = jnp.mean(value, axis=1, keepdims=True)
    centred = value - average
    spread = jnp.mean(centred * centred, axis=1, keepdims=True)
    reciprocal = lax.rsqrt(spread + NORM_EPSILON)
    return centred * reciprocal, reciprocal


def norm_backward(upstream, standard, reciprocal, gain):
    scaled = upstream * gain
    mean_scaled = jnp.mean(scaled, axis=1, keepdims=True)
    mean_along = jnp.mean(scaled * standard, axis=1, keepdims=True)
    return reciprocal * (scaled - mean_scaled - standard * mean_along)


def norm_kernel(x, vec, cot, normed, normed_t, cot_t):
    standard, _r = standardize(x[...].astype(F32))
    value = standard * vec[STRETCH : STRETCH + 1] + vec[LIFTING : LIFTING + 1]
    normed[...] = value.astype(BF16)
    normed_t[...] = value.T.astype(BF16)
    cot_t[...] = cot[...].astype(F32).T.astype(BF16)


def norm_call(x, vec, cot):
    return call(
        norm_kernel,
        (1,),
        [whole((PAD, D)), whole(vec.shape), whole((PAD, D))],
        [whole((PAD, D)), whole((D, PAD)), whole((D, PAD))],
        [sds((PAD, D)), sds((D, PAD)), sds((D, PAD))],
        10 * PAD * D,
        10 * PAD * D,
    )(x, vec, cot)


BLOCK_ROWS = (KB, PLANE + SHARED, PLANE + SHARED, PLANE, SHARED, SHARED, SHARED, SHARED)


def weight_specs(tile, at):
    pieces = [pl.BlockSpec((rows, tile), lambda *step: (0, at(*step))) for rows in BLOCK_ROWS]
    return [pl.BlockSpec(memory_space=pltpu.SMEM)] + pieces


def plain_specs(tile, at):
    half = pl.BlockSpec((KB // 2, tile), lambda *step: (0, at(*step)))
    return [pl.BlockSpec((KB, tile), lambda *step: (0, at(*step)))] * 3 + [half] * 2


def weight_buffer(tile):
    return pltpu.VMEM((RB, KB, tile), BF16)


def joined(pieces, buffer):
    plane, own, near_x, near_y, far_plane, far_shared, other_x, other_y, other_far = pieces
    mine = pl.multiple_of(PLANE + SHARED * plane[0], 16)
    others = pl.multiple_of(PLANE + SHARED * (1 - plane[0]), 16)
    buffer[0] = own[...]
    for k, (near, other) in enumerate(((near_x, other_x), (near_y, other_y)), 1):
        buffer[k, :PLANE] = near[:PLANE]
        buffer[k, pl.ds(mine, SHARED)] = near[PLANE:]
        buffer[k, pl.ds(others, SHARED)] = other[...]
    buffer[3, :PLANE] = far_plane[...]
    buffer[3, pl.ds(mine, SHARED)] = far_shared[...]
    buffer[3, pl.ds(others, SHARED)] = other_far[...]
    return buffer[...].reshape(D, buffer.shape[2])


def qkv_kernel(normed, *rest):
    weights, (bias, qkv, buffer) = rest[:9], rest[9:]
    qkv[...] = (bias[0] + mm(normed[...], joined(weights, buffer))).astype(BF16)


def qkv_call(normed, blocks, bias):
    width = bias.shape[2]
    return call(
        qkv_kernel,
        (3,),
        [whole((PAD, D))]
        + weight_specs(width, lambda j: j)
        + [pl.BlockSpec((1, 1, width), lambda j: (j, 0, 0))],
        pl.BlockSpec((PAD, width), lambda j: (0, j)),
        sds((PAD, 3 * width)),
        2 * PAD * D * 3 * width,
        2 * D * 3 * width + 2 * PAD * D + 6 * PAD * width,
        [weight_buffer(width)],
    )(normed, *blocks, bias)


def head_mask(i, shape):
    lane = lax.broadcasted_iota(jnp.int32, shape, 1)
    return (lane >= i * HD) & (lane < (i + 1) * HD)


def attend_kernel(q, k, v, mixed, probs):
    queries = q[...]
    keys = k[...]
    values_t = v[...].astype(F32).T.astype(BF16)
    outs = []
    for i in range(2):
        picked = jnp.where(head_mask(i, queries.shape), queries.astype(F32) * HD ** (-0.5), 0.0)
        scores = mm_nt(keys, picked.astype(BF16))
        scores = jnp.where(row_mask(scores.shape), scores, -1e30)
        top = jnp.max(scores, axis=0, keepdims=True)
        weights = jnp.exp(scores - top)
        total = jnp.sum(weights, axis=0, keepdims=True)
        rounded = (weights * (1.0 / total)).astype(BF16)
        probs[i] = rounded
        outs.append(mm(values_t[i * HD : (i + 1) * HD], rounded))
    mixed[...] = jnp.concatenate(outs, axis=0).T.astype(BF16)


def attend_call(qkv):
    width = qkv.shape[1] // 3
    pairs = width // 128
    spec = lambda j: pl.BlockSpec((PAD, 128), lambda h, j=j: (0, j * pairs + h))
    return call(
        attend_kernel,
        (pairs,),
        [spec(0), spec(1), spec(2)],
        [pl.BlockSpec((PAD, 128), lambda h: (0, h)), pl.BlockSpec((2, PAD, PAD), lambda h: (h, 0, 0))],
        [sds((PAD, width)), sds((2 * pairs, PAD, PAD))],
        pairs * 2 * 2 * 2 * PAD * PAD * 128,
        pairs * 2 * PAD * PAD * 2,
        transcendentals=pairs * 2 * PAD * PAD,
    )(qkv, qkv, qkv)


def combine_kernel(mixed, *rest):
    top, bottom, buffer = rest[9:]
    store_pieces((top, bottom), mm_nt(mixed[...], joined(rest[:9], buffer)))


def combine_call(mixed, blocks):
    width = mixed.shape[1]
    return call(
        combine_kernel,
        (1,),
        [whole((PAD, width))] + weight_specs(width, lambda i: 3),
        piece_specs(),
        piece_shapes(),
        2 * PAD * D * width,
        2 * (PAD * D + width * D + PAD * width),
        [weight_buffer(width)],
    )(mixed, *blocks)


def split_rows(value, refs):
    own, first_x, first_y, later_x, later_y = refs
    half = KB // 2
    value = value.astype(BF16)
    own[...] = value[:KB]
    first_x[:half] = value[6 * half : 7 * half]
    first_x[half:] = value[2 * half : 3 * half]
    first_y[:half] = value[7 * half :]
    first_y[half:] = value[5 * half : 6 * half]
    later_x[...] = value[3 * half : 4 * half]
    later_y[...] = value[4 * half : 5 * half]


def delta_specs(tile, at):
    half = KB // 2
    return [pl.BlockSpec((KB, tile), at)] * 3 + [pl.BlockSpec((half, tile), at)] * 2


def delta_shapes(width):
    half = KB // 2
    return [sds((KB, width))] * 3 + [sds((half, width))] * 2


def forward_kernel(x, *rest):
    parts, vec, rest = rest[:4], rest[4], rest[5:]
    weights, (thresholds, cot_t), rest = rest[:9], rest[9:11], rest[11:]
    resid, normed_t, hidden, slope = rest[:4]
    deltas = rest[4:9]
    normed, buffer = rest[9:]

    @pl.when(pl.program_id(0) == 0)
    def _():
        total = x[...].astype(F32) + load_sum(parts) + vec[BASELINE : BASELINE + 1]
        total = jnp.where(row_mask(total.shape), total, 0.0)
        resid[...] = total
        standard, _r = standardize(total)
        value = standard * vec[DILATION : DILATION + 1] + vec[ELEVATION : ELEVATION + 1]
        normed[...] = value.astype(BF16)
        normed_t[...] = value.T.astype(BF16)

    expanded = thresholds[...] + mm(normed[...], joined(weights, buffer))
    gate = jax.nn.sigmoid(SIGMOID_SLOPE * expanded)
    active = (expanded * gate).astype(BF16)
    hidden[...] = active
    slope[...] = (gate + SIGMOID_SLOPE * expanded * gate * (1.0 - gate)).astype(BF16)
    split_rows(mm(cot_t[...], active), deltas)


def forward_call(x, parts, vec, blocks, thresholds, cot_t):
    width = thresholds.shape[1]
    tile = min(512, width)
    cols = pl.BlockSpec((PAD, tile), lambda t: (0, t))
    return call(
        forward_kernel,
        (width // tile,),
        [whole((PAD, D))]
        + piece_specs() * 2
        + [whole(vec.shape)]
        + weight_specs(tile, lambda t: t)
        + [pl.BlockSpec((1, tile), lambda t: (0, t)), whole((D, PAD))],
        [whole((PAD, D)), whole((D, PAD)), cols, cols] + delta_specs(tile, lambda t: (0, t)),
        [sds((PAD, D), F32), sds((D, PAD)), sds((PAD, width)), sds((PAD, width))] + delta_shapes(width),
        4 * PAD * D * width,
        4 * D * width + 14 * PAD * D + 4 * PAD * width,
        [pltpu.VMEM((PAD, D), BF16), weight_buffer(tile)],
        transcendentals=PAD * width,
    )(x, *parts, vec, *blocks, thresholds, cot_t)


def backward_kernel(cot, *rest):
    narrow, (slope, hidden, normed_t), wide, rest = rest[:5], rest[5:8], rest[8:17], rest[17:]
    part, out, thresholds_sum = rest[:2], rest[2:4], rest[4]
    deltas, (total, out_total, buffer) = rest[5:10], rest[10:]
    step = pl.program_id(0)
    n = jnp.concatenate([n[...] for n in narrow], axis=0)
    grad = (mm(cot[...], n) * slope[...].astype(F32)).astype(BF16)
    out_term = mm_nt(hidden[...], n)
    thresholds_sum[...] = jnp.sum(grad.astype(F32), axis=0, keepdims=True)
    split_rows(mm(normed_t[...], grad), deltas)
    term = mm_nt(grad, joined(wide, buffer))

    @pl.when(step == 0)
    def _():
        total[...] = term
        out_total[...] = out_term

    @pl.when(step > 0)
    def _():
        total[...] += term
        out_total[...] += out_term

    @pl.when(step == pl.num_programs(0) - 1)
    def _():
        store_pieces(part, total[...])
        store_pieces(out, out_total[...])


def backward_call(cot, narrow_blocks, slope, hidden, normed_t, wide_blocks):
    width = slope.shape[1]
    tile = min(512, width)
    cols = pl.BlockSpec((PAD, tile), lambda t: (0, t))
    return call(
        backward_kernel,
        (width // tile,),
        [whole((PAD, D))]
        + plain_specs(tile, lambda t: t)
        + [cols, cols, whole((D, PAD))]
        + weight_specs(tile, lambda t: t),
        piece_specs() * 2 + [pl.BlockSpec((1, tile), lambda t: (0, t))] + delta_specs(tile, lambda t: (0, t)),
        piece_shapes() * 2 + [sds((1, width), F32)] + delta_shapes(width),
        8 * PAD * D * width,
        6 * D * width + 8 * PAD * D + 4 * PAD * width,
        [pltpu.VMEM((PAD, D), F32)] * 2 + [weight_buffer(tile)],
    )(cot, *narrow_blocks, slope, hidden, normed_t, *wide_blocks)


def resid_kernel(*rest):
    parts, (resid, cot, vec), rest = rest[:4], rest[4:7], rest[7:]
    weights, (grad_resid, grad_mixed, grad_t, sums, buffer) = rest[:9], rest[9:]
    upstream = load_sum(parts)
    standard, reciprocal = standardize(resid[...])
    sums[0:1] = jnp.sum(upstream * standard, axis=0, keepdims=True)
    sums[1:2] = jnp.sum(upstream, axis=0, keepdims=True)
    grad = cot[...].astype(F32) + norm_backward(upstream, standard, reciprocal, vec[DILATION : DILATION + 1])
    sums[2:3] = jnp.sum(grad, axis=0, keepdims=True)
    sums[3:4] = jnp.sum(cot[...].astype(F32), axis=0, keepdims=True)
    sums[4:8] = jnp.zeros((4, D), F32)
    grad_resid[...] = grad
    rounded = grad.astype(BF16)
    grad_mixed[...] = mm(rounded, joined(weights, buffer)).astype(BF16)
    grad_t[...] = grad.T.astype(BF16)


def resid_call(parts, resid, cot, vec, blocks):
    width = blocks[1].shape[1] // 4
    return call(
        resid_kernel,
        (1,),
        piece_specs() * 2 + [whole((PAD, D))] * 2 + [whole(vec.shape)] + weight_specs(width, lambda i: 3),
        [whole((PAD, D)), whole((PAD, width)), whole((D, PAD)), whole((8, D))],
        [sds((PAD, D), F32), sds((PAD, width)), sds((D, PAD)), sds((8, D), F32)],
        2 * PAD * D * width,
        16 * PAD * D + 2 * width * D + 2 * PAD * width,
        [weight_buffer(width)],
    )(*parts, resid, cot, vec, *blocks)


def attend_back_kernel(q, k, v, upstream, probs, grad_q, grad_k, grad_v):
    scaled = (q[...].astype(F32) * HD ** (-0.5)).astype(BF16)
    keys_t = (k[...].astype(F32) * HD ** (-0.5)).T.astype(BF16)
    values = v[...]
    up = upstream[...]
    grads_q = []
    kept_k = None
    kept_v = None
    for i in range(2):
        mask = head_mask(i, values.shape)
        rounded = probs[i]
        weights = rounded.astype(F32)
        picked = jnp.where(mask, values.astype(F32), 0.0).astype(BF16)
        weight_grad = mm_nt(picked, up)
        along = jnp.sum(weights * weight_grad, axis=0, keepdims=True)
        score_grad = (weights * (weight_grad - along)).astype(BF16)
        value_grad = mm(rounded, up)
        key_grad = mm(score_grad, scaled)
        kept_v = value_grad if i == 0 else jnp.where(mask, value_grad, kept_v)
        kept_k = key_grad if i == 0 else jnp.where(mask, key_grad, kept_k)
        grads_q.append(mm(keys_t[i * HD : (i + 1) * HD], score_grad))
    grad_q[...] = jnp.concatenate(grads_q, axis=0).T.astype(BF16)
    grad_k[...] = kept_k.astype(BF16)
    grad_v[...] = kept_v.astype(BF16)


def attend_back_call(qkv, upstream, probs):
    width = qkv.shape[1] // 3
    pairs = width // 128
    spec = lambda j: pl.BlockSpec((PAD, 128), lambda h, j=j: (0, j * pairs + h))
    return call(
        attend_back_kernel,
        (pairs,),
        [spec(0), spec(1), spec(2), spec(0), pl.BlockSpec((2, PAD, PAD), lambda h: (h, 0, 0))],
        [spec(0)] * 3,
        [sds((PAD, width))] * 3,
        pairs * 2 * 4 * 2 * PAD * PAD * 128,
        pairs * 2 * PAD * PAD * 2,
    )(qkv, qkv, qkv, upstream, probs)


def project_kernel(gq, gk, gv, normed_t, grad_t, mixed, *rest):
    weights, part, sums, deltas, (total, buffer) = rest[:9], rest[9:11], rest[11], rest[12:17], rest[17:]
    step = pl.program_id(0)

    def one(j, g):
        grad = g[...]
        sums[0] = jnp.sum(grad.astype(F32), axis=0, keepdims=True)
        split_rows(mm(normed_t[...], grad), deltas)
        term = mm_nt(grad, joined(weights, buffer))
        if j == 0:
            total[...] = term
        else:
            total[...] += term
        if j == 2:
            store_pieces(part, total[...])

    for j, g in enumerate((gq, gk, gv)):
        pl.when(step == j)(lambda j=j, g=g: one(j, g))

    @pl.when(step == 3)
    def _():
        split_rows(mm(grad_t[...], mixed[...]), deltas)


def project_call(grads, normed_t, grad_t, mixed, blocks):
    width = grads[0].shape[1]
    at = lambda j: jnp.minimum(j, 2)
    return call(
        project_kernel,
        (4,),
        [whole((PAD, width))] * 3 + [whole((D, PAD))] * 2 + [whole((PAD, width))] + weight_specs(width, at),
        piece_specs()
        + [pl.BlockSpec((1, 1, width), lambda j: (at(j), 0, 0))]
        + delta_specs(width, lambda j: (0, j)),
        piece_shapes() + [sds((3, 1, width), F32)] + delta_shapes(4 * width),
        4 * PAD * D * 3 * width + 2 * PAD * D * width,
        4 * D * 4 * width + 6 * PAD * D + 6 * PAD * width,
        [pltpu.VMEM((PAD, D), F32), weight_buffer(width)],
    )(*grads, normed_t, grad_t, mixed, *blocks)


def share(refs, at, value):
    owners, _rows, features = refs.shape
    for i in range(owners):
        refs[i, at : at + PAD] = value[:, i * features : (i + 1) * features].astype(BF16)


def tokens_kernel(*refs):
    parts, ffn_parts, (x, resid, grad_resid, cot, vec, deltas, sums) = refs[:4], refs[4:8], refs[8:]
    upstream = load_sum(parts)
    tokens = x[...].astype(F32)
    standard, reciprocal = standardize(tokens)
    sums[0:1] = jnp.sum(upstream * standard, axis=0, keepdims=True)
    sums[1:2] = jnp.sum(upstream, axis=0, keepdims=True)
    sums[2:8] = jnp.zeros((6, D), F32)
    share(deltas, 0, load_sum(ffn_parts) + vec[RESIDUE : RESIDUE + 1] + (resid[...] - tokens))
    grad = grad_resid[...] + norm_backward(upstream, standard, reciprocal, vec[STRETCH : STRETCH + 1])
    share(deltas, PAD, grad - cot[...].astype(F32))


def tokens_call(parts, ffn_parts, x, resid, grad_resid, cot, vec, features):
    return call(
        tokens_kernel,
        (1,),
        piece_specs() * 4 + [whole((PAD, D))] * 4 + [whole(vec.shape)],
        [whole((D // features, 2 * PAD, features)), whole((8, D))],
        [sds((D // features, 2 * PAD, features)), sds((8, D), F32)],
        24 * PAD * D,
        24 * PAD * D,
    )(*parts, *ffn_parts, x, resid, grad_resid, cot, vec)


def images_kernel(got, tokens, cot, layer, delta):
    for j in range(RB):
        at = slice(j * SEQ, (j + 1) * SEQ)
        layer[at] = got[j, :SEQ].astype(F32) + tokens[at].astype(F32)
        delta[at] = got[j, PAD : PAD + SEQ].astype(F32) + cot[at].astype(F32)


def images_call(got, tokens, cot):
    rows, features = tokens.shape
    return call(
        images_kernel,
        (1,),
        [whole(got.shape), whole((rows, features)), whole((rows, features))],
        [whole((rows, features))] * 2,
        [sds((rows, features), F32)] * 2,
        4 * rows * features,
        16 * rows * features,
    )(got, tokens, cot)


def swap(value, k):
    return lax.ppermute(value, "row", [(i, i ^ k) for i in range(RB)])


def after(value, *earlier):
    return lax.optimization_barrier((value,) + earlier)[0]


def sibling(part):
    size = lax.axis_size("col")
    if size == 2:
        return lax.ppermute(part, "col", [(0, 1), (1, 0)])
    total = None
    for s in range(1, size):
        term = lax.ppermute(part, "col", [(i, (i + s) % size) for i in range(size)]).astype(F32)
        total = term if total is None else total + term
    return total.astype(BF16)


def col_gather(values):
    size = lax.axis_size("col")
    lanes = values[0].shape[1]
    wide = jnp.concatenate(values, axis=1)
    if size == 2:
        other = lax.ppermute(wide, "col", [(0, 1), (1, 0)])
        first = lax.axis_index("col") == 0
        columns = [jnp.where(first, wide, other), jnp.where(first, other, wide)]
    else:
        columns = list(lax.all_gather(wide, "col"))
    parts = [column[:, k * lanes : (k + 1) * lanes] for k in range(len(values)) for column in columns]
    return jnp.concatenate(parts, axis=1)


class Gather:
    def __init__(self, clock, weight, *earlier):
        self.clock = clock
        self.plane = lax.axis_index("dp") % 2
        self.weight = weight
        shared = lax.dynamic_slice_in_dim(weight, PLANE + SHARED * self.plane, SHARED, axis=0)
        mine = after(jnp.concatenate([weight[:PLANE], shared]), *earlier)
        self.near = [swap(mine, 1), swap(mine, 2)]

    def across(self, value):
        return lax.ppermute(value, "dp", [(i, i ^ 1) for i in range(lax.axis_size("dp"))])

    def relay(self):
        near_x, near_y = self.near = self.clock(*self.near)
        self.far = [swap(near_x[:PLANE], 2), swap(near_y[PLANE:], 1)]
        self.other = [self.across(near_x[PLANE:]), self.across(near_y[PLANE:])]

    def hand_over(self, *earlier):
        *self.far, self.other[0] = self.clock(*self.far, self.other[0], *earlier)[:3]
        self.other.append(self.across(self.far[1]))

    def pieces(self):
        self.other[1:] = self.clock(*self.other[1:])
        return [self.plane.astype(jnp.int32)[None], self.weight, *self.near, *self.far, *self.other]


def add(*terms):
    total = terms[0].astype(F32)
    for term in terms[1:]:
        total = total + term.astype(F32)
    return total.astype(terms[0].dtype)


class Clock:
    def __init__(self):
        self.last = ()

    def __call__(self, *values):
        values = lax.optimization_barrier(tuple(values) + self.last)[: len(values)]
        self.last = values[:1]
        return values


class LineSum:
    def __init__(self, clock, value):
        size = lax.axis_size("dp")
        half = size // 2
        inward = [(s, s + 1) for s in range(half - 1)]
        self.clock = clock
        self.value = value
        if size % 2:
            self.value = lax.psum(value, "dp")
            self.steps = []
            return
        self.steps = [(None, [pair, (size - 1 - pair[0], size - 1 - pair[1])]) for pair in inward]
        self.steps.append((None, [(half - 1, half), (half, half - 1)]))
        for s, t in reversed(inward):
            self.steps.append((s, [(t, s), (size - 1 - t, size - 1 - s)]))
        self.send()

    def send(self):
        if self.steps:
            self.moved = lax.ppermute(self.value, "dp", self.steps[0][1])

    def advance(self):
        if not self.steps:
            return
        moved = self.clock(self.moved)[0]
        outer, pairs = self.steps.pop(0)
        if outer is None:
            self.value = add(self.value, moved)
        else:
            where = lax.axis_index("dp")
            far = lax.axis_size("dp") - 1 - outer
            self.value = jnp.where((where == outer) | (where == far), moved, self.value)
        self.send()


def first_sends(blocks):
    return swap(blocks[1], 1), swap(blocks[2], 2)


def last_terms(blocks, came):
    return add(blocks[3], came[1][: KB // 2]), add(blocks[4], came[0][: KB // 2])


def last_sends(terms):
    return swap(terms[0], 1), swap(terms[1], 2)


def own_sums(blocks, came, last):
    half = KB // 2
    return add(blocks[0][:half], came[0][half:], last[1]), add(blocks[0][half:], came[1][half:], last[0])


def afters(values, *earlier):
    return [after(value, *earlier) for value in values]


def per_device(
    tokens,
    projector,
    offsets,
    combiner,
    baseline,
    widener,
    thresholds,
    narrower,
    residue,
    stretch,
    lifting,
    dilation,
    elevation,
    cotangent,
):
    row = lax.axis_index("row")
    columns = lax.axis_size("col")
    features = tokens.shape[1]
    width = projector.shape[2]

    clock = Clock()

    def pick(stack, index, axis=0):
        return lax.dynamic_index_in_dim(stack, index, axis, keepdims=False)

    def padded(value):
        return jnp.pad(value.reshape(RB, SEQ, features), ((0, 0), (0, PAD - SEQ), (0, 0)))

    vectors = jnp.stack([stretch, lifting, baseline, dilation, elevation, residue, residue, residue])
    coarse = lax.optimization_barrier(vectors.astype(BF16))
    fine = (vectors - coarse.astype(F32)).astype(BF16)
    images = jnp.concatenate([padded(tokens), padded(cotangent)], axis=1)
    to = [jnp.concatenate([pick(images, row ^ k), coarse, fine]) for k in range(RB)]
    near = clock(*[swap(to[k], k) for k in range(1, RB)])
    attn_w = Gather(clock, jnp.concatenate([*projector, combiner.T], axis=1), *near)
    got = clock(col_gather([to[0], *near]))[0]
    x, cot = got[:PAD], got[PAD : 2 * PAD]
    vec = got[2 * PAD : 2 * PAD + 8].astype(F32) + got[2 * PAD + 8 :].astype(F32)
    x, cot, vec = clock(x, cot, vec)
    normed_one, normed_one_t, cot_t = clock(*norm_call(x, vec, cot))
    attn_w.relay()
    attn_w.hand_over()
    wide_w = Gather(clock, widener, *attn_w.far)
    attn_w = attn_w.pieces()
    wide_w.relay()

    bias = jnp.stack([offsets[0], jnp.zeros((width,), F32), offsets[1]])[:, None]
    qkv = qkv_call(normed_one, attn_w, bias)
    wide_w.hand_over(qkv)
    narrow = after(narrower.T, *wide_w.far)
    near_n = [swap(narrow, 1), swap(narrow, 2)]
    mixed, probs = attend_call(qkv)
    parts = combine_call(mixed, attn_w)
    others = [sibling(part) for part in parts]
    wide_w = wide_w.pieces()
    near_n = clock(*near_n)
    far_n = [swap(near_n[0][: KB // 2], 2), swap(near_n[1][KB // 2 :], 1)]
    others = clock(*others)
    out = forward_call(x, [*parts, *others], vec, wide_w, thresholds[None], cot_t)
    resid, normed_two_t, hidden, slope = out[:4]
    *far_n, slope = clock(*far_n, slope)
    blocks_n = afters(out[4:], *far_n)
    came_n = first_sends(blocks_n)
    narrow_w = [narrow, *near_n, *far_n]

    out = backward_call(cot, narrow_w, slope, hidden, normed_two_t, wide_w)
    parts, ffn_parts, thresholds_sum = out[:2], out[2:4], out[4]
    blocks_w = out[5:]
    *came_n, top = clock(*came_n, parts[0])
    parts = [top, parts[1]]
    terms = last_terms(blocks_n, came_n)
    last_n = last_sends(terms)
    came_w = list(first_sends(afters(blocks_w, *terms)))
    others = [sibling(part) for part in parts]
    grad_resid, grad_mixed, grad_t, sums_two = resid_call([*parts, *others], resid, cot, vec, attn_w)
    *last_n, grad_mixed = clock(*last_n, grad_mixed)
    halves = jnp.concatenate(own_sums(blocks_n, came_n, last_n))
    sum_n = LineSum(clock, halves)
    ffn_others = [sibling(after(part, *last_n)) for part in ffn_parts]
    grads = attend_back_call(qkv, after(grad_mixed, halves), probs)
    out = project_call(grads, normed_one_t, grad_t, mixed, attn_w)
    parts, grad_sums = out[:2], out[2]
    came_w[0], came_w[1], top, *ffn_others = clock(*came_w, parts[0], *ffn_others)
    parts = [top, parts[1]]
    terms = last_terms(blocks_w, came_w)
    last_w = list(last_sends(terms))
    blocks_p = afters(out[3:], *terms)
    came_p = list(first_sends(blocks_p))
    others = clock(*[sibling(part) for part in parts])
    deltas, sums_one = tokens_call(
        [*parts, *others], [*ffn_parts, *ffn_others], x, resid, grad_resid, cot, vec, features
    )
    featured = jnp.concatenate([sums_one[:2], sums_two[:4]]).reshape(6, RB, columns, features)
    featured = pick(featured, lax.axis_index("col"), 2)
    shared = jnp.concatenate([grad_sums[0, 0], grad_sums[2, 0], thresholds_sum[0]])
    size = 6 * features + shared.shape[0]
    lines = -(-size // (16 * features)) * 16
    mine = pick(deltas.reshape(RB, columns, 2 * PAD, features), lax.axis_index("col"), 1)
    fill = jnp.zeros((lines * features - size,), F32)
    to = []
    for j in range(RB):
        small = pick(featured, row ^ j, 1).reshape(-1)
        small = jnp.concatenate([small, shared, fill]).reshape(lines, features)
        to.append(jnp.concatenate([pick(mine, row ^ j), small.astype(BF16)]))
    last_w[0], last_w[1], to = clock(*last_w, jnp.stack(to))
    sum_w = [LineSum(clock, half) for half in own_sums(blocks_w, came_w, last_w)]
    sum_n.advance()
    came_p = clock(*came_p)
    last_p = last_sends(last_terms(blocks_p, came_p))
    sum_n.advance()
    sum_w[0].advance()
    sum_w[1].advance()
    last_p = clock(*last_p)
    halves_p = own_sums(blocks_p, came_p, last_p)
    sum_p = [LineSum(clock, half) for half in halves_p]
    got = lax.all_to_all(after(to, *halves_p), "row", 0, 0)
    sum_w[0].advance()
    sum_n.advance()
    sum_w[1].advance()
    sum_p[0].advance()
    sum_p[0].advance()
    sum_p[1].advance()
    got = clock(got)[0]
    small = got[:, 2 * PAD :].astype(F32)
    sum_s = LineSum(clock, sum([small[j] for j in range(1, RB)], small[0]))
    narrower_delta = clock(sum_n.value.astype(F32).T)[0]
    sum_w[0].advance()
    sum_w[1].advance()
    sum_p[1].advance()
    sum_s.advance()
    layer_output, tokens_delta = images_call(got, tokens, cotangent)
    sum_s.advance()
    for line_sum in (sum_n, sum_s, *sum_w, *sum_p):
        while line_sum.steps:
            line_sum.advance()
    widener_delta = jnp.concatenate([line_sum.value for line_sum in sum_w]).astype(F32)
    small = sum_s.value.reshape(-1)[:size]
    total_p = jnp.concatenate([line_sum.value for line_sum in sum_p]).astype(F32)
    projector_delta = jnp.stack([total_p[:, j * width : (j + 1) * width] for j in range(3)])
    combiner_delta = total_p[:, 3 * width :].T

    count = 6 * features
    vector = small[:count].reshape(6, features)
    offsets_delta = small[count : count + 2 * width].reshape(2, width)
    thresholds_delta = small[count + 2 * width :]
    return (
        layer_output,
        tokens_delta,
        projector_delta,
        offsets_delta,
        combiner_delta,
        vector[4],
        widener_delta,
        thresholds_delta,
        narrower_delta,
        vector[5],
        vector[0],
        vector[1],
        vector[2],
        vector[3],
    )


def solution(mesh):
    features = P(("row", "col"))
    specs = {
        "tokens": P("dp", ("row", "col")),
        "projector": P(None, "row", "col"),
        "offsets": P(None, "col"),
        "combiner": P("col", "row"),
        "baseline": features,
        "widener": P("row", "col"),
        "thresholds": P("col"),
        "narrower": P("col", "row"),
        "residue": features,
        "stretch": features,
        "lifting": features,
        "dilation": features,
        "elevation": features,
    }
    weights = tuple(specs.values())
    return jax.shard_map(
        per_device,
        mesh=mesh,
        in_specs=weights + (specs["tokens"],),
        out_specs=(specs["tokens"], specs["tokens"]) + weights[1:],
        check_vma=False,
    )
```

```python
import jax
import jax.numpy as jnp
from jax import lax
from jax.experimental import pallas as pl
from jax.experimental.pallas import tpu as pltpu
from jax.sharding import PartitionSpec as P

D = 1024
HD = 64
SEQ = 577
PAD = 592
RB = 4
KB = D // RB
PLANE = 96
SHARED = 80
TOP = 304

NORM_EPSILON = 1e-05
SIGMOID_SLOPE = 1.702
F32 = jnp.float32
BF16 = jnp.bfloat16
VMEM_LIMIT = 60 * 1024 * 1024
SHRINK = 64
DEPTH = 2

STRETCH, LIFTING, BASELINE, DILATION, ELEVATION, RESIDUE = range(6)


def mm(a, b):
    return lax.dot_general(a, b, (((1,), (0,)), ((), ())), preferred_element_type=F32)


def mm_nt(a, b):
    return lax.dot_general(a, b, (((1,), (1,)), ((), ())), preferred_element_type=F32)


def mm_tn(a, b):
    return lax.dot_general(a, b, (((0,), (0,)), ((), ())), preferred_element_type=F32)


def sds(shape, dtype=BF16):
    return jax.ShapeDtypeStruct(shape, dtype)


def whole(shape):
    return pl.BlockSpec(shape, lambda *_: (0,) * len(shape))


def call(body, grid, in_specs, out_specs, out_shape, flops, nbytes, scratch=(), transcendentals=0):
    return pl.pallas_call(
        body,
        grid=grid,
        in_specs=in_specs,
        out_specs=out_specs,
        out_shape=out_shape,
        scratch_shapes=list(scratch),
        compiler_params=pltpu.CompilerParams(
            vmem_limit_bytes=VMEM_LIMIT, dimension_semantics=("arbitrary",) * len(grid)
        ),
        cost_estimate=pl.CostEstimate(
            flops=int(flops) // SHRINK, bytes_accessed=int(nbytes) // SHRINK, transcendentals=int(transcendentals) // SHRINK
        ),
    )


PIECES = (TOP, PAD - TOP)


def piece_specs():
    return [pl.BlockSpec((rows, D), lambda *step: (0, 0)) for rows in PIECES]


def piece_shapes():
    return [sds((rows, D)) for rows in PIECES]


def store_pieces(refs, value):
    refs[0][...] = value[:TOP].astype(BF16)
    refs[1][...] = value[TOP:].astype(BF16)


def load_sum(pieces):
    top, bottom, other_top, other_bottom = [piece[...].astype(F32) for piece in pieces]
    return jnp.concatenate([top + other_top, bottom + other_bottom], axis=0)


def row_mask(shape):
    return lax.broadcasted_iota(jnp.int32, shape, 0) < SEQ


def standardize(value):
    average = jnp.mean(value, axis=1, keepdims=True)
    centred = value - average
    spread = jnp.mean(centred * centred, axis=1, keepdims=True)
    reciprocal = lax.rsqrt(spread + NORM_EPSILON)
    return centred * reciprocal, reciprocal


def norm_backward(upstream, standard, reciprocal, gain):
    scaled = upstream * gain
    mean_scaled = jnp.mean(scaled, axis=1, keepdims=True)
    mean_along = jnp.mean(scaled * standard, axis=1, keepdims=True)
    return reciprocal * (scaled - mean_scaled - standard * mean_along)


def norm_kernel(x, vec, cot, normed, normed_t, cot_t):
    standard, _r = standardize(x[...].astype(F32))
    value = standard * vec[STRETCH : STRETCH + 1] + vec[LIFTING : LIFTING + 1]
    normed[...] = value.astype(BF16)
    normed_t[...] = value.T.astype(BF16)
    cot_t[...] = cot[...].astype(F32).T.astype(BF16)


def norm_call(x, vec, cot):
    return call(
        norm_kernel,
        (1,),
        [whole((PAD, D)), whole(vec.shape), whole((PAD, D))],
        [whole((PAD, D)), whole((D, PAD)), whole((D, PAD))],
        [sds((PAD, D)), sds((D, PAD)), sds((D, PAD))],
        10 * PAD * D,
        10 * PAD * D,
    )(x, vec, cot)


BLOCK_ROWS = (KB, PLANE + SHARED, PLANE + SHARED, PLANE, SHARED, SHARED, SHARED, SHARED)


def weight_specs(tile, at):
    pieces = [pl.BlockSpec((rows, tile), lambda *step: (0, at(*step))) for rows in BLOCK_ROWS]
    return [pl.BlockSpec(memory_space=pltpu.SMEM)] + pieces


def plain_specs(tile, at):
    half = pl.BlockSpec((KB // 2, tile), lambda *step: (0, at(*step)))
    return [pl.BlockSpec((KB, tile), lambda *step: (0, at(*step)))] * 3 + [half] * 2


def weight_buffer(tile):
    return pltpu.VMEM((RB, KB, tile), BF16)


def joined(pieces, buffer):
    plane, own, near_x, near_y, far_plane, far_shared, other_x, other_y, other_far = pieces
    mine = pl.multiple_of(PLANE + SHARED * plane[0], 16)
    others = pl.multiple_of(PLANE + SHARED * (1 - plane[0]), 16)
    buffer[0] = own[...]
    for k, (near, other) in enumerate(((near_x, other_x), (near_y, other_y)), 1):
        buffer[k, :PLANE] = near[:PLANE]
        buffer[k, pl.ds(mine, SHARED)] = near[PLANE:]
        buffer[k, pl.ds(others, SHARED)] = other[...]
    buffer[3, :PLANE] = far_plane[...]
    buffer[3, pl.ds(mine, SHARED)] = far_shared[...]
    buffer[3, pl.ds(others, SHARED)] = other_far[...]
    return buffer[...].reshape(D, buffer.shape[2])


def qkv_kernel(normed, *rest):
    weights, (bias, qkv, buffer) = rest[:9], rest[9:]
    qkv[...] = (bias[0] + mm(normed[...], joined(weights, buffer))).astype(BF16)


def qkv_call(normed, blocks, bias):
    width = bias.shape[2]
    return call(
        qkv_kernel,
        (3,),
        [whole((PAD, D))]
        + weight_specs(width, lambda j: j)
        + [pl.BlockSpec((1, 1, width), lambda j: (j, 0, 0))],
        pl.BlockSpec((PAD, width), lambda j: (0, j)),
        sds((PAD, 3 * width)),
        2 * PAD * D * 3 * width,
        2 * D * 3 * width + 2 * PAD * D + 6 * PAD * width,
        [weight_buffer(width)],
    )(normed, *blocks, bias)


def head_mask(i, shape):
    lane = lax.broadcasted_iota(jnp.int32, shape, 1)
    return (lane >= i * HD) & (lane < (i + 1) * HD)


def attend_kernel(q, k, v, mixed, probs):
    queries = q[...]
    keys = k[...]
    values_t = v[...].astype(F32).T.astype(BF16)
    outs = []
    for i in range(2):
        picked = jnp.where(head_mask(i, queries.shape), queries.astype(F32) * HD ** (-0.5), 0.0)
        scores = mm_nt(keys, picked.astype(BF16))
        scores = jnp.where(row_mask(scores.shape), scores, -1e30)
        top = jnp.max(scores, axis=0, keepdims=True)
        weights = jnp.exp(scores - top)
        total = jnp.sum(weights, axis=0, keepdims=True)
        rounded = (weights * (1.0 / total)).astype(BF16)
        probs[i] = rounded
        outs.append(mm(values_t[i * HD : (i + 1) * HD], rounded))
    mixed[...] = jnp.concatenate(outs, axis=0).T.astype(BF16)


def attend_call(qkv):
    width = qkv.shape[1] // 3
    pairs = width // 128
    spec = lambda j: pl.BlockSpec((PAD, 128), lambda h, j=j: (0, j * pairs + h))
    return call(
        attend_kernel,
        (pairs,),
        [spec(0), spec(1), spec(2)],
        [pl.BlockSpec((PAD, 128), lambda h: (0, h)), pl.BlockSpec((2, PAD, PAD), lambda h: (h, 0, 0))],
        [sds((PAD, width)), sds((2 * pairs, PAD, PAD))],
        pairs * 2 * 2 * 2 * PAD * PAD * 128,
        pairs * 2 * PAD * PAD * 2,
        transcendentals=pairs * 2 * PAD * PAD,
    )(qkv, qkv, qkv)


def combine_kernel(mixed, *rest):
    top, bottom, buffer = rest[9:]
    store_pieces((top, bottom), mm_nt(mixed[...], joined(rest[:9], buffer)))


def combine_call(mixed, blocks):
    width = mixed.shape[1]
    return call(
        combine_kernel,
        (1,),
        [whole((PAD, width))] + weight_specs(width, lambda i: 3),
        piece_specs(),
        piece_shapes(),
        2 * PAD * D * width,
        2 * (PAD * D + width * D + PAD * width),
        [weight_buffer(width)],
    )(mixed, *blocks)


def split_rows(value, refs):
    own, first_x, first_y, later_x, later_y = refs
    half = KB // 2
    value = value.astype(BF16)
    own[...] = value[:KB]
    first_x[:half] = value[6 * half : 7 * half]
    first_x[half:] = value[2 * half : 3 * half]
    first_y[:half] = value[7 * half :]
    first_y[half:] = value[5 * half : 6 * half]
    later_x[...] = value[3 * half : 4 * half]
    later_y[...] = value[4 * half : 5 * half]


def delta_specs(tile, at):
    half = KB // 2
    return [pl.BlockSpec((KB, tile), at)] * 3 + [pl.BlockSpec((half, tile), at)] * 2


def delta_shapes(width):
    half = KB // 2
    return [sds((KB, width))] * 3 + [sds((half, width))] * 2


def forward_kernel(x, *rest):
    parts, vec, rest = rest[:4], rest[4], rest[5:]
    weights, (thresholds, cot_t), rest = rest[:9], rest[9:11], rest[11:]
    resid, normed_t, hidden, slope = rest[:4]
    deltas = rest[4:9]
    normed, buffer = rest[9:]

    @pl.when(pl.program_id(0) == 0)
    def _():
        total = x[...].astype(F32) + load_sum(parts) + vec[BASELINE : BASELINE + 1]
        total = jnp.where(row_mask(total.shape), total, 0.0)
        resid[...] = total
        standard, _r = standardize(total)
        value = standard * vec[DILATION : DILATION + 1] + vec[ELEVATION : ELEVATION + 1]
        normed[...] = value.astype(BF16)
        normed_t[...] = value.T.astype(BF16)

    expanded = thresholds[...] + mm(normed[...], joined(weights, buffer))
    gate = jax.nn.sigmoid(SIGMOID_SLOPE * expanded)
    active = (expanded * gate).astype(BF16)
    hidden[...] = active
    slope[...] = (gate + SIGMOID_SLOPE * expanded * gate * (1.0 - gate)).astype(BF16)
    split_rows(mm(cot_t[...], active), deltas)


def forward_call(x, parts, vec, blocks, thresholds, cot_t):
    width = thresholds.shape[1]
    tile = min(512, width)
    cols = pl.BlockSpec((PAD, tile), lambda t: (0, t))
    return call(
        forward_kernel,
        (width // tile,),
        [whole((PAD, D))]
        + piece_specs() * 2
        + [whole(vec.shape)]
        + weight_specs(tile, lambda t: t)
        + [pl.BlockSpec((1, tile), lambda t: (0, t)), whole((D, PAD))],
        [whole((PAD, D)), whole((D, PAD)), cols, cols] + delta_specs(tile, lambda t: (0, t)),
        [sds((PAD, D), F32), sds((D, PAD)), sds((PAD, width)), sds((PAD, width))] + delta_shapes(width),
        4 * PAD * D * width,
        4 * D * width + 14 * PAD * D + 4 * PAD * width,
        [pltpu.VMEM((PAD, D), BF16), weight_buffer(tile)],
        transcendentals=PAD * width,
    )(x, *parts, vec, *blocks, thresholds, cot_t)


def backward_kernel(cot, *rest):
    narrow, (slope, hidden, normed_t), wide, rest = rest[:5], rest[5:8], rest[8:17], rest[17:]
    part, out, thresholds_sum = rest[:2], rest[2:4], rest[4]
    deltas, (total, out_total, buffer) = rest[5:10], rest[10:]
    step = pl.program_id(0)
    n = jnp.concatenate([n[...] for n in narrow], axis=0)
    grad = (mm(cot[...], n) * slope[...].astype(F32)).astype(BF16)
    out_term = mm_nt(hidden[...], n)
    thresholds_sum[...] = jnp.sum(grad.astype(F32), axis=0, keepdims=True)
    split_rows(mm(normed_t[...], grad), deltas)
    term = mm_nt(grad, joined(wide, buffer))

    @pl.when(step == 0)
    def _():
        total[...] = term
        out_total[...] = out_term

    @pl.when(step > 0)
    def _():
        total[...] += term
        out_total[...] += out_term

    @pl.when(step == pl.num_programs(0) - 1)
    def _():
        store_pieces(part, total[...])
        store_pieces(out, out_total[...])


def backward_call(cot, narrow_blocks, slope, hidden, normed_t, wide_blocks):
    width = slope.shape[1]
    tile = min(512, width)
    cols = pl.BlockSpec((PAD, tile), lambda t: (0, t))
    return call(
        backward_kernel,
        (width // tile,),
        [whole((PAD, D))]
        + plain_specs(tile, lambda t: t)
        + [cols, cols, whole((D, PAD))]
        + weight_specs(tile, lambda t: t),
        piece_specs() * 2 + [pl.BlockSpec((1, tile), lambda t: (0, t))] + delta_specs(tile, lambda t: (0, t)),
        piece_shapes() * 2 + [sds((1, width), F32)] + delta_shapes(width),
        8 * PAD * D * width,
        6 * D * width + 8 * PAD * D + 4 * PAD * width,
        [pltpu.VMEM((PAD, D), F32)] * 2 + [weight_buffer(tile)],
    )(cot, *narrow_blocks, slope, hidden, normed_t, *wide_blocks)


def resid_kernel(*rest):
    parts, (resid, cot, vec), rest = rest[:4], rest[4:7], rest[7:]
    weights, (grad_resid, grad_mixed, grad_t, sums, buffer) = rest[:9], rest[9:]
    upstream = load_sum(parts)
    standard, reciprocal = standardize(resid[...])
    sums[0:1] = jnp.sum(upstream * standard, axis=0, keepdims=True)
    sums[1:2] = jnp.sum(upstream, axis=0, keepdims=True)
    grad = cot[...].astype(F32) + norm_backward(upstream, standard, reciprocal, vec[DILATION : DILATION + 1])
    sums[2:3] = jnp.sum(grad, axis=0, keepdims=True)
    sums[3:4] = jnp.sum(cot[...].astype(F32), axis=0, keepdims=True)
    sums[4:8] = jnp.zeros((4, D), F32)
    grad_resid[...] = grad
    rounded = grad.astype(BF16)
    grad_mixed[...] = mm(rounded, joined(weights, buffer)).astype(BF16)
    grad_t[...] = grad.T.astype(BF16)


def resid_call(parts, resid, cot, vec, blocks):
    width = blocks[1].shape[1] // 4
    return call(
        resid_kernel,
        (1,),
        piece_specs() * 2 + [whole((PAD, D))] * 2 + [whole(vec.shape)] + weight_specs(width, lambda i: 3),
        [whole((PAD, D)), whole((PAD, width)), whole((D, PAD)), whole((8, D))],
        [sds((PAD, D), F32), sds((PAD, width)), sds((D, PAD)), sds((8, D), F32)],
        2 * PAD * D * width,
        16 * PAD * D + 2 * width * D + 2 * PAD * width,
        [weight_buffer(width)],
    )(*parts, resid, cot, vec, *blocks)


def attend_back_kernel(q, k, v, upstream, probs, grad_q, grad_k, grad_v):
    scaled = (q[...].astype(F32) * HD ** (-0.5)).astype(BF16)
    keys_t = (k[...].astype(F32) * HD ** (-0.5)).T.astype(BF16)
    values = v[...]
    up = upstream[...]
    grads_q = []
    kept_k = None
    kept_v = None
    for i in range(2):
        mask = head_mask(i, values.shape)
        rounded = probs[i]
        weights = rounded.astype(F32)
        picked = jnp.where(mask, values.astype(F32), 0.0).astype(BF16)
        weight_grad = mm_nt(picked, up)
        along = jnp.sum(weights * weight_grad, axis=0, keepdims=True)
        score_grad = (weights * (weight_grad - along)).astype(BF16)
        value_grad = mm(rounded, up)
        key_grad = mm(score_grad, scaled)
        kept_v = value_grad if i == 0 else jnp.where(mask, value_grad, kept_v)
        kept_k = key_grad if i == 0 else jnp.where(mask, key_grad, kept_k)
        grads_q.append(mm(keys_t[i * HD : (i + 1) * HD], score_grad))
    grad_q[...] = jnp.concatenate(grads_q, axis=0).T.astype(BF16)
    grad_k[...] = kept_k.astype(BF16)
    grad_v[...] = kept_v.astype(BF16)


def attend_back_call(qkv, upstream, probs):
    width = qkv.shape[1] // 3
    pairs = width // 128
    spec = lambda j: pl.BlockSpec((PAD, 128), lambda h, j=j: (0, j * pairs + h))
    return call(
        attend_back_kernel,
        (pairs,),
        [spec(0), spec(1), spec(2), spec(0), pl.BlockSpec((2, PAD, PAD), lambda h: (h, 0, 0))],
        [spec(0)] * 3,
        [sds((PAD, width))] * 3,
        pairs * 2 * 4 * 2 * PAD * PAD * 128,
        pairs * 2 * PAD * PAD * 2,
    )(qkv, qkv, qkv, upstream, probs)


def project_kernel(gq, gk, gv, normed_t, grad_t, mixed, *rest):
    weights, part, sums, deltas, (total, buffer) = rest[:9], rest[9:11], rest[11], rest[12:17], rest[17:]
    step = pl.program_id(0)

    def one(j, g):
        grad = g[...]
        sums[0] = jnp.sum(grad.astype(F32), axis=0, keepdims=True)
        split_rows(mm(normed_t[...], grad), deltas)
        term = mm_nt(grad, joined(weights, buffer))
        if j == 0:
            total[...] = term
        else:
            total[...] += term
        if j == 2:
            store_pieces(part, total[...])

    for j, g in enumerate((gq, gk, gv)):
        pl.when(step == j)(lambda j=j, g=g: one(j, g))

    @pl.when(step == 3)
    def _():
        split_rows(mm(grad_t[...], mixed[...]), deltas)


def project_call(grads, normed_t, grad_t, mixed, blocks):
    width = grads[0].shape[1]
    at = lambda j: jnp.minimum(j, 2)
    return call(
        project_kernel,
        (4,),
        [whole((PAD, width))] * 3 + [whole((D, PAD))] * 2 + [whole((PAD, width))] + weight_specs(width, at),
        piece_specs()
        + [pl.BlockSpec((1, 1, width), lambda j: (at(j), 0, 0))]
        + delta_specs(width, lambda j: (0, j)),
        piece_shapes() + [sds((3, 1, width), F32)] + delta_shapes(4 * width),
        4 * PAD * D * 3 * width + 2 * PAD * D * width,
        4 * D * 4 * width + 6 * PAD * D + 6 * PAD * width,
        [pltpu.VMEM((PAD, D), F32), weight_buffer(width)],
    )(*grads, normed_t, grad_t, mixed, *blocks)


def share(refs, at, value):
    owners, _rows, features = refs.shape
    for i in range(owners):
        refs[i, at : at + PAD] = value[:, i * features : (i + 1) * features].astype(BF16)


def tokens_kernel(*refs):
    parts, ffn_parts, (x, resid, grad_resid, cot, vec, deltas, sums) = refs[:4], refs[4:8], refs[8:]
    upstream = load_sum(parts)
    tokens = x[...].astype(F32)
    standard, reciprocal = standardize(tokens)
    sums[0:1] = jnp.sum(upstream * standard, axis=0, keepdims=True)
    sums[1:2] = jnp.sum(upstream, axis=0, keepdims=True)
    sums[2:8] = jnp.zeros((6, D), F32)
    share(deltas, 0, load_sum(ffn_parts) + vec[RESIDUE : RESIDUE + 1] + (resid[...] - tokens))
    grad = grad_resid[...] + norm_backward(upstream, standard, reciprocal, vec[STRETCH : STRETCH + 1])
    share(deltas, PAD, grad - cot[...].astype(F32))


def tokens_call(parts, ffn_parts, x, resid, grad_resid, cot, vec, features):
    return call(
        tokens_kernel,
        (1,),
        piece_specs() * 4 + [whole((PAD, D))] * 4 + [whole(vec.shape)],
        [whole((D // features, 2 * PAD, features)), whole((8, D))],
        [sds((D // features, 2 * PAD, features)), sds((8, D), F32)],
        24 * PAD * D,
        24 * PAD * D,
    )(*parts, *ffn_parts, x, resid, grad_resid, cot, vec)


def images_kernel(got, tokens, cot, layer, delta):
    for j in range(RB):
        at = slice(j * SEQ, (j + 1) * SEQ)
        layer[at] = got[j, :SEQ].astype(F32) + tokens[at].astype(F32)
        delta[at] = got[j, PAD : PAD + SEQ].astype(F32) + cot[at].astype(F32)


def images_call(got, tokens, cot):
    rows, features = tokens.shape
    return call(
        images_kernel,
        (1,),
        [whole(got.shape), whole((rows, features)), whole((rows, features))],
        [whole((rows, features))] * 2,
        [sds((rows, features), F32)] * 2,
        4 * rows * features,
        16 * rows * features,
    )(got, tokens, cot)


def swap(value, k):
    return lax.ppermute(value, "row", [(i, i ^ k) for i in range(RB)])


def after(value, *earlier):
    return lax.optimization_barrier((value,) + earlier)[0]


def sibling(part):
    size = lax.axis_size("col")
    if size == 2:
        return lax.ppermute(part, "col", [(0, 1), (1, 0)])
    total = None
    for s in range(1, size):
        term = lax.ppermute(part, "col", [(i, (i + s) % size) for i in range(size)]).astype(F32)
        total = term if total is None else total + term
    return total.astype(BF16)


def col_gather(values):
    size = lax.axis_size("col")
    lanes = values[0].shape[1]
    wide = jnp.concatenate(values, axis=1)
    if size == 2:
        other = lax.ppermute(wide, "col", [(0, 1), (1, 0)])
        first = lax.axis_index("col") == 0
        columns = [jnp.where(first, wide, other), jnp.where(first, other, wide)]
    else:
        columns = list(lax.all_gather(wide, "col"))
    parts = [column[:, k * lanes : (k + 1) * lanes] for k in range(len(values)) for column in columns]
    return jnp.concatenate(parts, axis=1)


class Gather:
    def __init__(self, clock, weight, *earlier):
        self.clock = clock
        self.plane = lax.axis_index("dp") % 2
        self.weight = weight
        shared = lax.dynamic_slice_in_dim(weight, PLANE + SHARED * self.plane, SHARED, axis=0)
        mine = after(jnp.concatenate([weight[:PLANE], shared]), *earlier)
        self.near = [swap(mine, 1), swap(mine, 2)]

    def across(self, value):
        return lax.ppermute(value, "dp", [(i, i ^ 1) for i in range(lax.axis_size("dp"))])

    def relay(self):
        near_x, near_y = self.near = self.clock(*self.near)
        self.far = [swap(near_x[:PLANE], 2), swap(near_y[PLANE:], 1)]
        self.other = [self.across(near_x[PLANE:]), self.across(near_y[PLANE:])]

    def hand_over(self, *earlier):
        *self.far, self.other[0] = self.clock(*self.far, self.other[0], *earlier)[:3]
        self.other.append(self.across(self.far[1]))

    def pieces(self):
        self.other[1:] = self.clock(*self.other[1:])
        return [self.plane.astype(jnp.int32)[None], self.weight, *self.near, *self.far, *self.other]


def add(*terms):
    total = terms[0].astype(F32)
    for term in terms[1:]:
        total = total + term.astype(F32)
    return total.astype(terms[0].dtype)


class Clock:
    def __init__(self):
        self.last = ()

    def __call__(self, *values):
        values = lax.optimization_barrier(tuple(values) + self.last)[: len(values)]
        self.last = values[:1]
        return values


class LineSum:
    def __init__(self, clock, value):
        size = lax.axis_size("dp")
        half = size // 2
        inward = [(s, s + 1) for s in range(half - 1)]
        self.clock = clock
        self.value = value
        if size % 2:
            self.value = lax.psum(value, "dp")
            self.steps = []
            return
        self.steps = [(None, [pair, (size - 1 - pair[0], size - 1 - pair[1])]) for pair in inward]
        self.steps.append((None, [(half - 1, half), (half, half - 1)]))
        for s, t in reversed(inward):
            self.steps.append((s, [(t, s), (size - 1 - t, size - 1 - s)]))
        self.send()

    def send(self):
        if self.steps:
            self.moved = lax.ppermute(self.value, "dp", self.steps[0][1])

    def advance(self):
        if not self.steps:
            return
        moved = self.clock(self.moved)[0]
        outer, pairs = self.steps.pop(0)
        if outer is None:
            self.value = add(self.value, moved)
        else:
            where = lax.axis_index("dp")
            far = lax.axis_size("dp") - 1 - outer
            self.value = jnp.where((where == outer) | (where == far), moved, self.value)
        self.send()


def first_sends(blocks):
    return swap(blocks[1], 1), swap(blocks[2], 2)


def last_terms(blocks, came):
    return add(blocks[3], came[1][: KB // 2]), add(blocks[4], came[0][: KB // 2])


def last_sends(terms):
    return swap(terms[0], 1), swap(terms[1], 2)


def own_sums(blocks, came, last):
    half = KB // 2
    return add(blocks[0][:half], came[0][half:], last[1]), add(blocks[0][half:], came[1][half:], last[0])


def afters(values, *earlier):
    return [after(value, *earlier) for value in values]


def per_device(
    tokens,
    projector,
    offsets,
    combiner,
    baseline,
    widener,
    thresholds,
    narrower,
    residue,
    stretch,
    lifting,
    dilation,
    elevation,
    cotangent,
):
    row = lax.axis_index("row")
    columns = lax.axis_size("col")
    features = tokens.shape[1]
    width = projector.shape[2]

    clock = Clock()

    def pick(stack, index, axis=0):
        return lax.dynamic_index_in_dim(stack, index, axis, keepdims=False)

    def padded(value):
        return jnp.pad(value.reshape(RB, SEQ, features), ((0, 0), (0, PAD - SEQ), (0, 0)))

    vectors = jnp.stack([stretch, lifting, baseline, dilation, elevation, residue, residue, residue])
    coarse = lax.optimization_barrier(vectors.astype(BF16))
    fine = (vectors - coarse.astype(F32)).astype(BF16)
    images = jnp.concatenate([padded(tokens), padded(cotangent)], axis=1)
    to = [jnp.concatenate([pick(images, row ^ k), coarse, fine]) for k in range(RB)]
    near = clock(*[swap(to[k], k) for k in range(1, RB)])
    attn_w = Gather(clock, jnp.concatenate([*projector, combiner.T], axis=1), *near)
    got = clock(col_gather([to[0], *near]))[0]
    x, cot = got[:PAD], got[PAD : 2 * PAD]
    vec = got[2 * PAD : 2 * PAD + 8].astype(F32) + got[2 * PAD + 8 :].astype(F32)
    x, cot, vec = clock(x, cot, vec)
    normed_one, normed_one_t, cot_t = clock(*norm_call(x, vec, cot))
    attn_w.relay()
    attn_w.hand_over()
    wide_w = Gather(clock, widener, *attn_w.far)
    attn_w = attn_w.pieces()
    wide_w.relay()

    bias = jnp.stack([offsets[0], jnp.zeros((width,), F32), offsets[1]])[:, None]
    qkv = qkv_call(normed_one, attn_w, bias)
    wide_w.hand_over(qkv)
    narrow = after(narrower.T, *wide_w.far)
    near_n = [swap(narrow, 1), swap(narrow, 2)]
    mixed, probs = attend_call(qkv)
    parts = combine_call(mixed, attn_w)
    others = [sibling(part) for part in parts]
    wide_w = wide_w.pieces()
    near_n = clock(*near_n)
    far_n = [swap(near_n[0][: KB // 2], 2), swap(near_n[1][KB // 2 :], 1)]
    others = clock(*others)
    out = forward_call(x, [*parts, *others], vec, wide_w, thresholds[None], cot_t)
    resid, normed_two_t, hidden, slope = out[:4]
    *far_n, slope = clock(*far_n, slope)
    blocks_n = afters(out[4:], *far_n)
    came_n = first_sends(blocks_n)
    narrow_w = [narrow, *near_n, *far_n]

    out = backward_call(cot, narrow_w, slope, hidden, normed_two_t, wide_w)
    parts, ffn_parts, thresholds_sum = out[:2], out[2:4], out[4]
    blocks_w = out[5:]
    *came_n, top = clock(*came_n, parts[0])
    parts = [top, parts[1]]
    terms = last_terms(blocks_n, came_n)
    last_n = last_sends(terms)
    came_w = list(first_sends(afters(blocks_w, *terms)))
    others = [sibling(part) for part in parts]
    grad_resid, grad_mixed, grad_t, sums_two = resid_call([*parts, *others], resid, cot, vec, attn_w)
    *last_n, grad_mixed = clock(*last_n, grad_mixed)
    halves = jnp.concatenate(own_sums(blocks_n, came_n, last_n))
    sum_n = LineSum(clock, halves)
    ffn_others = [sibling(after(part, *last_n)) for part in ffn_parts]
    grads = attend_back_call(qkv, after(grad_mixed, halves), probs)
    out = project_call(grads, normed_one_t, grad_t, mixed, attn_w)
    parts, grad_sums = out[:2], out[2]
    came_w[0], came_w[1], top, *ffn_others = clock(*came_w, parts[0], *ffn_others)
    parts = [top, parts[1]]
    terms = last_terms(blocks_w, came_w)
    last_w = list(last_sends(terms))
    blocks_p = afters(out[3:], *terms)
    came_p = list(first_sends(blocks_p))
    others = clock(*[sibling(part) for part in parts])
    deltas, sums_one = tokens_call(
        [*parts, *others], [*ffn_parts, *ffn_others], x, resid, grad_resid, cot, vec, features
    )
    featured = jnp.concatenate([sums_one[:2], sums_two[:4]]).reshape(6, RB, columns, features)
    featured = pick(featured, lax.axis_index("col"), 2)
    shared = jnp.concatenate([grad_sums[0, 0], grad_sums[2, 0], thresholds_sum[0]])
    size = 6 * features + shared.shape[0]
    lines = -(-size // (16 * features)) * 16
    mine = pick(deltas.reshape(RB, columns, 2 * PAD, features), lax.axis_index("col"), 1)
    fill = jnp.zeros((lines * features - size,), F32)
    to = []
    for j in range(RB):
        small = pick(featured, row ^ j, 1).reshape(-1)
        small = jnp.concatenate([small, shared, fill]).reshape(lines, features)
        to.append(jnp.concatenate([pick(mine, row ^ j), small.astype(BF16)]))
    last_w[0], last_w[1], to = clock(*last_w, jnp.stack(to))
    sum_w = [LineSum(clock, half) for half in own_sums(blocks_w, came_w, last_w)]
    sum_n.advance()
    came_p = clock(*came_p)
    last_p = last_sends(last_terms(blocks_p, came_p))
    sum_n.advance()
    sum_w[0].advance()
    sum_w[1].advance()
    last_p = clock(*last_p)
    halves_p = own_sums(blocks_p, came_p, last_p)
    sum_p = [LineSum(clock, half) for half in halves_p]
    got = lax.all_to_all(after(to, *halves_p), "row", 0, 0)
    sum_w[0].advance()
    sum_n.advance()
    sum_w[1].advance()
    sum_p[0].advance()
    sum_p[0].advance()
    sum_p[1].advance()
    got = clock(got)[0]
    small = got[:, 2 * PAD :].astype(F32)
    sum_s = LineSum(clock, sum([small[j] for j in range(1, RB)], small[0]))
    narrower_delta = clock(sum_n.value.astype(F32).T)[0]
    sum_w[0].advance()
    sum_w[1].advance()
    sum_s.advance()
    sum_p[1].advance()
    layer_output, tokens_delta = images_call(after(got, sum_p[1].value), tokens, cotangent)
    layer_output = clock(layer_output)[0]
    sum_s.advance()
    for line_sum in (sum_n, sum_s, *sum_w, *sum_p):
        while line_sum.steps:
            line_sum.advance()
    widener_delta = jnp.concatenate([line_sum.value for line_sum in sum_w]).astype(F32)
    small = sum_s.value.reshape(-1)[:size]
    total_p = jnp.concatenate([line_sum.value for line_sum in sum_p]).astype(F32)
    projector_delta = jnp.stack([total_p[:, j * width : (j + 1) * width] for j in range(3)])
    combiner_delta = total_p[:, 3 * width :].T

    count = 6 * features
    vector = small[:count].reshape(6, features)
    offsets_delta = small[count : count + 2 * width].reshape(2, width)
    thresholds_delta = small[count + 2 * width :]
    return (
        layer_output,
        tokens_delta,
        projector_delta,
        offsets_delta,
        combiner_delta,
        vector[4],
        widener_delta,
        thresholds_delta,
        narrower_delta,
        vector[5],
        vector[0],
        vector[1],
        vector[2],
        vector[3],
    )


def solution(mesh):
    features = P(("row", "col"))
    specs = {
        "tokens": P("dp", ("row", "col")),
        "projector": P(None, "row", "col"),
        "offsets": P(None, "col"),
        "combiner": P("col", "row"),
        "baseline": features,
        "widener": P("row", "col"),
        "thresholds": P("col"),
        "narrower": P("col", "row"),
        "residue": features,
        "stretch": features,
        "lifting": features,
        "dilation": features,
        "elevation": features,
    }
    weights = tuple(specs.values())
    return jax.shard_map(
        per_device,
        mesh=mesh,
        in_specs=weights + (specs["tokens"],),
        out_specs=(specs["tokens"], specs["tokens"]) + weights[1:],
        check_vma=False,
    )
```
